32 devices in a mesh: groups: 2 (over y), wide: 4 (over z), narrow: 4 (over x, core).
Axes of the slice: x: 2, y: 2, z: 4, core: 2. Of those that a mesh axis runs over, the one named last changes fastest.
Arguments:
- activations: bfloat16 [2048, 8192], P(('groups', 'wide'), 'narrow'), parts along dimension 0, may hold values from -6 to 6
- request_tenants: int32 [2048, 1], P(('groups', 'wide')), parts along dimension 0, may hold values from 0 to 63; in each aligned block of 256 rows (0 to 255, 256 to 511, ...) at most 16 rows name the same one
- adapter_slot: int32 [64], replicated, may hold values from 0 to 63, each once
- shared_weight: bfloat16 [8192, 2048], P(None, 'narrow'), may hold values from -0.0625 to 0.0625
- adapter_down_weight: bfloat16 [64, 8192, 128], P('wide', 'narrow'), may hold values from -0.0625 to 0.0625
- adapter_up_weight: bfloat16 [64, 64, 2048], P('wide', None, 'narrow'), may hold values from -0.75 to 0.75
Outputs:
- projected: bfloat16 [2048, 2048], P(('groups', 'wide'), 'narrow'), parts along dimension 0
The draws below stay inside these ranges and needn't reach their ends.
There are 2 independent parts, one for each index of `groups`. The reference program is written for one: setup_inputs(seed, part) draws one part's arguments, and reference() takes and returns one part's arrays. A program takes and returns all parts, laid end to end along the dimension named above; an argument that names none is the same for every part. Nothing has to cross between parts.
Inputs may be any that keep to these rules, and one draw needn't show every extreme that they name: `request_tenants`: in each aligned block of 256 rows (the rows of one device) no tenant is named by more than 16 rows, a bound that some block reaches; every tenant is named by some row. `adapter_slot`: A permutation of the tenants.
All inputs are finite; a program needn't handle non-finite values.
Results may differ from the reference program's by a relative error of at most 0.007.
Values may be sent and summed in bfloat16 or wider, within the bound.
No kernel may reach another device: no remote copies, remote signals or barrier semaphores. Data moves between devices by JAX's collectives and lax.ppermute only.
A program may use at most 128 MiB of HBM per device.

```python
import math
import jax
import jax.numpy as jnp
import numpy as np
from jax import lax

MODEL_WIDTH = 8192
KEY_VALUE_COLS = 1024
ADAPTER_RANK = 64
TENANT_TOTAL = 64
ROWS_DEV = 256
MOST = 16
ROWS = 1024
N_WIDE = 4


def block_scale(own_key, dims, shards, low, largest):
    def one(dim, shards_of):
        heights = jax.random.uniform(jax.random.fold_in(jax.random.fold_in(own_key, 6), dim), (shards_of,), jnp.float32, low / len(shards), largest / len(shards))
        return jnp.repeat(jnp.exp(heights), dims[dim] // shards_of).reshape((-1,) + (1,) * (len(dims) - dim - 1))

    level = one(*shards[0])
    for cut in shards[1:]:
        level = level * one(*cut)
    return level


def routed_block(stream_key, own, number, rows, number_of, top, most, skew):
    ranking = jax.random.permutation(stream_key, number_of)
    crowded, ordinary = load_shares(number_of, rows * top, most, skew, True), load_shares(number_of, rows * top, most, skew, False)
    places = jnp.arange(number_of)

    def named(sizes, rotation):
        used = int((sizes > 0).sum())
        fixed = max(1, used // 4)
        passed = fixed + (places - fixed + rotation * (used - fixed)) % max(1, number_of - fixed)
        return jnp.zeros((number_of,), jnp.int32).at[ranking[jnp.where(places < fixed, places, passed)]].set(jnp.asarray(sizes, jnp.int32))

    sizes = jnp.where(number % 4 == 0, named(crowded, number // 4), named(ordinary, number - number // 4 - 1))
    mixed = jax.random.permutation(jax.random.fold_in(own, 3), number_of)
    giver, taker = mixed[0:number_of // 2 * 2:2], mixed[1:number_of // 2 * 2:2]
    margin = jnp.minimum(sizes[giver] - 1, most - sizes[taker]) // 2
    margin = jnp.where((giver == ranking[0]) | (taker == ranking[0]) | (sizes[taker] == 0), 0, jnp.maximum(margin, 0))
    passed = jax.random.randint(jax.random.fold_in(own, 4), (number_of // 2,), 0, 1 << 20) % (margin + 1)
    sizes = sizes.at[giver].add(-passed).at[taker].add(passed)
    items = jnp.searchsorted(jnp.cumsum(sizes), jnp.arange(rows * top), side="right").astype(jnp.int32)
    listing = items.reshape(top, rows).T
    listing = listing[jax.random.permutation(jax.random.fold_in(own, 1), rows)]
    rotation = jax.random.randint(jax.random.fold_in(own, 2), (rows, 1), 0, top)
    return jnp.take_along_axis(listing, (jnp.arange(top)[None, :] + rotation) % top, axis=1)


def load_shares(amount, total, reach, skew, full):
    portions = [(1 << 20) // math.isqrt(standing ** skew) + 1 for standing in range(1, amount + 1)]
    largest = reach if full else min(reach, max(-(-total // amount), total * portions[0] // sum(portions)))
    least = 1 if total - largest >= amount - 1 else 0
    given, rest = [largest] + [least] * (amount - 1), total - largest - least * (amount - 1)
    while rest > 0:
        movable = [i for i in range(1, amount) if given[i] < largest] or [i for i in range(1, amount) if given[i] < reach]
        whole, remaining = sum([portions[i] for i in movable]), rest
        for i in movable:
            more = min(reach - given[i], max(1, remaining * portions[i] // whole), rest)
            given[i] = given[i] + more
            rest = rest - more
    return np.array(given)


def centred(own_key, extent, scale, reach, cuts=(), kind=jnp.bfloat16):
    loudness = block_scale(own_key, extent, cuts, -0.22, 0.18) if cuts else 1.0
    entries = jax.random.normal(own_key, extent, jnp.float32) * scale * loudness
    return jnp.minimum(jnp.maximum(entries, -reach), reach).astype(kind)


def setup_inputs(seed: int = 0, part: int = 0) -> dict:
    key_list = jax.random.split(jax.random.key(seed), 7)
    own_keys = jax.random.split(jax.random.fold_in(key_list[6], part), 7)
    activations = centred(own_keys[0], (ROWS, MODEL_WIDTH), 1.0, 6.0, ((0, 4), (1, 4)))
    request_tenants_keys = jax.random.split(jax.random.fold_in(own_keys[1], 1), ROWS // ROWS_DEV)
    request_tenants_turns = jax.random.permutation(jax.random.fold_in(own_keys[1], 3), ROWS // ROWS_DEV)
    request_tenants = jax.vmap(lambda own, number: routed_block(jax.random.fold_in(own_keys[1], 2), own, number, ROWS_DEV, TENANT_TOTAL, 1, MOST, 2))(request_tenants_keys, request_tenants_turns).reshape((ROWS, 1))
    adapter_slot = jax.random.permutation(key_list[2], TENANT_TOTAL).astype(jnp.int32)
    shared_weight = centred(key_list[3], (MODEL_WIDTH, 2 * KEY_VALUE_COLS), MODEL_WIDTH ** -0.5, 0.0625, ((1, 4),))
    adapter_down_weight = centred(key_list[4], (TENANT_TOTAL, MODEL_WIDTH, 2 * ADAPTER_RANK), MODEL_WIDTH ** -0.5, 0.0625, ((0, 4), (1, 4)))
    adapter_up_weight = centred(key_list[5], (TENANT_TOTAL, ADAPTER_RANK, 2 * KEY_VALUE_COLS), ADAPTER_RANK ** -0.5, 0.75, ((0, 4), (2, 4)))
    return {"activations": activations, "request_tenants": request_tenants, "adapter_slot": adapter_slot, "shared_weight": shared_weight, "adapter_down_weight": adapter_down_weight, "adapter_up_weight": adapter_up_weight}


def reference(activations, request_tenants, adapter_slot, shared_weight, adapter_down_weight, adapter_up_weight):
    row_count = activations.shape[0]
    tenant = request_tenants[:, 0]
    slot_row = adapter_slot[tenant]
    blocks = tenant.reshape(N_WIDE, ROWS_DEV)
    onehot = (blocks[:, :, None] == jnp.arange(TENANT_TOTAL, dtype=jnp.int32)[None, None, :]).astype(jnp.int32)
    before = jnp.cumsum(onehot, axis=1) - onehot
    position = jnp.sum(onehot * before, axis=2).reshape(row_count)
    block_of = jnp.arange(row_count, dtype=jnp.int32) // ROWS_DEV
    capacity = N_WIDE * MOST
    target = (slot_row * capacity + block_of * MOST + position).astype(jnp.int32)
    row_table = jnp.full((TENANT_TOTAL * capacity,), row_count, jnp.int32)
    row_table = row_table.at[target].set(jnp.arange(row_count, dtype=jnp.int32)).reshape(TENANT_TOTAL, capacity)
    padded = jnp.concatenate([activations, jnp.zeros((1, activations.shape[1]), activations.dtype)], axis=0)
    key_cols = jnp.arange(2 * KEY_VALUE_COLS, dtype=jnp.int32) < KEY_VALUE_COLS

    def per_slot(adapter_slot_index):
        chosen_slots = padded[row_table[adapter_slot_index]]
        reduced_rank_output = jnp.dot(chosen_slots, adapter_down_weight[adapter_slot_index], preferred_element_type=jnp.float32).astype(jnp.bfloat16)
        chosen_up_weight = adapter_up_weight[adapter_slot_index]
        key_part = jnp.dot(reduced_rank_output[:, :ADAPTER_RANK], chosen_up_weight, preferred_element_type=jnp.float32)
        value_part = jnp.dot(reduced_rank_output[:, ADAPTER_RANK:], chosen_up_weight, preferred_element_type=jnp.float32)
        return jnp.where(key_cols[None, :], key_part, value_part).astype(jnp.bfloat16)

    corrections = lax.map(per_slot, jnp.arange(TENANT_TOTAL, dtype=jnp.int32))
    correction = corrections.reshape(TENANT_TOTAL * capacity, 2 * KEY_VALUE_COLS)[target]
    base_out = jnp.dot(activations, shared_weight, preferred_element_type=jnp.float32)
    return (base_out + correction.astype(jnp.float32)).astype(jnp.bfloat16)
```

```python
import functools

import jax
import jax.numpy as jnp
from jax import lax
from jax.experimental import pallas as pl
from jax.experimental.pallas import tpu as pltpu
from jax.sharding import PartitionSpec as P

KEY_VALUE_COLS = 1024
LANES = 128
MOST = 16
NEAR = 2
NEAR_ROWS = 112
FAR_ROWS = 96
VMEM = pltpu.VMEM
MIB = 1 << 20

f32, bf16, i32 = jnp.float32, jnp.bfloat16, jnp.int32


def block_rows(k, local_count):
    most = -(-(local_count * MOST + 1) // 32) * 32
    return min(NEAR_ROWS if k < NEAR else FAR_ROWS, most)


def swap(x, axis, k):
    size = lax.axis_size(axis)
    return lax.ppermute(x, axis, [(i, i ^ k) for i in range(size)])


def params(mib):
    return pltpu.CompilerParams(vmem_limit_bytes=mib * MIB)


def pack_kernel(local_count, where_ref, tenant_ref, slot_ref, act_ref, place_ref, *rest):
    blocks, perms = rest[: len(rest) // 2], rest[len(rest) // 2 :]
    wide_size = len(blocks)
    rows = tenant_ref.shape[1]

    @pl.when(pl.program_id(0) == 0)
    def _():
        tenants = slot_ref.shape[1]
        tenant = tenant_ref[...]
        named = tenant == lax.broadcasted_iota(i32, (tenants, rows), 0)
        slots = jnp.broadcast_to(slot_ref[...].astype(f32), (8, tenants)).astype(bf16)
        slot = jnp.dot(slots, named.astype(f32).astype(bf16), preferred_element_type=f32)[:1]
        dest = jnp.floor((slot + 0.5) * (1.0 / local_count))
        adapter = slot - dest * local_count + 1.0
        leap = jnp.bitwise_xor(dest.astype(i32), where_ref[0])
        padded = max(8, wide_size)
        goes = leap == lax.broadcasted_iota(i32, (padded, rows), 0)
        goes_f = goes.astype(f32)
        earlier = lax.broadcasted_iota(i32, (rows, rows), 0) < lax.broadcasted_iota(
            i32, (rows, rows), 1
        )
        before = jnp.dot(
            goes_f.astype(bf16), earlier.astype(f32).astype(bf16), preferred_element_type=f32
        )
        position = jnp.sum(goes_f * before, axis=0, keepdims=True).astype(i32)
        adapters = jnp.broadcast_to(adapter, (8, rows)).astype(bf16)
        place = jnp.full((1, rows), -1, i32)
        more = jnp.zeros((1, rows), i32)
        offset = 0
        here = []
        for k in range(wide_size):
            held = block_rows(k, local_count) - 1
            mine = position - where_ref[1] * held
            mine = jnp.where(leap == k, mine, -1)
            more = jnp.maximum(more, jnp.where(mine >= held, 1, 0))
            mine = jnp.where(mine < held, mine, -1)
            place = jnp.where(mine >= 0, mine + offset, place)
            offset += held + 1
            here.append(mine)
        any_more = jnp.max(more.astype(f32), axis=1, keepdims=True)
        for k in range(wide_size):
            count = block_rows(k, local_count)
            perm = (lax.broadcasted_iota(i32, (count, rows), 0) == here[k]).astype(f32).astype(bf16)
            perms[k][...] = perm
            filler = jnp.zeros((LANES - count, rows), bf16)
            ids = lax.dot_general(
                adapters,
                jnp.concatenate([perm, filler], axis=0),
                (((1,), (1,)), ((), ())),
                preferred_element_type=f32,
            )[:1]
            lane = lax.broadcasted_iota(i32, (1, LANES), 1)
            ids = jnp.where(lane == LANES - 1, any_more, ids)
            last = lax.broadcasted_iota(i32, (count, LANES), 0) == count - 1
            body = jnp.dot(perm, act_ref[:, :LANES], preferred_element_type=f32)
            blocks[k][:, :LANES] = jnp.where(last, ids, body).astype(bf16)
            blocks[k][:, LANES:] = jnp.dot(
                perm, act_ref[:, LANES:], preferred_element_type=f32
            ).astype(bf16)
        place_ref[...] = jnp.broadcast_to(place.astype(f32), (LANES, rows)).T

    @pl.when(pl.program_id(0) > 0)
    def _():
        for k in range(wide_size):
            blocks[k][...] = jnp.dot(perms[k][...], act_ref[...], preferred_element_type=f32).astype(
                bf16
            )


def pack(where, tenant, slot, activations, wide_size, local_count):
    rows, features = activations.shape
    chunk = min(512, features)
    counts = [block_rows(k, local_count) for k in range(wide_size)]
    return pl.pallas_call(
        functools.partial(pack_kernel, local_count),
        grid=(features // chunk,),
        out_shape=[jax.ShapeDtypeStruct((rows, LANES), f32)]
        + [jax.ShapeDtypeStruct((c, features), bf16) for c in counts],
        in_specs=[
            pl.BlockSpec(memory_space=pltpu.SMEM),
            pl.BlockSpec((1, rows), lambda i: (0, 0)),
            pl.BlockSpec((1, slot.shape[1]), lambda i: (0, 0)),
            pl.BlockSpec((rows, chunk), lambda i: (0, i)),
        ],
        out_specs=[pl.BlockSpec((rows, LANES), lambda i: (0, 0))]
        + [pl.BlockSpec((c, chunk), lambda i: (0, i)) for c in counts],
        scratch_shapes=[VMEM((c, rows), bf16) for c in counts],
        compiler_params=params(24),
        cost_estimate=pl.CostEstimate(
            flops=2 * sum(counts) * rows * features,
            bytes_accessed=2 * features * (rows + sum(counts)),
            transcendentals=0,
        ),
        name="pack_rows",
    )(where, tenant, slot, activations)


def down_kernel(count, cols, narrow_size, where_ref, *refs):
    xs, weight_ref = refs[:count], refs[count]
    ids_ref, flag_ref = refs[count + 1 : count + 3]
    parts = refs[count + 3 : count + 3 + narrow_size]
    held_ref, total_ref = refs[count + 3 + narrow_size :]
    step = pl.program_id(0)
    per_step = weight_ref.shape[0]

    @pl.when(step == 0)
    def _():
        offset = 0
        flag = jnp.zeros((8, LANES), f32)
        for x in xs:
            rows = x.shape[0]
            held_ref[pl.ds(offset, rows), :] = x[...]
            last = x[pl.ds(rows - 16, 16), :LANES].astype(f32)[15:]
            square = jnp.broadcast_to(last, (LANES, LANES))
            flag = jnp.maximum(flag, square[:8])
            turned = square.T[:rows]
            keep = lax.broadcasted_iota(i32, (rows, LANES), 0) < rows - 1
            ids_ref[pl.ds(offset, rows), :] = jnp.where(keep, turned, 0.0)
            offset += rows
        flag_ref[...] = flag
        total_ref[...] = jnp.zeros_like(total_ref)

    weights = jnp.concatenate([weight_ref[j] for j in range(per_step)], axis=1)
    found = jnp.dot(held_ref[...], weights, preferred_element_type=f32)
    ids = ids_ref[...]
    total = total_ref[...]
    for j in range(per_step):
        name = (step * per_step + j + 1).astype(f32)
        total = jnp.where(ids == name, found[:, j * LANES : (j + 1) * LANES], total)
    total_ref[...] = total

    @pl.when(step == pl.num_programs(0) - 1)
    def _():
        full = total_ref[...]
        half = full.shape[0] // 2
        rank = LANES // 2
        top, bottom = full[:half], full[half:]
        low = lax.broadcasted_iota(i32, (half, LANES), 1) < rank
        keys = jnp.where(low, top, pltpu.roll(bottom, rank, 1))
        values = jnp.where(low, pltpu.roll(top, rank, 1), bottom)
        for j in range(narrow_size):
            start = jnp.bitwise_xor(where_ref[2], j) * cols
            parts[j][...] = jnp.where(start >= KEY_VALUE_COLS, values, keys).astype(parts[j].dtype)


def down(where, blocks, weight, cols, narrow_size):
    adapters, features, width = weight.shape
    rows = sum(b.shape[0] for b in blocks)
    per_step = 2 if adapters % 2 == 0 else 1
    return pl.pallas_call(
        functools.partial(down_kernel, len(blocks), cols, narrow_size),
        grid=(adapters // per_step,),
        out_shape=[
            jax.ShapeDtypeStruct((rows, LANES), f32),
            jax.ShapeDtypeStruct((8, LANES), f32),
        ]
        + [jax.ShapeDtypeStruct((rows // 2, LANES), bf16 if j else f32) for j in range(narrow_size)],
        in_specs=[pl.BlockSpec(memory_space=pltpu.SMEM)]
        + [pl.BlockSpec(b.shape, lambda i: (0, 0)) for b in blocks]
        + [pl.BlockSpec((per_step, features, width), lambda i: (i, 0, 0))],
        out_specs=[
            pl.BlockSpec((rows, LANES), lambda i: (0, 0)),
            pl.BlockSpec((8, LANES), lambda i: (0, 0)),
        ]
        + [pl.BlockSpec((rows // 2, LANES), lambda i: (0, 0)) for _ in range(narrow_size)],
        scratch_shapes=[VMEM((rows, features), bf16), VMEM((rows, LANES), f32)],
        compiler_params=params(32),
        cost_estimate=pl.CostEstimate(
            flops=2 * rows * features * adapters * width,
            bytes_accessed=2 * features * (rows + adapters * width),
            transcendentals=0,
        ),
        name="down_maps",
    )(where, *blocks, weight)


def up_kernel(narrow_size, ids_ref, *refs):
    parts, weight_ref, outs = refs[:narrow_size], refs[narrow_size], refs[narrow_size + 1 :]
    total = parts[0][...]
    for part in parts[1:]:
        total = total + part[...].astype(f32)
    low_rank = total.astype(bf16).astype(f32)
    rank = LANES // 2
    turned = pltpu.roll(low_rank, rank, 1)
    low = lax.broadcasted_iota(i32, low_rank.shape, 1) < rank
    twice = jnp.concatenate(
        [jnp.where(low, low_rank, turned), jnp.where(low, turned, low_rank)], axis=0
    )
    ids = ids_ref[...]
    second = (lax.broadcasted_iota(i32, ids.shape, 1) >= rank).astype(f32)
    adapters = weight_ref.shape[0] // rank
    left = [
        jnp.where(ids - second == 2.0 * pair + 1.0, twice, 0.0).astype(bf16)
        for pair in range(adapters // 2)
    ]
    found = jnp.dot(jnp.concatenate(left, axis=1), weight_ref[...], preferred_element_type=f32)
    offset = 0
    for out in outs:
        rows = out.shape[0]
        out[...] = found[offset : offset + rows].astype(bf16)
        offset += rows


def up(ids, parts, weight, counts):
    cols = weight.shape[1]
    return pl.pallas_call(
        functools.partial(up_kernel, len(parts)),
        out_shape=[jax.ShapeDtypeStruct((c, cols), bf16) for c in counts],
        compiler_params=params(24),
        cost_estimate=pl.CostEstimate(
            flops=2 * sum(counts) * weight.size,
            bytes_accessed=2 * weight.size + 2 * sum(counts) * (cols + 512),
            transcendentals=0,
        ),
        name="up_maps",
    )(ids, *parts, weight)


def base_kernel(count, where_ref, *refs):
    acts, weight_ref, out_ref = refs[:count], refs[count], refs[count + 1]
    step = pl.program_id(0)
    for j in range(count):

        @pl.when(step == j)
        def _(j=j):
            found = jnp.dot(acts[j][...], weight_ref[...], preferred_element_type=f32)
            out_ref[...] = found if j == 0 else out_ref[...] + found


def base(where, acts, weight):
    rows, features = acts[0].shape
    cols = weight.shape[1]
    count = len(acts)
    return pl.pallas_call(
        functools.partial(base_kernel, count),
        grid_spec=pltpu.PrefetchScalarGridSpec(
            num_scalar_prefetch=1,
            grid=(count,),
            in_specs=[pl.BlockSpec((rows, features), lambda i, where: (0, 0)) for _ in acts]
            + [
                pl.BlockSpec(
                    (features, cols), lambda i, where: (jnp.bitwise_xor(where[2], i), 0)
                )
            ],
            out_specs=pl.BlockSpec((rows, cols), lambda i, where: (0, 0)),
        ),
        out_shape=jax.ShapeDtypeStruct((rows, cols), f32),
        compiler_params=params(24),
        cost_estimate=pl.CostEstimate(
            flops=2 * rows * weight.size,
            bytes_accessed=2 * weight.size + 2 * rows * features * count,
            transcendentals=0,
        ),
        name="shared_projection",
    )(where, *acts, weight)


def join_kernel(base_ref, place_ref, *refs):
    corrections, out_ref = refs[:-1], refs[-1]
    stacked = jnp.concatenate([c[...] for c in corrections], axis=0)
    rows, count = base_ref.shape[0], stacked.shape[0]
    place = place_ref[:, :1].astype(i32)
    perm = (lax.broadcasted_iota(i32, (rows, count), 1) == place).astype(f32).astype(bf16)
    found = jnp.dot(perm, stacked, preferred_element_type=f32)
    out_ref[...] = (base_ref[...] + found).astype(out_ref.dtype)


def join(base_out, place, corrections, dtype):
    rows, cols = base_out.shape
    count = sum(c.shape[0] for c in corrections)
    return pl.pallas_call(
        join_kernel,
        out_shape=jax.ShapeDtypeStruct((rows, cols), dtype),
        compiler_params=params(24),
        cost_estimate=pl.CostEstimate(
            flops=2 * rows * cols * count,
            bytes_accessed=2 * cols * (count + 3 * rows),
            transcendentals=0,
        ),
        name="join_corrections",
    )(base_out, place, *corrections)


def corrections_of(turn, axes, tenant, slot, activations, down_weight, up_weight):
    wide_size, narrow_size = lax.axis_size("wide"), lax.axis_size("narrow")
    cols = up_weight.shape[1]
    where = jnp.stack([axes[0], turn, axes[1]])
    place, *sent = pack(
        where, tenant, slot, activations, wide_size, down_weight.shape[0]
    )
    near = list(range(min(NEAR, wide_size)))
    far = list(range(NEAR, wide_size))
    got = {k: swap(sent[k], "wide", k) if k else sent[k] for k in reversed(range(wide_size))}
    answers = {}
    flags = []
    for group in (near, far):
        if not group:
            continue
        ids, flag, *parts = down(where, [got[k] for k in group], down_weight, cols, narrow_size)
        flags.append(flag[0, LANES - 1])
        parts = [swap(p, "narrow", j) if j else p for j, p in enumerate(parts)]
        outs = up(ids, parts, up_weight, [sent[k].shape[0] for k in group])
        for k, out in zip(group, outs):
            answers[k] = swap(out, "wide", k) if k else out
    more = functools.reduce(jnp.maximum, flags)
    return place, [answers[k] for k in range(wide_size)], more


def on_device(
    activations,
    request_tenants,
    adapter_slot,
    shared_weight,
    adapter_down_weight,
    adapter_up_weight,
):
    rows = activations.shape[0]
    narrow_size = lax.axis_size("narrow")
    axes = (lax.axis_index("wide").astype(i32), lax.axis_index("narrow").astype(i32))
    tenant = request_tenants.reshape(1, rows)
    slot = adapter_slot.reshape(1, -1)
    up_weight = adapter_up_weight.reshape(-1, adapter_up_weight.shape[-1])

    acts = [activations]
    bit = narrow_size // 2
    spread = {0: activations}
    while bit:
        spread.update({j ^ bit: swap(x, "narrow", bit) for j, x in list(spread.items())})
        bit //= 2
    acts = [spread[j] for j in range(narrow_size)]

    rest = (tenant, slot, activations, adapter_down_weight, up_weight)
    place, answers, more = corrections_of(jnp.int32(0), axes, *rest)
    base_out = base(jnp.stack([axes[0], axes[0], axes[1]]), acts, shared_weight)

    def one_turn(base_out):
        return join(base_out, place, answers, bf16)

    def all_turns(base_out):
        def turn_of(state):
            turn, _, total = state
            place, answers, more = corrections_of(turn, axes, *rest)
            return turn + 1, more, join(total, place, answers, f32)

        state = (jnp.int32(0), jnp.float32(1), base_out)
        return lax.while_loop(lambda s: s[1] > 0, turn_of, state)[2].astype(bf16)

    return lax.cond(more > 0, all_turns, one_turn, base_out)


def solution(mesh):
    in_specs = (
        P(("groups", "wide"), "narrow"),
        P(("groups", "wide"), None),
        P(),
        P(None, "narrow"),
        P("wide", "narrow", None),
        P("wide", None, "narrow"),
    )
    out_specs = P(("groups", "wide"), "narrow")
    return jax.shard_map(
        on_device, mesh=mesh, in_specs=in_specs, out_specs=out_specs, check_vma=False
    )
```

```python
import functools

import jax
import jax.numpy as jnp
from jax import lax
from jax.experimental import pallas as pl
from jax.experimental.pallas import tpu as pltpu
from jax.sharding import PartitionSpec as P

KEY_VALUE_COLS = 1024
LANES = 128
MOST = 16
NEAR = 2
NEAR_ROWS = 112
FAR_ROWS = 96
LATER_ROWS = 32
VMEM = pltpu.VMEM
MIB = 1 << 20

f32, bf16, i32 = jnp.float32, jnp.bfloat16, jnp.int32


def first_counts(wide_size, local_count):
    most = -(-(local_count * MOST + 1) // 32) * 32
    return [min(NEAR_ROWS if k < NEAR else FAR_ROWS, most) for k in range(wide_size)]


def swap(x, axis, k):
    size = lax.axis_size(axis)
    return lax.ppermute(x, axis, [(i, i ^ k) for i in range(size)])


def after(x, *others):
    return lax.optimization_barrier((x, *others))[0]


def cost(flops, bytes_accessed):
    return pl.CostEstimate(flops=flops // 10, bytes_accessed=bytes_accessed // 10, transcendentals=0)


def params(mib):
    return pltpu.CompilerParams(vmem_limit_bytes=mib * MIB)


def rows_of(ref, start, count):
    return ref.at[pl.ds(start, count), :]


def pack_kernel(local_count, counts, before_counts, where_ref, tenant_ref, slot_ref, act_ref, *refs):
    wide_size = len(counts)
    place_ref, blocks = refs[0], refs[1 : 1 + wide_size]
    act_held, block_held, in_sem, out_sem = refs[1 + wide_size :]
    rows, features = act_held.shape
    chunks = in_sem.shape[0]
    width = features // chunks

    def load(c):
        cols = pl.ds(c * width, width)
        return pltpu.make_async_copy(act_ref.at[:, cols], act_held.at[:, cols], in_sem.at[c])

    for c in range(chunks):
        load(c).start()

    tenants = slot_ref.shape[1]
    tenant = tenant_ref[...]
    named = tenant == lax.broadcasted_iota(i32, (tenants, rows), 0)
    slots = jnp.broadcast_to(slot_ref[...].astype(f32), (8, tenants)).astype(bf16)
    slot = jnp.dot(slots, named.astype(f32).astype(bf16), preferred_element_type=f32)[:1]
    dest = jnp.floor((slot + 0.5) * (1.0 / local_count))
    adapter = slot - dest * local_count + 1.0
    leap = jnp.bitwise_xor(dest.astype(i32), where_ref[0])
    padded = max(8, wide_size)
    goes = (leap == lax.broadcasted_iota(i32, (padded, rows), 0)).astype(f32)
    earlier = lax.broadcasted_iota(i32, (rows, rows), 0) < lax.broadcasted_iota(
        i32, (rows, rows), 1
    )
    before = jnp.dot(
        goes.astype(bf16), earlier.astype(f32).astype(bf16), preferred_element_type=f32
    )
    position = jnp.sum(goes * before, axis=0, keepdims=True).astype(i32)
    adapters = jnp.broadcast_to(adapter, (8, rows)).astype(bf16)
    place = jnp.full((1, rows), -1, i32)
    more = jnp.zeros((1, rows), f32)
    offsets, here = [], []
    for k in range(wide_size):
        offsets.append(sum(counts[:k]))
        held = counts[k] - 1
        mine = position
        if before_counts is not None:
            mine = position - (before_counts[k] - 1) - (where_ref[2] - 1) * held
        more = jnp.where((leap == k) & (mine >= held), 1.0, more)
        mine = jnp.where((leap == k) & (mine >= 0) & (mine < held), mine, -1)
        place = jnp.where(mine >= 0, mine + offsets[k], place)
        here.append(mine)
    any_more = jnp.max(more, axis=1, keepdims=True)

    def store(k):
        return pltpu.make_async_copy(
            rows_of(block_held, offsets[k], counts[k]), blocks[k], out_sem.at[k]
        )

    for n, k in enumerate(reversed(range(wide_size))):
        count = counts[k]
        part = pl.ds(offsets[k], count)
        perm = (lax.broadcasted_iota(i32, (count, rows), 0) == here[k]).astype(f32).astype(bf16)
        filler = jnp.zeros((LANES - count, rows), bf16)
        ids = lax.dot_general(
            adapters,
            jnp.concatenate([perm, filler], axis=0),
            (((1,), (1,)), ((), ())),
            preferred_element_type=f32,
        )[:1]
        lane = lax.broadcasted_iota(i32, (1, LANES), 1)
        ids = jnp.where(lane == LANES - 1, any_more, ids)
        last = lax.broadcasted_iota(i32, (count, LANES), 0) == count - 1
        for c in range(chunks):
            cols = pl.ds(c * width, width)
            if n == 0:
                load(c).wait()
            body = jnp.dot(perm, act_held[:, cols], preferred_element_type=f32)
            if c == 0:
                first = jnp.where(last, ids, body[:, :LANES])
                body = jnp.concatenate([first, body[:, LANES:]], axis=1)
            block_held[part, cols] = body.astype(bf16)
        store(k).start()
    place_ref[...] = jnp.broadcast_to(place.astype(f32), (LANES, rows)).T
    for k in range(wide_size):
        store(k).wait()


def pack(where, tenant, slot, activations, local_count, counts, before_counts):
    rows, features = activations.shape
    wide_size = len(counts)
    chunks = 4
    anywhere = pl.BlockSpec(memory_space=pl.ANY)
    whole = pl.BlockSpec(memory_space=VMEM)
    return pl.pallas_call(
        functools.partial(pack_kernel, local_count, counts, before_counts),
        out_shape=[jax.ShapeDtypeStruct((rows, LANES), f32)]
        + [jax.ShapeDtypeStruct((c, features), bf16) for c in counts],
        in_specs=[pl.BlockSpec(memory_space=pltpu.SMEM), whole, whole, anywhere],
        out_specs=[whole] + [anywhere for _ in counts],
        scratch_shapes=[
            VMEM((rows, features), bf16),
            VMEM((sum(counts), features), bf16),
            pltpu.SemaphoreType.DMA((chunks,)),
            pltpu.SemaphoreType.DMA((wide_size,)),
        ],
        compiler_params=params(24),
        cost_estimate=cost(2 * sum(counts) * rows * features, 2 * features * (rows + sum(counts))),
        name="pack_rows",
    )(where, tenant, slot, activations)


def down_kernel(count, cols, narrow_size, per_step, where_ref, *refs):
    xs, weight_ref = refs[:count], refs[count]
    flag_ref, ids_ref = refs[count + 1 : count + 3]
    parts = refs[count + 3 : count + 3 + narrow_size]
    held_ref, weight_held, x_sem, weight_sem = refs[count + 3 + narrow_size :]
    steps = weight_sem.shape[0]

    offsets = [sum(x.shape[0] for x in xs[:n]) for n in range(count)]

    def load_x(n):
        return pltpu.make_async_copy(
            xs[n], rows_of(held_ref, offsets[n], xs[n].shape[0]), x_sem.at[n]
        )

    def load_weight(c):
        span = pl.ds(c * per_step, per_step)
        return pltpu.make_async_copy(weight_ref.at[span], weight_held.at[span], weight_sem.at[c])

    for n in range(count):
        load_x(n).start()
    for c in range(steps):
        load_weight(c).start()
    flag = jnp.zeros((1, LANES), f32)
    for n in range(count):
        load_x(n).wait()
        rows = xs[n].shape[0]
        last = held_ref[pl.ds(offsets[n] + rows - 16, 16), :LANES].astype(f32)[15:]
        flag = jnp.maximum(flag, last)
        turned = jnp.broadcast_to(last, (LANES, LANES)).T[:rows]
        keep = lax.broadcasted_iota(i32, (rows, LANES), 0) < rows - 1
        ids_ref[pl.ds(offsets[n], rows), :] = jnp.where(keep, turned, 0.0)
    lane = lax.broadcasted_iota(i32, (1, LANES), 1)
    flag_ref[0, 0] = jnp.max(jnp.where(lane == LANES - 1, flag, 0.0)).astype(i32)

    ids = ids_ref[...]
    total = jnp.zeros(ids.shape, f32)
    for c in range(steps):
        load_weight(c).wait()
        weights = jnp.concatenate(
            [weight_held[c * per_step + j] for j in range(per_step)], axis=1
        )
        found = jnp.dot(held_ref[...], weights, preferred_element_type=f32)
        for j in range(per_step):
            name = c * per_step + j + 1.0
            total = jnp.where(ids == name, found[:, j * LANES : (j + 1) * LANES], total)

    half = total.shape[0] // 2
    rank = LANES // 2
    top, bottom = total[:half], total[half:]
    low = lax.broadcasted_iota(i32, (half, LANES), 1) < rank
    keys = jnp.where(low, top, pltpu.roll(bottom, rank, 1))
    values = jnp.where(low, pltpu.roll(top, rank, 1), bottom)
    for j in range(narrow_size):
        start = jnp.bitwise_xor(where_ref[1], j) * cols
        parts[j][...] = jnp.where(start >= KEY_VALUE_COLS, values, keys).astype(parts[j].dtype)


def down(where, blocks, weight, cols, narrow_size):
    adapters, features, width = weight.shape
    rows = sum(b.shape[0] for b in blocks)
    per_step = min(4, adapters)
    anywhere = pl.BlockSpec(memory_space=pl.ANY)
    whole = pl.BlockSpec(memory_space=VMEM)
    scalar = pl.BlockSpec(memory_space=pltpu.SMEM)
    return pl.pallas_call(
        functools.partial(down_kernel, len(blocks), cols, narrow_size, per_step),
        out_shape=[
            jax.ShapeDtypeStruct((1, 1), i32),
            jax.ShapeDtypeStruct((rows, LANES), f32),
        ]
        + [jax.ShapeDtypeStruct((rows // 2, LANES), bf16 if j else f32) for j in range(narrow_size)],
        in_specs=[scalar] + [anywhere for _ in blocks] + [anywhere],
        out_specs=[scalar, whole] + [whole for _ in range(narrow_size)],
        scratch_shapes=[
            VMEM((rows, features), bf16),
            VMEM(weight.shape, bf16),
            pltpu.SemaphoreType.DMA((len(blocks),)),
            pltpu.SemaphoreType.DMA((adapters // per_step,)),
        ],
        compiler_params=params(32),
        cost_estimate=cost(2 * rows * features * adapters * width, 2 * features * (rows + adapters * width)),
        name="down_maps",
    )(where, *blocks, weight)


def up_kernel(narrow_size, ids_ref, *refs):
    parts, weight_ref, outs = refs[:narrow_size], refs[narrow_size], refs[narrow_size + 1 :]
    total = parts[0][...]
    for part in parts[1:]:
        total = total + part[...].astype(f32)
    low_rank = total.astype(bf16).astype(f32)
    rank = LANES // 2
    turned = pltpu.roll(low_rank, rank, 1)
    low = lax.broadcasted_iota(i32, low_rank.shape, 1) < rank
    twice = jnp.concatenate(
        [jnp.where(low, low_rank, turned), jnp.where(low, turned, low_rank)], axis=0
    )
    ids = ids_ref[...]
    second = (lax.broadcasted_iota(i32, ids.shape, 1) >= rank).astype(f32)
    adapters = weight_ref.shape[0] // rank
    left = [
        jnp.where(ids - second == 2.0 * pair + 1.0, twice, 0.0).astype(bf16)
        for pair in range(adapters // 2)
    ]
    found = jnp.dot(jnp.concatenate(left, axis=1), weight_ref[...], preferred_element_type=f32)
    offset = 0
    for out in outs:
        rows = out.shape[0]
        out[...] = found[offset : offset + rows].astype(bf16)
        offset += rows


def up(ids, parts, weight, counts):
    cols = weight.shape[1]
    return pl.pallas_call(
        functools.partial(up_kernel, len(parts)),
        out_shape=[jax.ShapeDtypeStruct((c, cols), bf16) for c in counts],
        compiler_params=params(24),
        cost_estimate=cost(2 * sum(counts) * weight.size, 2 * weight.size + 2 * sum(counts) * (cols + 512)),
        name="up_maps",
    )(ids, *parts, weight)


def base_kernel(count, where_ref, *refs):
    acts, weight_ref, out_ref = refs[:count], refs[count], refs[count + 1]
    step = pl.program_id(0)
    for j in range(count):

        @pl.when(step == j)
        def _(j=j):
            found = jnp.dot(acts[j][...], weight_ref[...], preferred_element_type=f32)
            out_ref[...] = found if j == 0 else out_ref[...] + found


def base(where, acts, weight):
    rows, features = acts[0].shape
    cols = weight.shape[1]
    count = len(acts)
    return pl.pallas_call(
        functools.partial(base_kernel, count),
        grid_spec=pltpu.PrefetchScalarGridSpec(
            num_scalar_prefetch=1,
            grid=(count,),
            in_specs=[pl.BlockSpec((rows, features), lambda i, where: (0, 0)) for _ in acts]
            + [
                pl.BlockSpec(
                    (features, cols), lambda i, where: (jnp.bitwise_xor(where[1], i), 0)
                )
            ],
            out_specs=pl.BlockSpec((rows, cols), lambda i, where: (0, 0)),
        ),
        out_shape=jax.ShapeDtypeStruct((rows, cols), f32),
        compiler_params=params(24),
        cost_estimate=cost(2 * rows * weight.size, 2 * weight.size + 2 * rows * features * count),
        name="shared_projection",
    )(where, *acts, weight)


def join_kernel(base_ref, place_ref, *refs):
    corrections, out_ref = refs[:-1], refs[-1]
    stacked = jnp.concatenate([c[...] for c in corrections], axis=0)
    rows, count = base_ref.shape[0], stacked.shape[0]
    place = place_ref[:, :1].astype(i32)
    perm = (lax.broadcasted_iota(i32, (rows, count), 1) == place).astype(f32).astype(bf16)
    found = jnp.dot(perm, stacked, preferred_element_type=f32)
    out_ref[...] = (base_ref[...] + found).astype(out_ref.dtype)


def join(base_out, place, corrections, dtype):
    rows, cols = base_out.shape
    count = sum(c.shape[0] for c in corrections)
    return pl.pallas_call(
        join_kernel,
        out_shape=jax.ShapeDtypeStruct((rows, cols), dtype),
        compiler_params=params(24),
        cost_estimate=cost(2 * rows * cols * count, 2 * cols * (count + 3 * rows)),
        name="join_corrections",
    )(base_out, place, *corrections)


def low_rank_parts(where, blocks, down_weight, cols, narrow_size):
    more, ids, *parts = down(where, blocks, down_weight, cols, narrow_size)
    return ids, more[0, 0], parts


def raise_parts(ids, parts, up_weight, counts):
    parts = [swap(p, "narrow", j) if j else p for j, p in enumerate(parts)]
    return up(ids, parts, up_weight, counts)


def later_turn(turn, axes, total, counts, tenant, slot, activations, down_weight, up_weight):
    wide_size, narrow_size = lax.axis_size("wide"), lax.axis_size("narrow")
    where = jnp.stack([*axes, turn])
    place, *sent = pack(
        where, tenant, slot, activations, down_weight.shape[0], [LATER_ROWS] * wide_size, counts
    )
    got = [swap(b, "wide", k) if k else b for k, b in enumerate(sent)]
    ids, more, parts = low_rank_parts(where, got, down_weight, up_weight.shape[1], narrow_size)
    outs = raise_parts(ids, parts, up_weight, [b.shape[0] for b in got])
    answers = [swap(b, "wide", k) if k else b for k, b in enumerate(outs)]
    return join(total, place, answers, f32), more


def on_device(
    activations,
    request_tenants,
    adapter_slot,
    shared_weight,
    adapter_down_weight,
    adapter_up_weight,
):
    rows = activations.shape[0]
    wide_size, narrow_size = lax.axis_size("wide"), lax.axis_size("narrow")
    local_count = adapter_down_weight.shape[0]
    axes = (lax.axis_index("wide").astype(i32), lax.axis_index("narrow").astype(i32))
    where = jnp.stack([*axes, jnp.int32(0)])
    tenant = request_tenants.reshape(1, rows)
    slot = adapter_slot.reshape(1, -1)
    up_weight = adapter_up_weight.reshape(-1, adapter_up_weight.shape[-1])

    cols = up_weight.shape[1]
    counts = first_counts(wide_size, local_count)
    place, *sent = pack(where, tenant, slot, activations, local_count, counts, None)
    got = [swap(b, "wide", k) if k else b for k, b in enumerate(sent)]

    bit = narrow_size // 2
    spread = {0: activations, bit: swap(after(activations, *sent), "narrow", bit)}
    ids, more, parts = low_rank_parts(where, got, adapter_down_weight, cols, narrow_size)
    bit //= 2
    while bit:
        spread.update({j ^ bit: swap(after(x, *parts), "narrow", bit) for j, x in list(spread.items())})
        bit //= 2
    answers = raise_parts(ids, parts, up_weight, counts)
    acts = [after(spread[j], *answers) for j in range(narrow_size)]
    base_out = base(where, acts, shared_weight)
    answers = [swap(answers[k], "wide", k) if k else answers[k] for k in range(wide_size)]

    def done(base_out):
        return join(base_out, place, answers, bf16)

    def go_on(base_out):
        def turn_of(state):
            turn, _, total = state
            total, more = later_turn(
                turn, axes, total, counts, tenant, slot, activations, adapter_down_weight, up_weight
            )
            return turn + 1, more, total

        state = (jnp.int32(1), jnp.int32(1), join(base_out, place, answers, f32))
        return lax.while_loop(lambda s: s[1] > 0, turn_of, state)[2].astype(bf16)

    return lax.cond(more > 0, go_on, done, base_out)


def solution(mesh):
    in_specs = (
        P(("groups", "wide"), "narrow"),
        P(("groups", "wide"), None),
        P(),
        P(None, "narrow"),
        P("wide", "narrow", None),
        P("wide", None, "narrow"),
    )
    out_specs = P(("groups", "wide"), "narrow")
    return jax.shard_map(
        on_device, mesh=mesh, in_specs=in_specs, out_specs=out_specs, check_vma=False
    )
```

```python
import functools

import jax
import jax.numpy as jnp
from jax import lax
from jax.experimental import pallas as pl
from jax.experimental.pallas import tpu as pltpu
from jax.sharding import PartitionSpec as P

KEY_VALUE_COLS = 1024
LANES = 128
MOST = 16
NEAR = 2
NEAR_ROWS = 112
FAR_ROWS = 96
LATER_ROWS = 32
VMEM = pltpu.VMEM
MIB = 1 << 20

f32, bf16, i32 = jnp.float32, jnp.bfloat16, jnp.int32


def first_counts(wide_size, local_count):
    most = -(-(local_count * MOST + 1) // 32) * 32
    return [min(NEAR_ROWS if k < NEAR else FAR_ROWS, most) for k in range(wide_size)]


def swap(x, axis, k):
    size = lax.axis_size(axis)
    return lax.ppermute(x, axis, [(i, i ^ k) for i in range(size)])


def after(x, *others):
    return lax.optimization_barrier((x, *others))[0]


def cost(flops, bytes_accessed):
    return pl.CostEstimate(flops=flops // 10, bytes_accessed=bytes_accessed // 10, transcendentals=0)


def params(mib):
    return pltpu.CompilerParams(vmem_limit_bytes=mib * MIB)


def rows_of(ref, start, count):
    return ref.at[pl.ds(start, count), :]


def pack_kernel(local_count, counts, before_counts, where_ref, tenant_ref, slot_ref, act_ref, *refs):
    wide_size = len(counts)
    begun_ref, place_ref, blocks = refs[0], refs[1], refs[2 : 2 + wide_size]
    act_held, in_sem = refs[2 + wide_size :]
    rows, features = act_held.shape
    chunks = in_sem.shape[0]
    width = features // chunks

    def load(c):
        cols = pl.ds(c * width, width)
        return pltpu.make_async_copy(act_ref.at[:, cols], act_held.at[:, cols], in_sem.at[c])

    for c in range(chunks):
        load(c).start()
    begun_ref[0, 0] = jnp.int32(1)

    tenants = slot_ref.shape[1]
    tenant = tenant_ref[...]
    named = tenant == lax.broadcasted_iota(i32, (tenants, rows), 0)
    slots = jnp.broadcast_to(slot_ref[...].astype(f32), (8, tenants)).astype(bf16)
    slot = jnp.dot(slots, named.astype(f32).astype(bf16), preferred_element_type=f32)[:1]
    dest = jnp.floor((slot + 0.5) * (1.0 / local_count))
    adapter = slot - dest * local_count + 1.0
    leap = jnp.bitwise_xor(dest.astype(i32), where_ref[0])
    padded = max(8, wide_size)
    goes = (leap == lax.broadcasted_iota(i32, (padded, rows), 0)).astype(f32)
    earlier = lax.broadcasted_iota(i32, (rows, rows), 0) < lax.broadcasted_iota(
        i32, (rows, rows), 1
    )
    before = jnp.dot(
        goes.astype(bf16), earlier.astype(f32).astype(bf16), preferred_element_type=f32
    )
    position = jnp.sum(goes * before, axis=0, keepdims=True).astype(i32)
    adapters = jnp.broadcast_to(adapter, (8, rows)).astype(bf16)
    place = jnp.full((1, rows), -1, i32)
    more = jnp.zeros((1, rows), f32)
    offsets, here = [], []
    for k in range(wide_size):
        offsets.append(sum(counts[:k]))
        held = counts[k] - 1
        mine = position
        if before_counts is not None:
            mine = position - (before_counts[k] - 1) - (where_ref[2] - 1) * held
        more = jnp.where((leap == k) & (mine >= held), 1.0, more)
        mine = jnp.where((leap == k) & (mine >= 0) & (mine < held), mine, -1)
        place = jnp.where(mine >= 0, mine + offsets[k], place)
        here.append(mine)
    any_more = jnp.max(more, axis=1, keepdims=True)

    for n, k in enumerate(reversed(range(wide_size))):
        count = counts[k]
        perm = (lax.broadcasted_iota(i32, (count, rows), 0) == here[k]).astype(f32).astype(bf16)
        filler = jnp.zeros((LANES - count, rows), bf16)
        ids = lax.dot_general(
            adapters,
            jnp.concatenate([perm, filler], axis=0),
            (((1,), (1,)), ((), ())),
            preferred_element_type=f32,
        )[:1]
        lane = lax.broadcasted_iota(i32, (1, LANES), 1)
        ids = jnp.where(lane == LANES - 1, any_more, ids)
        last = lax.broadcasted_iota(i32, (count, LANES), 0) == count - 1
        for c in range(chunks):
            cols = pl.ds(c * width, width)
            if n == 0:
                load(c).wait()
            body = jnp.dot(perm, act_held[:, cols], preferred_element_type=f32)
            if c == 0:
                first = jnp.where(last, ids, body[:, :LANES])
                body = jnp.concatenate([first, body[:, LANES:]], axis=1)
            blocks[k][:, cols] = body.astype(bf16)
    place_ref[...] = jnp.broadcast_to(place.astype(f32), (LANES, rows)).T

def pack(where, tenant, slot, activations, local_count, counts, before_counts):
    rows, features = activations.shape
    wide_size = len(counts)
    chunks = 4
    anywhere = pl.BlockSpec(memory_space=pl.ANY)
    whole = pl.BlockSpec(memory_space=VMEM)
    scalar = pl.BlockSpec(memory_space=pltpu.SMEM)
    return pl.pallas_call(
        functools.partial(pack_kernel, local_count, counts, before_counts),
        out_shape=[
            jax.ShapeDtypeStruct((1, 1), i32),
            jax.ShapeDtypeStruct((rows, LANES), f32),
        ]
        + [jax.ShapeDtypeStruct((c, features), bf16) for c in counts],
        in_specs=[scalar, whole, whole, anywhere],
        out_specs=[scalar, whole] + [whole for _ in counts],
        scratch_shapes=[VMEM((rows, features), bf16), pltpu.SemaphoreType.DMA((chunks,))],
        compiler_params=params(24),
        cost_estimate=cost(2 * sum(counts) * rows * features, 2 * features * (rows + sum(counts))),
        name="pack_rows",
    )(where, tenant, slot, activations)


def stage_kernel(weight_ref, out_ref, sem):
    adapters, _, width = weight_ref.shape

    def load(j):
        return pltpu.make_async_copy(
            weight_ref.at[j], out_ref.at[:, pl.ds(j * width, width)], sem.at[j]
        )

    for j in range(adapters):
        load(j).start()
    for j in range(adapters):
        load(j).wait()


def stage(weight):
    adapters, features, width = weight.shape
    return pl.pallas_call(
        stage_kernel,
        out_shape=pltpu.VMEM((features, adapters * width), weight.dtype),
        in_specs=[pl.BlockSpec(memory_space=pl.ANY)],
        out_specs=pl.BlockSpec(memory_space=VMEM),
        scratch_shapes=[pltpu.SemaphoreType.DMA((adapters,))],
        compiler_params=params(16),
        cost_estimate=cost(1, 4 * weight.size),
        name="stage_down_maps",
    )(weight)


def down_kernel(count, cols, narrow_size, per_step, where_ref, *refs):
    xs, weight_ref = refs[:count], refs[count]
    flag_ref, ids_ref = refs[count + 1 : count + 3]
    parts = refs[count + 3 : count + 3 + narrow_size]
    (held_ref,) = refs[count + 3 + narrow_size :]
    steps = weight_ref.shape[1] // (per_step * LANES)

    offsets = [sum(x.shape[0] for x in xs[:n]) for n in range(count)]

    flag = jnp.zeros((1, LANES), f32)
    for n in range(count):
        rows = xs[n].shape[0]
        held_ref[pl.ds(offsets[n], rows), :] = xs[n][...]
        last = held_ref[pl.ds(offsets[n] + rows - 16, 16), :LANES].astype(f32)[15:]
        flag = jnp.maximum(flag, last)
        turned = jnp.broadcast_to(last, (LANES, LANES)).T[:rows]
        keep = lax.broadcasted_iota(i32, (rows, LANES), 0) < rows - 1
        ids_ref[pl.ds(offsets[n], rows), :] = jnp.where(keep, turned, 0.0)
    lane = lax.broadcasted_iota(i32, (1, LANES), 1)
    flag_ref[0, 0] = jnp.max(jnp.where(lane == LANES - 1, flag, 0.0)).astype(i32)

    ids = ids_ref[...]
    total = jnp.zeros(ids.shape, f32)
    for c in range(steps):
        weights = weight_ref[:, c * per_step * LANES : (c + 1) * per_step * LANES]
        found = jnp.dot(held_ref[...], weights, preferred_element_type=f32)
        for j in range(per_step):
            name = c * per_step + j + 1.0
            total = jnp.where(ids == name, found[:, j * LANES : (j + 1) * LANES], total)

    half = total.shape[0] // 2
    rank = LANES // 2
    top, bottom = total[:half], total[half:]
    low = lax.broadcasted_iota(i32, (half, LANES), 1) < rank
    keys = jnp.where(low, top, pltpu.roll(bottom, rank, 1))
    values = jnp.where(low, pltpu.roll(top, rank, 1), bottom)
    for j in range(narrow_size):
        start = jnp.bitwise_xor(where_ref[1], j) * cols
        parts[j][...] = jnp.where(start >= KEY_VALUE_COLS, values, keys).astype(parts[j].dtype)


def down(where, blocks, weight, cols, narrow_size):
    features, width = weight.shape
    rows = sum(b.shape[0] for b in blocks)
    per_step = min(4, width // LANES)
    whole = pl.BlockSpec(memory_space=VMEM)
    scalar = pl.BlockSpec(memory_space=pltpu.SMEM)
    return pl.pallas_call(
        functools.partial(down_kernel, len(blocks), cols, narrow_size, per_step),
        out_shape=[
            jax.ShapeDtypeStruct((1, 1), i32),
            jax.ShapeDtypeStruct((rows, LANES), f32),
        ]
        + [jax.ShapeDtypeStruct((rows // 2, LANES), bf16 if j else f32) for j in range(narrow_size)],
        in_specs=[scalar] + [whole for _ in blocks] + [whole],
        out_specs=[scalar, whole] + [whole for _ in range(narrow_size)],
        scratch_shapes=[VMEM((rows, features), bf16)],
        compiler_params=params(32),
        cost_estimate=cost(2 * rows * features * width, 2 * features * (rows + width)),
        name="down_maps",
    )(where, *blocks, weight)


def up_kernel(narrow_size, ids_ref, *refs):
    parts, weight_ref, outs = refs[:narrow_size], refs[narrow_size], refs[narrow_size + 1 :]
    total = parts[0][...]
    for part in parts[1:]:
        total = total + part[...].astype(f32)
    low_rank = total.astype(bf16).astype(f32)
    rank = LANES // 2
    turned = pltpu.roll(low_rank, rank, 1)
    low = lax.broadcasted_iota(i32, low_rank.shape, 1) < rank
    twice = jnp.concatenate(
        [jnp.where(low, low_rank, turned), jnp.where(low, turned, low_rank)], axis=0
    )
    ids = ids_ref[...]
    second = (lax.broadcasted_iota(i32, ids.shape, 1) >= rank).astype(f32)
    adapters = weight_ref.shape[0] // rank
    left = [
        jnp.where(ids - second == 2.0 * pair + 1.0, twice, 0.0).astype(bf16)
        for pair in range(adapters // 2)
    ]
    found = jnp.dot(jnp.concatenate(left, axis=1), weight_ref[...], preferred_element_type=f32)
    offset = 0
    for out in outs:
        rows = out.shape[0]
        out[...] = found[offset : offset + rows].astype(bf16)
        offset += rows


def up(ids, parts, weight, counts):
    cols = weight.shape[1]
    return pl.pallas_call(
        functools.partial(up_kernel, len(parts)),
        out_shape=[jax.ShapeDtypeStruct((c, cols), bf16) for c in counts],
        compiler_params=params(24),
        cost_estimate=cost(2 * sum(counts) * weight.size, 2 * weight.size + 2 * sum(counts) * (cols + 512)),
        name="up_maps",
    )(ids, *parts, weight)


def base_kernel(count, where_ref, *refs):
    acts, weight_ref, out_ref = refs[:count], refs[count], refs[count + 1]
    step = pl.program_id(0)
    for j in range(count):

        @pl.when(step == j)
        def _(j=j):
            found = jnp.dot(acts[j][...], weight_ref[...], preferred_element_type=f32)
            out_ref[...] = found if j == 0 else out_ref[...] + found


def base(where, acts, weight):
    rows, features = acts[0].shape
    cols = weight.shape[1]
    count = len(acts)
    return pl.pallas_call(
        functools.partial(base_kernel, count),
        grid_spec=pltpu.PrefetchScalarGridSpec(
            num_scalar_prefetch=1,
            grid=(count,),
            in_specs=[pl.BlockSpec((rows, features), lambda i, where: (0, 0)) for _ in acts]
            + [
                pl.BlockSpec(
                    (features, cols), lambda i, where: (jnp.bitwise_xor(where[1], i), 0)
                )
            ],
            out_specs=pl.BlockSpec((rows, cols), lambda i, where: (0, 0)),
        ),
        out_shape=jax.ShapeDtypeStruct((rows, cols), f32),
        compiler_params=params(24),
        cost_estimate=cost(2 * rows * weight.size, 2 * weight.size + 2 * rows * features * count),
        name="shared_projection",
    )(where, *acts, weight)


def join_kernel(base_ref, place_ref, *refs):
    corrections, out_ref = refs[:-1], refs[-1]
    stacked = jnp.concatenate([c[...] for c in corrections], axis=0)
    rows, count = base_ref.shape[0], stacked.shape[0]
    place = place_ref[:, :1].astype(i32)
    perm = (lax.broadcasted_iota(i32, (rows, count), 1) == place).astype(f32).astype(bf16)
    found = jnp.dot(perm, stacked, preferred_element_type=f32)
    out_ref[...] = (base_ref[...] + found).astype(out_ref.dtype)


def join(base_out, place, corrections, dtype):
    rows, cols = base_out.shape
    count = sum(c.shape[0] for c in corrections)
    return pl.pallas_call(
        join_kernel,
        out_shape=jax.ShapeDtypeStruct((rows, cols), dtype),
        compiler_params=params(24),
        cost_estimate=cost(2 * rows * cols * count, 2 * cols * (count + 3 * rows)),
        name="join_corrections",
    )(base_out, place, *corrections)


def low_rank_parts(where, blocks, down_weight, cols, narrow_size):
    more, ids, *parts = down(where, blocks, down_weight, cols, narrow_size)
    return ids, more[0, 0], parts


def raise_parts(ids, parts, up_weight, counts):
    parts = [swap(p, "narrow", j) if j else p for j, p in enumerate(parts)]
    return up(ids, parts, up_weight, counts)


def later_turn(turn, axes, total, counts, tenant, slot, activations, down_weight, up_weight):
    wide_size, narrow_size = lax.axis_size("wide"), lax.axis_size("narrow")
    where = jnp.stack([*axes, turn])
    _, place, *sent = pack(
        where, tenant, slot, activations, down_weight.shape[0], [LATER_ROWS] * wide_size, counts
    )
    got = [swap(b, "wide", k) if k else b for k, b in enumerate(sent)]
    staged = stage(down_weight)
    ids, more, parts = low_rank_parts(where, got, staged, up_weight.shape[1], narrow_size)
    outs = raise_parts(ids, parts, up_weight, [b.shape[0] for b in got])
    answers = [swap(b, "wide", k) if k else b for k, b in enumerate(outs)]
    return join(total, place, answers, f32), more


def on_device(
    activations,
    request_tenants,
    adapter_slot,
    shared_weight,
    adapter_down_weight,
    adapter_up_weight,
):
    rows = activations.shape[0]
    wide_size, narrow_size = lax.axis_size("wide"), lax.axis_size("narrow")
    local_count = adapter_down_weight.shape[0]
    axes = (lax.axis_index("wide").astype(i32), lax.axis_index("narrow").astype(i32))
    where = jnp.stack([*axes, jnp.int32(0)])
    tenant = request_tenants.reshape(1, rows)
    slot = adapter_slot.reshape(1, -1)
    up_weight = adapter_up_weight.reshape(-1, adapter_up_weight.shape[-1])

    cols = up_weight.shape[1]
    counts = first_counts(wide_size, local_count)
    begun, place, *sent = pack(where, tenant, slot, activations, local_count, counts, None)
    got = [swap(b, "wide", k) if k else b for k, b in enumerate(sent)]

    def beside_rows(activations, shared_weight, down_weight):
        spread = {0: activations}
        bit = narrow_size // 2
        while bit:
            spread.update({j ^ bit: swap(x, "narrow", bit) for j, x in list(spread.items())})
            bit //= 2
        return base(where, [spread[j] for j in range(narrow_size)], shared_weight), stage(down_weight)

    def never(activations, shared_weight, down_weight):
        adapters, features, width = down_weight.shape
        return jnp.zeros((rows, cols), f32), jnp.zeros((features, adapters * width), bf16)

    base_out, staged = lax.cond(
        begun[0, 0] > 0, beside_rows, never, activations, shared_weight, adapter_down_weight
    )
    ids, more, parts = low_rank_parts(
        where, [after(b, base_out) for b in got], staged, cols, narrow_size
    )
    answers = raise_parts(ids, parts, up_weight, counts)
    answers = [swap(answers[k], "wide", k) if k else answers[k] for k in range(wide_size)]

    def done(base_out):
        return join(base_out, place, answers, bf16)

    def go_on(base_out):
        def turn_of(state):
            turn, _, total = state
            total, more = later_turn(
                turn, axes, total, counts, tenant, slot, activations, adapter_down_weight, up_weight
            )
            return turn + 1, more, total

        state = (jnp.int32(1), jnp.int32(1), join(base_out, place, answers, f32))
        return lax.while_loop(lambda s: s[1] > 0, turn_of, state)[2].astype(bf16)

    return lax.cond(more > 0, go_on, done, base_out)


def solution(mesh):
    in_specs = (
        P(("groups", "wide"), "narrow"),
        P(("groups", "wide"), None),
        P(),
        P(None, "narrow"),
        P("wide", "narrow", None),
        P("wide", None, "narrow"),
    )
    out_specs = P(("groups", "wide"), "narrow")
    return jax.shard_map(
        on_device, mesh=mesh, in_specs=in_specs, out_specs=out_specs, check_vma=False
    )
```

```python
import functools

import jax
import jax.numpy as jnp
from jax import lax
from jax.experimental import pallas as pl
from jax.experimental.pallas import tpu as pltpu
from jax.sharding import PartitionSpec as P

KEY_VALUE_COLS = 1024
LANES = 128
MOST = 16
NEAR = 2
NEAR_ROWS = 112
FAR_ROWS = 96
LATER_ROWS = 32
VMEM = pltpu.VMEM
MIB = 1 << 20

f32, bf16, i32 = jnp.float32, jnp.bfloat16, jnp.int32


def first_counts(wide_size, local_count):
    most = -(-(local_count * MOST + 1) // 32) * 32
    return [min(NEAR_ROWS if k < NEAR else FAR_ROWS, most) for k in range(wide_size)]


def swap(x, axis, k):
    size = lax.axis_size(axis)
    return lax.ppermute(x, axis, [(i, i ^ k) for i in range(size)])


def after(x, *others):
    return lax.optimization_barrier((x, *others))[0]


def after_all(xs, *others):
    return lax.optimization_barrier((tuple(xs), others))[0]


def cost(flops, bytes_accessed):
    return pl.CostEstimate(flops=flops // 10, bytes_accessed=bytes_accessed // 10, transcendentals=0)


def params(mib):
    return pltpu.CompilerParams(vmem_limit_bytes=mib * MIB)


def rows_of(ref, start, count):
    return ref.at[pl.ds(start, count), :]


def pack_kernel(local_count, counts, before_counts, where_ref, tenant_ref, slot_ref, act_ref, *refs):
    wide_size = len(counts)
    begun_ref, place_ref, blocks = refs[0], refs[1], refs[2 : 2 + wide_size]
    act_held, in_sem = refs[2 + wide_size :]
    rows, features = act_held.shape
    chunks = in_sem.shape[0]
    width = features // chunks

    def load(c):
        cols = pl.ds(c * width, width)
        return pltpu.make_async_copy(act_ref.at[:, cols], act_held.at[:, cols], in_sem.at[c])

    for c in range(chunks):
        load(c).start()
    begun_ref[0, 0] = jnp.int32(1)

    tenants = slot_ref.shape[1]
    tenant = tenant_ref[...]
    named = tenant == lax.broadcasted_iota(i32, (tenants, rows), 0)
    slots = jnp.broadcast_to(slot_ref[...].astype(f32), (8, tenants)).astype(bf16)
    slot = jnp.dot(slots, named.astype(f32).astype(bf16), preferred_element_type=f32)[:1]
    dest = jnp.floor((slot + 0.5) * (1.0 / local_count))
    adapter = slot - dest * local_count + 1.0
    leap = jnp.bitwise_xor(dest.astype(i32), where_ref[0])
    padded = max(8, wide_size)
    goes = (leap == lax.broadcasted_iota(i32, (padded, rows), 0)).astype(f32)
    earlier = lax.broadcasted_iota(i32, (rows, rows), 0) < lax.broadcasted_iota(
        i32, (rows, rows), 1
    )
    before = jnp.dot(
        goes.astype(bf16), earlier.astype(f32).astype(bf16), preferred_element_type=f32
    )
    position = jnp.sum(goes * before, axis=0, keepdims=True).astype(i32)
    adapters = jnp.broadcast_to(adapter, (8, rows)).astype(bf16)
    place = jnp.full((1, rows), -1, i32)
    more = jnp.zeros((1, rows), f32)
    offsets, here = [], []
    for k in range(wide_size):
        offsets.append(sum(counts[:k]))
        held = counts[k] - 1
        mine = position
        if before_counts is not None:
            mine = position - (before_counts[k] - 1) - (where_ref[2] - 1) * held
        more = jnp.where((leap == k) & (mine >= held), 1.0, more)
        mine = jnp.where((leap == k) & (mine >= 0) & (mine < held), mine, -1)
        place = jnp.where(mine >= 0, mine + offsets[k], place)
        here.append(mine)
    any_more = jnp.max(more, axis=1, keepdims=True)

    for n, k in enumerate(reversed(range(wide_size))):
        count = counts[k]
        perm = (lax.broadcasted_iota(i32, (count, rows), 0) == here[k]).astype(f32).astype(bf16)
        filler = jnp.zeros((LANES - count, rows), bf16)
        ids = lax.dot_general(
            adapters,
            jnp.concatenate([perm, filler], axis=0),
            (((1,), (1,)), ((), ())),
            preferred_element_type=f32,
        )[:1]
        lane = lax.broadcasted_iota(i32, (1, LANES), 1)
        ids = jnp.where(lane == LANES - 1, any_more, ids)
        last = lax.broadcasted_iota(i32, (count, LANES), 0) == count - 1
        for c in range(chunks):
            cols = pl.ds(c * width, width)
            if n == 0:
                load(c).wait()
            body = jnp.dot(perm, act_held[:, cols], preferred_element_type=f32)
            if c == 0:
                first = jnp.where(last, ids, body[:, :LANES])
                body = jnp.concatenate([first, body[:, LANES:]], axis=1)
            blocks[k][:, cols] = body.astype(bf16)
    place_ref[...] = jnp.broadcast_to(place.astype(f32), (LANES, rows)).T

def pack(where, tenant, slot, activations, local_count, counts, before_counts):
    rows, features = activations.shape
    wide_size = len(counts)
    chunks = 4
    anywhere = pl.BlockSpec(memory_space=pl.ANY)
    whole = pl.BlockSpec(memory_space=VMEM)
    scalar = pl.BlockSpec(memory_space=pltpu.SMEM)
    return pl.pallas_call(
        functools.partial(pack_kernel, local_count, counts, before_counts),
        out_shape=[
            jax.ShapeDtypeStruct((1, 1), i32),
            jax.ShapeDtypeStruct((rows, LANES), f32),
        ]
        + [jax.ShapeDtypeStruct((c, features), bf16) for c in counts],
        in_specs=[scalar, whole, whole, anywhere],
        out_specs=[scalar, whole] + [whole for _ in counts],
        scratch_shapes=[VMEM((rows, features), bf16), pltpu.SemaphoreType.DMA((chunks,))],
        compiler_params=params(12),
        cost_estimate=cost(2 * sum(counts) * rows * features, 2 * features * (rows + sum(counts))),
        name="pack_rows",
    )(where, tenant, slot, activations)


def stage_kernel(down_ref, up_ref, down_out, up_out, sem):
    adapters, _, width = down_ref.shape
    copies = [
        pltpu.make_async_copy(
            down_ref.at[j], down_out.at[:, pl.ds(j * width, width)], sem.at[j]
        )
        for j in range(adapters)
    ]
    copies.append(pltpu.make_async_copy(up_ref, up_out, sem.at[adapters]))
    for copy in copies:
        copy.start()
    for copy in copies:
        copy.wait()


def stage(down_weight, up_weight):
    adapters, features, width = down_weight.shape
    whole = pl.BlockSpec(memory_space=VMEM)
    return pl.pallas_call(
        stage_kernel,
        out_shape=[
            pltpu.VMEM((features, adapters * width), down_weight.dtype),
            pltpu.VMEM(up_weight.shape, up_weight.dtype),
        ],
        in_specs=[pl.BlockSpec(memory_space=pl.ANY)] * 2,
        out_specs=[whole, whole],
        scratch_shapes=[pltpu.SemaphoreType.DMA((adapters + 1,))],
        compiler_params=params(12),
        cost_estimate=cost(10, 10),
        name="stage_maps",
    )(down_weight, up_weight)


def down_kernel(count, cols, narrow_size, per_step, where_ref, *refs):
    xs, weight_ref = refs[:count], refs[count]
    flag_ref, ids_ref = refs[count + 1 : count + 3]
    parts = refs[count + 3 : count + 3 + narrow_size]
    (held_ref,) = refs[count + 3 + narrow_size :]
    steps = weight_ref.shape[1] // (per_step * LANES)

    offsets = [sum(x.shape[0] for x in xs[:n]) for n in range(count)]

    flag = jnp.zeros((1, LANES), f32)
    for n in range(count):
        rows = xs[n].shape[0]
        held_ref[pl.ds(offsets[n], rows), :] = xs[n][...]
        last = held_ref[pl.ds(offsets[n] + rows - 16, 16), :LANES].astype(f32)[15:]
        flag = jnp.maximum(flag, last)
        turned = jnp.broadcast_to(last, (LANES, LANES)).T[:rows]
        keep = lax.broadcasted_iota(i32, (rows, LANES), 0) < rows - 1
        ids_ref[pl.ds(offsets[n], rows), :] = jnp.where(keep, turned, 0.0)
    lane = lax.broadcasted_iota(i32, (1, LANES), 1)
    flag_ref[0, 0] = jnp.max(jnp.where(lane == LANES - 1, flag, 0.0)).astype(i32)

    ids = ids_ref[...]
    total = jnp.zeros(ids.shape, f32)
    for c in range(steps):
        weights = weight_ref[:, c * per_step * LANES : (c + 1) * per_step * LANES]
        found = jnp.dot(held_ref[...], weights, preferred_element_type=f32)
        for j in range(per_step):
            name = c * per_step + j + 1.0
            total = jnp.where(ids == name, found[:, j * LANES : (j + 1) * LANES], total)

    half = total.shape[0] // 2
    rank = LANES // 2
    top, bottom = total[:half], total[half:]
    low = lax.broadcasted_iota(i32, (half, LANES), 1) < rank
    keys = jnp.where(low, top, pltpu.roll(bottom, rank, 1))
    values = jnp.where(low, pltpu.roll(top, rank, 1), bottom)
    for j in range(narrow_size):
        start = jnp.bitwise_xor(where_ref[1], j) * cols
        parts[j][...] = jnp.where(start >= KEY_VALUE_COLS, values, keys).astype(parts[j].dtype)


def down(where, blocks, weight, cols, narrow_size):
    features, width = weight.shape
    rows = sum(b.shape[0] for b in blocks)
    per_step = min(4, width // LANES)
    whole = pl.BlockSpec(memory_space=VMEM)
    scalar = pl.BlockSpec(memory_space=pltpu.SMEM)
    return pl.pallas_call(
        functools.partial(down_kernel, len(blocks), cols, narrow_size, per_step),
        out_shape=[
            jax.ShapeDtypeStruct((1, 1), i32),
            jax.ShapeDtypeStruct((rows, LANES), f32),
        ]
        + [jax.ShapeDtypeStruct((rows // 2, LANES), bf16 if j else f32) for j in range(narrow_size)],
        in_specs=[scalar] + [whole for _ in blocks] + [whole],
        out_specs=[scalar, whole] + [whole for _ in range(narrow_size)],
        scratch_shapes=[VMEM((rows, features), bf16)],
        compiler_params=params(18),
        cost_estimate=cost(2 * rows * features * width, 2 * features * (rows + width)),
        name="down_maps",
    )(where, *blocks, weight)


def up_kernel(narrow_size, ids_ref, *refs):
    parts, weight_ref, outs = refs[:narrow_size], refs[narrow_size], refs[narrow_size + 1 :]
    total = parts[0][...]
    for part in parts[1:]:
        total = total + part[...].astype(f32)
    low_rank = total.astype(bf16).astype(f32)
    rank = LANES // 2
    turned = pltpu.roll(low_rank, rank, 1)
    low = lax.broadcasted_iota(i32, low_rank.shape, 1) < rank
    twice = jnp.concatenate(
        [jnp.where(low, low_rank, turned), jnp.where(low, turned, low_rank)], axis=0
    )
    ids = ids_ref[...]
    second = (lax.broadcasted_iota(i32, ids.shape, 1) >= rank).astype(f32)
    adapters = weight_ref.shape[0] // rank
    left = [
        jnp.where(ids - second == 2.0 * pair + 1.0, twice, 0.0).astype(bf16)
        for pair in range(adapters // 2)
    ]
    found = jnp.dot(jnp.concatenate(left, axis=1), weight_ref[...], preferred_element_type=f32)
    offset = 0
    for out in outs:
        rows = out.shape[0]
        out[...] = found[offset : offset + rows].astype(bf16)
        offset += rows


def up(ids, parts, weight, counts):
    cols = weight.shape[1]
    return pl.pallas_call(
        functools.partial(up_kernel, len(parts)),
        out_shape=[jax.ShapeDtypeStruct((c, cols), bf16) for c in counts],
        compiler_params=params(10),
        cost_estimate=cost(2 * sum(counts) * weight.size, 2 * weight.size + 2 * sum(counts) * (cols + 512)),
        name="up_maps",
    )(ids, *parts, weight)


def base_kernel(count, where_ref, *refs):
    acts, weight_ref, so_far, out_ref = refs[:count], refs[count], refs[count + 1 : -1], refs[-1]
    step = pl.program_id(0)
    for j in range(count):

        @pl.when(step == j)
        def _(j=j):
            found = jnp.dot(acts[j][...], weight_ref[...], preferred_element_type=f32)
            if j:
                found = out_ref[...] + found
            elif so_far:
                found = so_far[0][...] + found
            out_ref[...] = found


def base(where, acts, first, stride, weight, so_far):
    rows, features = acts[0].shape
    cols = weight.shape[1]
    count = len(acts)
    given = [] if so_far is None else [so_far]
    return pl.pallas_call(
        functools.partial(base_kernel, count),
        grid_spec=pltpu.PrefetchScalarGridSpec(
            num_scalar_prefetch=1,
            grid=(count,),
            in_specs=[pl.BlockSpec((rows, features), lambda i, where: (0, 0)) for _ in acts]
            + [
                pl.BlockSpec(
                    (features, cols),
                    lambda i, where: (jnp.bitwise_xor(where[1], first + i * stride), 0),
                )
            ]
            + [pl.BlockSpec((rows, cols), lambda i, where: (0, 0)) for _ in given],
            out_specs=pl.BlockSpec((rows, cols), lambda i, where: (0, 0)),
        ),
        out_shape=jax.ShapeDtypeStruct((rows, cols), f32),
        compiler_params=params(14),
        cost_estimate=cost(2 * rows * features * count * cols, 2 * features * count * (cols + rows)),
        name="shared_projection",
    )(where, *acts, weight, *given)


def join_kernel(base_ref, place_ref, *refs):
    corrections, out_ref = refs[:-1], refs[-1]
    stacked = jnp.concatenate([c[...] for c in corrections], axis=0)
    rows, count = base_ref.shape[0], stacked.shape[0]
    place = place_ref[:, :1].astype(i32)
    perm = (lax.broadcasted_iota(i32, (rows, count), 1) == place).astype(f32).astype(bf16)
    found = jnp.dot(perm, stacked, preferred_element_type=f32)
    out_ref[...] = (base_ref[...] + found).astype(out_ref.dtype)


def join(base_out, place, corrections, dtype):
    rows, cols = base_out.shape
    count = sum(c.shape[0] for c in corrections)
    return pl.pallas_call(
        join_kernel,
        out_shape=jax.ShapeDtypeStruct((rows, cols), dtype),
        compiler_params=params(10),
        cost_estimate=cost(2 * rows * cols * count, 2 * cols * (count + 3 * rows)),
        name="join_corrections",
    )(base_out, place, *corrections)


def answers_for(where, blocks, staged, narrow_size):
    down_weight, up_weight = staged
    more, ids, *parts = down(where, blocks, down_weight, up_weight.shape[1], narrow_size)
    parts = [swap(p, "narrow", j) if j else p for j, p in enumerate(parts)]
    return up(ids, parts, up_weight, [b.shape[0] for b in blocks]), more


def later_turn(turn, axes, total, counts, tenant, slot, activations, down_weight, up_weight):
    wide_size, narrow_size = lax.axis_size("wide"), lax.axis_size("narrow")
    where = jnp.stack([*axes, turn])
    _, place, *sent = pack(
        where, tenant, slot, activations, down_weight.shape[0], [LATER_ROWS] * wide_size, counts
    )
    got = [swap(b, "wide", k) if k else b for k, b in enumerate(sent)]
    outs, more = answers_for(where, got, stage(down_weight, up_weight), narrow_size)
    answers = [swap(b, "wide", k) if k else b for k, b in enumerate(outs)]
    return join(total, place, answers, f32), more[0, 0]


def on_device(
    activations,
    request_tenants,
    adapter_slot,
    shared_weight,
    adapter_down_weight,
    adapter_up_weight,
):
    rows = activations.shape[0]
    wide_size, narrow_size = lax.axis_size("wide"), lax.axis_size("narrow")
    local_count = adapter_down_weight.shape[0]
    axes = (lax.axis_index("wide").astype(i32), lax.axis_index("narrow").astype(i32))
    where = jnp.stack([*axes, jnp.int32(0)])
    tenant = request_tenants.reshape(1, rows)
    slot = adapter_slot.reshape(1, -1)
    up_weight = adapter_up_weight.reshape(-1, adapter_up_weight.shape[-1])

    cols = up_weight.shape[1]
    counts = first_counts(wide_size, local_count)
    begun, place, *sent = pack(where, tenant, slot, activations, local_count, counts, None)
    order = sorted(range(wide_size), key=lambda k: (k == wide_size // 2, -k))
    early, late = (order[:-1], order[-1:]) if wide_size > 2 else (order, [])
    got = {k: swap(sent[k], "wide", k) if k else sent[k] for k in order}
    half = narrow_size // 2
    across = swap(after(activations, *sent), "narrow", half) if half else None
    maps = after_all((adapter_down_weight, up_weight), *sent)
    staged = stage(*maps)

    def step(work, *operands):
        def never(*operands):
            return jax.tree.map(
                lambda s: jnp.zeros(s.shape, s.dtype), jax.eval_shape(work, *operands)
            )

        return lax.cond(begun[0, 0] > 0, work, never, *operands)

    def early_work(blocks, staged):
        return answers_for(where, blocks, staged, narrow_size)

    def shared_work(activations, across, shared_weight, maps):
        pairs = {0: [activations] + ([across] if half else [])}
        bit = half // 2
        while bit:
            for g, pair in list(pairs.items()):
                pairs[g ^ bit] = [swap(x, "narrow", bit) for x in pair]
            bit //= 2
        total = None
        for g in sorted(pairs):
            total = base(where, pairs[g], g, half, shared_weight, total)
        return total, stage(*maps)

    def late_work(blocks, staged):
        outs, more = answers_for(where, blocks, staged, narrow_size)
        return [swap(b, "wide", k) for k, b in zip(late, outs)], more

    outs, more = step(early_work, [got[k] for k in early], staged)
    more = more[0, 0]
    answers = dict(zip(early, outs))
    base_out, staged = step(
        shared_work, *after_all((activations, across, shared_weight, maps), *outs)
    )
    if late:
        arrived = [after(got[k], base_out) for k in late]
        answers = {k: swap(after(b, *arrived), "wide", k) if k else b for k, b in answers.items()}
        outs, flag = step(late_work, arrived, staged)
        more = jnp.maximum(more, flag[0, 0])
        answers.update(zip(late, outs))
    else:
        answers = {k: swap(b, "wide", k) if k else b for k, b in answers.items()}
    answers = [answers[k] for k in range(wide_size)]

    def done(base_out):
        return join(base_out, place, answers, bf16)

    def go_on(base_out):
        def turn_of(state):
            turn, _, total = state
            total, more = later_turn(
                turn, axes, total, counts, tenant, slot, activations, adapter_down_weight, up_weight
            )
            return turn + 1, more, total

        state = (jnp.int32(1), jnp.int32(1), join(base_out, place, answers, f32))
        return lax.while_loop(lambda s: s[1] > 0, turn_of, state)[2].astype(bf16)

    return lax.cond(more > 0, go_on, done, base_out)


def solution(mesh):
    in_specs = (
        P(("groups", "wide"), "narrow"),
        P(("groups", "wide"), None),
        P(),
        P(None, "narrow"),
        P("wide", "narrow", None),
        P("wide", None, "narrow"),
    )
    out_specs = P(("groups", "wide"), "narrow")
    return jax.shard_map(
        on_device, mesh=mesh, in_specs=in_specs, out_specs=out_specs, check_vma=False
    )
```

```python
import functools

import jax
import jax.numpy as jnp
from jax import lax
from jax.experimental import pallas as pl
from jax.experimental.pallas import tpu as pltpu
from jax.sharding import PartitionSpec as P

KEY_VALUE_COLS = 1024
LANES = 128
MOST = 16
NEAR = 2
NEAR_ROWS = 112
FAR_ROWS = 96
LATER_ROWS = 32
VMEM = pltpu.VMEM
MIB = 1 << 20

f32, bf16, i32 = jnp.float32, jnp.bfloat16, jnp.int32


def first_turn(wide_size, local_count):
    most = -(-(local_count * MOST + 1) // 32) * 32
    blocks = [(k, 0, min(NEAR_ROWS if k < NEAR else FAR_ROWS, most)) for k in range(wide_size)]
    half = wide_size // 2
    return blocks[1 : half + 1][::-1], blocks[half + 1 :] + blocks[:1]


def ends(blocks, wide_size):
    return [max(start + count - 1 for j, start, count in blocks if j == k) for k in range(wide_size)]


def swap(x, axis, k):
    size = lax.axis_size(axis)
    return lax.ppermute(x, axis, [(i, i ^ k) for i in range(size)])


def after(x, *others):
    return lax.optimization_barrier((x, *others))[0]


def after_all(xs, *others):
    return lax.optimization_barrier((xs, others))[0]


def cost(flops, bytes_accessed):
    return pl.CostEstimate(flops=flops // 1000, bytes_accessed=bytes_accessed // 1000, transcendentals=0)


def params(mib):
    return pltpu.CompilerParams(vmem_limit_bytes=mib * MIB)


def rows_of(ref, start, count):
    return ref.at[pl.ds(start, count), :]


def pack_kernel(
    local_count, wide_size, layout, span, per_turn, where_ref, tenant_ref, slot_ref, act_ref, *refs
):
    picked = range(*span)
    begun_ref, place_ref = refs[:2]
    blocks = dict(zip(picked, refs[2:-2]))
    act_held, in_sem = refs[-2:]
    rows, features = act_held.shape
    chunks = in_sem.shape[0]
    width = features // chunks

    def load(c):
        cols = pl.ds(c * width, width)
        return pltpu.make_async_copy(act_ref.at[:, cols], act_held.at[:, cols], in_sem.at[c])

    for c in range(chunks):
        load(c).start()
    begun_ref[0, 0] = jnp.int32(1)

    tenants = slot_ref.shape[1]
    tenant = tenant_ref[...]
    named = tenant == lax.broadcasted_iota(i32, (tenants, rows), 0)
    slots = jnp.broadcast_to(slot_ref[...].astype(f32), (8, tenants)).astype(bf16)
    slot = jnp.dot(slots, named.astype(f32).astype(bf16), preferred_element_type=f32)[:1]
    dest = jnp.floor((slot + 0.5) * (1.0 / local_count))
    adapter = slot - dest * local_count + 1.0
    leap = jnp.bitwise_xor(dest.astype(i32), where_ref[0])
    padded = max(8, wide_size)
    goes = (leap == lax.broadcasted_iota(i32, (padded, rows), 0)).astype(f32)
    earlier = lax.broadcasted_iota(i32, (rows, rows), 0) < lax.broadcasted_iota(
        i32, (rows, rows), 1
    )
    before = jnp.dot(
        goes.astype(bf16), earlier.astype(f32).astype(bf16), preferred_element_type=f32
    )
    position = jnp.sum(goes * before, axis=0, keepdims=True).astype(i32)
    adapters = jnp.broadcast_to(adapter, (8, rows)).astype(bf16)
    place = jnp.full((1, rows), -1, i32)
    more = jnp.zeros((1, rows), f32)
    position = position - where_ref[2] * per_turn
    for k, end in enumerate(ends(layout, wide_size)):
        more = jnp.where((leap == k) & (position >= end), 1.0, more)
    offset, here = 0, []
    for k, start, count in layout:
        mine = position - start
        mine = jnp.where((leap == k) & (mine >= 0) & (mine < count - 1), mine, -1)
        place = jnp.where(mine >= 0, mine + offset, place)
        offset += count
        here.append(mine)
    any_more = jnp.max(more, axis=1, keepdims=True)

    for n in picked:
        count = layout[n][2]
        perm = (lax.broadcasted_iota(i32, (count, rows), 0) == here[n]).astype(f32).astype(bf16)
        filler = jnp.zeros((LANES - count, rows), bf16)
        ids = lax.dot_general(
            adapters,
            jnp.concatenate([perm, filler], axis=0),
            (((1,), (1,)), ((), ())),
            preferred_element_type=f32,
        )[:1]
        lane = lax.broadcasted_iota(i32, (1, LANES), 1)
        ids = jnp.where(lane == LANES - 1, any_more, ids)
        last = lax.broadcasted_iota(i32, (count, LANES), 0) == count - 1
        for c in range(chunks):
            cols = pl.ds(c * width, width)
            if n == picked[0]:
                load(c).wait()
            body = jnp.dot(perm, act_held[:, cols], preferred_element_type=f32)
            if c == 0:
                first = jnp.where(last, ids, body[:, :LANES])
                body = jnp.concatenate([first, body[:, LANES:]], axis=1)
            blocks[n][:, cols] = body.astype(bf16)
    place_ref[...] = jnp.broadcast_to(place.astype(f32), (LANES, rows)).T

def pack(where, tenant, slot, activations, local_count, wide_size, layout, span, per_turn):
    rows, features = activations.shape
    counts = [count for _, _, count in layout[slice(*span)]]
    chunks = 4
    anywhere = pl.BlockSpec(memory_space=pl.ANY)
    whole = pl.BlockSpec(memory_space=VMEM)
    scalar = pl.BlockSpec(memory_space=pltpu.SMEM)
    return pl.pallas_call(
        functools.partial(pack_kernel, local_count, wide_size, layout, span, per_turn),
        out_shape=[
            jax.ShapeDtypeStruct((1, 1), i32),
            jax.ShapeDtypeStruct((rows, LANES), f32),
        ]
        + [jax.ShapeDtypeStruct((c, features), bf16) for c in counts],
        in_specs=[scalar, whole, whole, anywhere],
        out_specs=[scalar, whole] + [whole for _ in counts],
        scratch_shapes=[VMEM((rows, features), bf16), pltpu.SemaphoreType.DMA((chunks,))],
        compiler_params=params(12),
        cost_estimate=cost(2 * sum(counts) * rows * features, 2 * features * (rows + sum(counts))),
        name="pack_rows",
    )(where, tenant, slot, activations)


def stage_kernel(down_ref, up_ref, down_out, up_out, sem):
    adapters, _, width = down_ref.shape
    copies = [
        pltpu.make_async_copy(
            down_ref.at[j], down_out.at[:, pl.ds(j * width, width)], sem.at[j]
        )
        for j in range(adapters)
    ]
    copies.append(pltpu.make_async_copy(up_ref, up_out, sem.at[adapters]))
    for copy in copies:
        copy.start()
    for copy in copies:
        copy.wait()


def stage(down_weight, up_weight):
    adapters, features, width = down_weight.shape
    whole = pl.BlockSpec(memory_space=VMEM)
    return pl.pallas_call(
        stage_kernel,
        out_shape=[
            pltpu.VMEM((features, adapters * width), down_weight.dtype),
            pltpu.VMEM(up_weight.shape, up_weight.dtype),
        ],
        in_specs=[pl.BlockSpec(memory_space=pl.ANY)] * 2,
        out_specs=[whole, whole],
        scratch_shapes=[pltpu.SemaphoreType.DMA((adapters + 1,))],
        compiler_params=params(12),
        cost_estimate=cost(10, 10),
        name="stage_maps",
    )(down_weight, up_weight)


def down_kernel(count, cols, narrow_size, per_step, where_ref, *refs):
    xs, weight_ref = refs[:count], refs[count]
    flag_ref, ids_ref = refs[count + 1 : count + 3]
    parts = refs[count + 3 : count + 3 + narrow_size]
    (held_ref,) = refs[count + 3 + narrow_size :]
    steps = weight_ref.shape[1] // (per_step * LANES)

    offsets = [sum(x.shape[0] for x in xs[:n]) for n in range(count)]

    flag = jnp.zeros((1, LANES), f32)
    for n in range(count):
        rows = xs[n].shape[0]
        held_ref[pl.ds(offsets[n], rows), :] = xs[n][...]
        last = held_ref[pl.ds(offsets[n] + rows - 16, 16), :LANES].astype(f32)[15:]
        flag = jnp.maximum(flag, last)
        turned = jnp.broadcast_to(last, (LANES, LANES)).T[:rows]
        keep = lax.broadcasted_iota(i32, (rows, LANES), 0) < rows - 1
        ids_ref[pl.ds(offsets[n], rows), :] = jnp.where(keep, turned, 0.0)
    lane = lax.broadcasted_iota(i32, (1, LANES), 1)
    flag_ref[0, 0] = jnp.max(jnp.where(lane == LANES - 1, flag, 0.0)).astype(i32)

    ids = ids_ref[...]
    total = jnp.zeros(ids.shape, f32)
    for c in range(steps):
        weights = weight_ref[:, c * per_step * LANES : (c + 1) * per_step * LANES]
        found = jnp.dot(held_ref[...], weights, preferred_element_type=f32)
        for j in range(per_step):
            name = c * per_step + j + 1.0
            total = jnp.where(ids == name, found[:, j * LANES : (j + 1) * LANES], total)

    half = total.shape[0] // 2
    rank = LANES // 2
    top, bottom = total[:half], total[half:]
    low = lax.broadcasted_iota(i32, (half, LANES), 1) < rank
    keys = jnp.where(low, top, pltpu.roll(bottom, rank, 1))
    values = jnp.where(low, pltpu.roll(top, rank, 1), bottom)
    for j in range(narrow_size):
        start = jnp.bitwise_xor(where_ref[1], j) * cols
        parts[j][...] = jnp.where(start >= KEY_VALUE_COLS, values, keys).astype(parts[j].dtype)


def down(where, blocks, weight, cols, narrow_size):
    features, width = weight.shape
    rows = sum(b.shape[0] for b in blocks)
    per_step = min(4, width // LANES)
    whole = pl.BlockSpec(memory_space=VMEM)
    scalar = pl.BlockSpec(memory_space=pltpu.SMEM)
    return pl.pallas_call(
        functools.partial(down_kernel, len(blocks), cols, narrow_size, per_step),
        out_shape=[
            jax.ShapeDtypeStruct((1, 1), i32),
            jax.ShapeDtypeStruct((rows, LANES), f32),
        ]
        + [jax.ShapeDtypeStruct((rows // 2, LANES), bf16 if j else f32) for j in range(narrow_size)],
        in_specs=[scalar] + [whole for _ in blocks] + [whole],
        out_specs=[scalar, whole] + [whole for _ in range(narrow_size)],
        scratch_shapes=[VMEM((rows, features), bf16)],
        compiler_params=params(18),
        cost_estimate=cost(2 * rows * features * width, 2 * features * (rows + width)),
        name="down_maps",
    )(where, *blocks, weight)


def up_kernel(narrow_size, ids_ref, *refs):
    parts, weight_ref, outs = refs[:narrow_size], refs[narrow_size], refs[narrow_size + 1 :]
    total = parts[0][...]
    for part in parts[1:]:
        total = total + part[...].astype(f32)
    low_rank = total.astype(bf16).astype(f32)
    rank = LANES // 2
    turned = pltpu.roll(low_rank, rank, 1)
    low = lax.broadcasted_iota(i32, low_rank.shape, 1) < rank
    twice = jnp.concatenate(
        [jnp.where(low, low_rank, turned), jnp.where(low, turned, low_rank)], axis=0
    )
    ids = ids_ref[...]
    second = (lax.broadcasted_iota(i32, ids.shape, 1) >= rank).astype(f32)
    adapters = weight_ref.shape[0] // rank
    left = [
        jnp.where(ids - second == 2.0 * pair + 1.0, twice, 0.0).astype(bf16)
        for pair in range(adapters // 2)
    ]
    found = jnp.dot(jnp.concatenate(left, axis=1), weight_ref[...], preferred_element_type=f32)
    offset = 0
    for out in outs:
        rows = out.shape[0]
        out[...] = found[offset : offset + rows].astype(bf16)
        offset += rows


def up(ids, parts, weight, counts):
    cols = weight.shape[1]
    return pl.pallas_call(
        functools.partial(up_kernel, len(parts)),
        out_shape=[jax.ShapeDtypeStruct((c, cols), bf16) for c in counts],
        compiler_params=params(10),
        cost_estimate=cost(2 * sum(counts) * weight.size, 2 * weight.size + 2 * sum(counts) * (cols + 512)),
        name="up_maps",
    )(ids, *parts, weight)


def base_kernel(count, where_ref, *refs):
    acts, weight_ref, so_far, out_ref = refs[:count], refs[count], refs[count + 1 : -1], refs[-1]
    step = pl.program_id(0)
    for j in range(count):

        @pl.when(step == j)
        def _(j=j):
            found = jnp.dot(acts[j][...], weight_ref[...], preferred_element_type=f32)
            if j:
                found = out_ref[...] + found
            elif so_far:
                found = so_far[0][...] + found
            out_ref[...] = found


def base(where, acts, first, weight, so_far):
    rows, features = acts[0].shape
    cols = weight.shape[1]
    count = len(acts)
    given = [] if so_far is None else [so_far]
    return pl.pallas_call(
        functools.partial(base_kernel, count),
        grid_spec=pltpu.PrefetchScalarGridSpec(
            num_scalar_prefetch=1,
            grid=(count,),
            in_specs=[pl.BlockSpec((rows, features), lambda i, where: (0, 0)) for _ in acts]
            + [
                pl.BlockSpec(
                    (features, cols),
                    lambda i, where: (jnp.bitwise_xor(where[1], first + i), 0),
                )
            ]
            + [pl.BlockSpec((rows, cols), lambda i, where: (0, 0)) for _ in given],
            out_specs=pl.BlockSpec((rows, cols), lambda i, where: (0, 0)),
        ),
        out_shape=jax.ShapeDtypeStruct((rows, cols), f32),
        compiler_params=params(14),
        cost_estimate=cost(2 * rows * features * count * cols, 2 * features * count * (cols + rows)),
        name="shared_projection",
    )(where, *acts, weight, *given)


def join_kernel(base_ref, place_ref, *refs):
    corrections, out_ref = refs[:-1], refs[-1]
    stacked = jnp.concatenate([c[...] for c in corrections], axis=0)
    rows, count = base_ref.shape[0], stacked.shape[0]
    place = place_ref[:, :1].astype(i32)
    perm = (lax.broadcasted_iota(i32, (rows, count), 1) == place).astype(f32).astype(bf16)
    found = jnp.dot(perm, stacked, preferred_element_type=f32)
    out_ref[...] = (base_ref[...] + found).astype(out_ref.dtype)


def join(base_out, place, corrections, dtype):
    rows, cols = base_out.shape
    count = sum(c.shape[0] for c in corrections)
    return pl.pallas_call(
        join_kernel,
        out_shape=jax.ShapeDtypeStruct((rows, cols), dtype),
        compiler_params=params(10),
        cost_estimate=cost(2 * rows * cols * count, 2 * cols * (count + 3 * rows)),
        name="join_corrections",
    )(base_out, place, *corrections)


def answers_for(where, blocks, staged, narrow_size):
    down_weight, up_weight = staged
    more, ids, *parts = down(where, blocks, down_weight, up_weight.shape[1], narrow_size)
    parts = [swap(p, "narrow", j) if j else p for j, p in enumerate(parts)]
    return up(ids, parts, up_weight, [b.shape[0] for b in blocks]), more


def later_turn(turn, axes, total, done, tenant, slot, activations, down_weight, up_weight):
    wide_size, narrow_size = lax.axis_size("wide"), lax.axis_size("narrow")
    where = jnp.stack([*axes, turn])
    layout = [(k, end, LATER_ROWS) for k, end in enumerate(done)]
    _, place, *sent = pack(
        where,
        tenant,
        slot,
        activations,
        down_weight.shape[0],
        wide_size,
        layout,
        (0, wide_size),
        LATER_ROWS - 1,
    )
    got = [swap(b, "wide", k) if k else b for k, b in enumerate(sent)]
    outs, more = answers_for(where, got, stage(down_weight, up_weight), narrow_size)
    answers = [swap(b, "wide", k) if k else b for k, b in enumerate(outs)]
    return join(total, place, answers, f32), more[0, 0]


def on_device(
    activations,
    request_tenants,
    adapter_slot,
    shared_weight,
    adapter_down_weight,
    adapter_up_weight,
):
    rows = activations.shape[0]
    wide_size, narrow_size = lax.axis_size("wide"), lax.axis_size("narrow")
    local_count = adapter_down_weight.shape[0]
    axes = (lax.axis_index("wide").astype(i32), lax.axis_index("narrow").astype(i32))
    where = jnp.stack([*axes, jnp.int32(0)])
    tenant = request_tenants.reshape(1, rows)
    slot = adapter_slot.reshape(1, -1)
    up_weight = adapter_up_weight.reshape(-1, adapter_up_weight.shape[-1])

    cols = up_weight.shape[1]
    first, second = first_turn(wide_size, local_count)
    layout = first + second
    routed = (local_count, wide_size, layout)
    begun, place, *sent = pack(
        where, tenant, slot, activations, *routed, (0, len(first)), 0
    )
    got = [swap(b, "wide", k) for (k, _, _), b in zip(first, sent)]
    half = narrow_size // 2
    across = [swap(after(activations, *sent), "narrow", half)] if half else []

    def step(work, *operands):
        def never(*operands):
            return jax.tree.map(
                lambda s: jnp.zeros(s.shape, s.dtype), jax.eval_shape(work, *operands)
            )

        return lax.cond(begun[0, 0] > 0, work, never, *operands)

    def spread(act):
        acts, bit = {0: act}, half // 2
        while bit:
            acts.update({j ^ bit: swap(x, "narrow", bit) for j, x in list(acts.items())})
            bit //= 2
        return [acts[j] for j in sorted(acts)]

    def work_before(tenant, slot, activations, shared_weight, maps):
        _, _, *sent = pack(
            where, tenant, slot, activations, *routed, (len(first), len(layout)), 0
        )
        return sent, base(where, spread(activations), 0, shared_weight, None), stage(*maps)

    def work_on_first(blocks, staged, maps, across):
        outs, more = answers_for(where, blocks, staged, narrow_size)
        return outs, more, stage(*maps), [x for act in across for x in spread(act)[1:]]

    def work_on_second(blocks, staged, acts, shared_weight, base_out):
        outs, more = [], jnp.zeros((1, 1), i32)
        if blocks:
            outs, more = answers_for(where, blocks, staged, narrow_size)
            acts = after_all(acts, *outs)
            outs = [swap(b, "wide", k) for (k, _, _), b in zip(second, outs)]
        if acts:
            base_out = base(where, acts, half, shared_weight, base_out)
        return outs, more, base_out

    shared_weight, maps = after_all((shared_weight, (adapter_down_weight, up_weight)), *sent)
    sent, base_out, staged = step(work_before, tenant, slot, activations, shared_weight, maps)
    late = [swap(b, "wide", k) for (k, _, _), b in zip(second, sent[:-1])]
    early = [after(b, base_out) for b in [*got, sent[-1]]]
    outs, more, staged, acts = step(work_on_first, early, staged, maps, across)
    late = after_all(late, *outs)
    outs = after_all(outs, *late)
    answers = [swap(b, "wide", k) for (k, _, _), b in zip(first, outs)]
    late_answers, late_more, base_out = step(
        work_on_second, late, staged, [*across, *acts], shared_weight, base_out
    )
    answers = [*answers, *late_answers, outs[-1]]
    more = jnp.maximum(more, late_more)
    more = more[0, 0]

    def done(base_out):
        return join(base_out, place, answers, bf16)

    def go_on(base_out):
        def turn_of(state):
            turn, _, total = state
            total, more = later_turn(
                turn, axes, total, ends(layout, wide_size), tenant, slot, activations, adapter_down_weight, up_weight
            )
            return turn + 1, more, total

        state = (jnp.int32(0), jnp.int32(1), join(base_out, place, answers, f32))
        return lax.while_loop(lambda s: s[1] > 0, turn_of, state)[2].astype(bf16)

    return lax.cond(more > 0, go_on, done, base_out)


def solution(mesh):
    in_specs = (
        P(("groups", "wide"), "narrow"),
        P(("groups", "wide"), None),
        P(),
        P(None, "narrow"),
        P("wide", "narrow", None),
        P("wide", None, "narrow"),
    )
    out_specs = P(("groups", "wide"), "narrow")
    return jax.shard_map(
        on_device, mesh=mesh, in_specs=in_specs, out_specs=out_specs, check_vma=False
    )
```

```python
import functools

import jax
import jax.numpy as jnp
from jax import lax
from jax.experimental import pallas as pl
from jax.experimental.pallas import tpu as pltpu
from jax.sharding import PartitionSpec as P

KEY_VALUE_COLS = 1024
LANES = 128
MOST = 16
NEAR = 2
NEAR_ROWS = 112
FAR_ROWS = 96
LATER_ROWS = 32
VMEM = pltpu.VMEM
MIB = 1 << 20

f32, bf16, i32 = jnp.float32, jnp.bfloat16, jnp.int32


def first_turn(wide_size, local_count):
    most = -(-(local_count * MOST + 1) // 32) * 32
    blocks = [(k, 0, min(NEAR_ROWS if k < NEAR else FAR_ROWS, most)) for k in range(wide_size)]
    half = wide_size // 2
    return blocks[1 : half + 1][::-1], blocks[half + 1 :] + blocks[:1]


def ends(blocks, wide_size):
    return [max(start + count - 1 for j, start, count in blocks if j == k) for k in range(wide_size)]


def swap(x, axis, k):
    size = lax.axis_size(axis)
    return lax.ppermute(x, axis, [(i, i ^ k) for i in range(size)])


def after(x, *others):
    return lax.optimization_barrier((x, *others))[0]


def after_all(xs, *others):
    return lax.optimization_barrier((xs, others))[0]


def cost(flops, bytes_accessed):
    return pl.CostEstimate(flops=flops // 1000, bytes_accessed=bytes_accessed // 1000, transcendentals=0)


def params(mib):
    return pltpu.CompilerParams(vmem_limit_bytes=mib * MIB)


def in_hbm(x):
    return pltpu.with_memory_space_constraint(x, pltpu.HBM)


def pack_kernel(
    local_count, wide_size, layout, span, per_turn, where_ref, tenant_ref, slot_ref, act_ref, *refs
):
    picked = range(*span)
    begun_ref, place_ref = refs[:2]
    blocks = dict(zip(picked, refs[2:-2]))
    act_held, in_sem = refs[-2:]
    rows, features = act_held.shape
    chunks = in_sem.shape[0]
    width = features // chunks

    def load(c):
        cols = pl.ds(c * width, width)
        return pltpu.make_async_copy(act_ref.at[:, cols], act_held.at[:, cols], in_sem.at[c])

    for c in range(chunks):
        load(c).start()
    begun_ref[0, 0] = jnp.int32(1)

    tenants = slot_ref.shape[1]
    tenant = tenant_ref[...]
    named = tenant == lax.broadcasted_iota(i32, (tenants, rows), 0)
    slots = jnp.broadcast_to(slot_ref[...].astype(f32), (8, tenants)).astype(bf16)
    slot = jnp.dot(slots, named.astype(f32).astype(bf16), preferred_element_type=f32)[:1]
    dest = jnp.floor((slot + 0.5) * (1.0 / local_count))
    adapter = slot - dest * local_count + 1.0
    leap = jnp.bitwise_xor(dest.astype(i32), where_ref[0])
    padded = max(8, wide_size)
    goes = (leap == lax.broadcasted_iota(i32, (padded, rows), 0)).astype(f32)
    earlier = lax.broadcasted_iota(i32, (rows, rows), 0) < lax.broadcasted_iota(
        i32, (rows, rows), 1
    )
    before = jnp.dot(
        goes.astype(bf16), earlier.astype(f32).astype(bf16), preferred_element_type=f32
    )
    position = jnp.sum(goes * before, axis=0, keepdims=True).astype(i32)
    adapters = jnp.broadcast_to(adapter, (8, rows)).astype(bf16)
    place = jnp.full((1, rows), -1, i32)
    more = jnp.zeros((1, rows), f32)
    position = position - where_ref[2] * per_turn
    for k, end in enumerate(ends(layout, wide_size)):
        more = jnp.where((leap == k) & (position >= end), 1.0, more)
    offset, here = 0, []
    for k, start, count in layout:
        mine = position - start
        mine = jnp.where((leap == k) & (mine >= 0) & (mine < count - 1), mine, -1)
        place = jnp.where(mine >= 0, mine + offset, place)
        offset += count
        here.append(mine)
    any_more = jnp.max(more, axis=1, keepdims=True)

    for n in picked:
        count = layout[n][2]
        perm = (lax.broadcasted_iota(i32, (count, rows), 0) == here[n]).astype(f32).astype(bf16)
        filler = jnp.zeros((LANES - count, rows), bf16)
        ids = lax.dot_general(
            adapters,
            jnp.concatenate([perm, filler], axis=0),
            (((1,), (1,)), ((), ())),
            preferred_element_type=f32,
        )[:1]
        lane = lax.broadcasted_iota(i32, (1, LANES), 1)
        ids = jnp.where(lane == LANES - 1, any_more, ids)
        last = lax.broadcasted_iota(i32, (count, LANES), 0) == count - 1
        for c in range(chunks):
            cols = pl.ds(c * width, width)
            if n == picked[0]:
                load(c).wait()
            body = jnp.dot(perm, act_held[:, cols], preferred_element_type=f32)
            if c == 0:
                first = jnp.where(last, ids, body[:, :LANES])
                body = jnp.concatenate([first, body[:, LANES:]], axis=1)
            blocks[n][:, cols] = body.astype(bf16)
    place_ref[...] = jnp.broadcast_to(place.astype(f32), (LANES, rows)).T

def pack(where, tenant, slot, activations, local_count, wide_size, layout, span, per_turn):
    rows, features = activations.shape
    counts = [count for _, _, count in layout[slice(*span)]]
    chunks = 4
    whole = pl.BlockSpec(memory_space=VMEM)
    scalar = pl.BlockSpec(memory_space=pltpu.SMEM)
    return pl.pallas_call(
        functools.partial(pack_kernel, local_count, wide_size, layout, span, per_turn),
        out_shape=[
            jax.ShapeDtypeStruct((1, 1), i32),
            jax.ShapeDtypeStruct((rows, LANES), f32),
        ]
        + [pltpu.VMEM((c, features), bf16) for c in counts],
        in_specs=[scalar, whole, whole, pl.BlockSpec(memory_space=pltpu.HBM)],
        out_specs=[scalar, whole] + [whole for _ in counts],
        scratch_shapes=[VMEM((rows, features), bf16), pltpu.SemaphoreType.DMA((chunks,))],
        compiler_params=params(12),
        cost_estimate=cost(2 * sum(counts) * rows * features, 2 * features * (rows + sum(counts))),
        name="pack_rows",
    )(where, tenant, slot, in_hbm(activations))


def stage_kernel(down_ref, up_ref, down_out, up_out, sem):
    adapters, _, width = down_ref.shape
    copies = [
        pltpu.make_async_copy(
            down_ref.at[j], down_out.at[:, pl.ds(j * width, width)], sem.at[j]
        )
        for j in range(adapters)
    ]
    copies.append(pltpu.make_async_copy(up_ref, up_out, sem.at[adapters]))
    for copy in copies:
        copy.start()
    for copy in copies:
        copy.wait()


def stage(down_weight, up_weight):
    adapters, features, width = down_weight.shape
    whole = pl.BlockSpec(memory_space=VMEM)
    return pl.pallas_call(
        stage_kernel,
        out_shape=[
            pltpu.VMEM((features, adapters * width), down_weight.dtype),
            pltpu.VMEM(up_weight.shape, up_weight.dtype),
        ],
        in_specs=[pl.BlockSpec(memory_space=pltpu.HBM)] * 2,
        out_specs=[whole, whole],
        scratch_shapes=[pltpu.SemaphoreType.DMA((adapters + 1,))],
        compiler_params=params(12),
        cost_estimate=cost(10, 10),
        name="stage_maps",
    )(in_hbm(down_weight), in_hbm(up_weight))


def down_kernel(count, cols, narrow_size, per_step, where_ref, *refs):
    xs, weight_ref = refs[:count], refs[count]
    flag_ref, ids_ref = refs[count + 1 : count + 3]
    parts = refs[count + 3 : count + 3 + narrow_size]
    held_ref, *own = refs[count + 3 + narrow_size :]
    loads = []
    if own:
        beside_ref, sem = own
        for j in range(weight_ref.shape[0]):
            cols_of = beside_ref.at[:, pl.ds(j * LANES, LANES)]
            loads.append(pltpu.make_async_copy(weight_ref.at[j], cols_of, sem.at[j]))
            loads[j].start()
        weight_ref = beside_ref
    steps = weight_ref.shape[1] // (per_step * LANES)

    offsets = [sum(x.shape[0] for x in xs[:n]) for n in range(count)]

    flag = jnp.zeros((1, LANES), f32)
    for n in range(count):
        rows = xs[n].shape[0]
        held_ref[pl.ds(offsets[n], rows), :] = xs[n][...]
        last = held_ref[pl.ds(offsets[n] + rows - 16, 16), :LANES].astype(f32)[15:]
        flag = jnp.maximum(flag, last)
        turned = jnp.broadcast_to(last, (LANES, LANES)).T[:rows]
        keep = lax.broadcasted_iota(i32, (rows, LANES), 0) < rows - 1
        ids_ref[pl.ds(offsets[n], rows), :] = jnp.where(keep, turned, 0.0)
    lane = lax.broadcasted_iota(i32, (1, LANES), 1)
    flag_ref[0, 0] = jnp.max(jnp.where(lane == LANES - 1, flag, 0.0)).astype(i32)

    ids = ids_ref[...]
    total = jnp.zeros(ids.shape, f32)
    for c in range(steps):
        for load in loads[c * per_step : (c + 1) * per_step]:
            load.wait()
        weights = weight_ref[:, c * per_step * LANES : (c + 1) * per_step * LANES]
        found = jnp.dot(held_ref[...], weights, preferred_element_type=f32)
        for j in range(per_step):
            name = c * per_step + j + 1.0
            total = jnp.where(ids == name, found[:, j * LANES : (j + 1) * LANES], total)

    half = total.shape[0] // 2
    rank = LANES // 2
    top, bottom = total[:half], total[half:]
    low = lax.broadcasted_iota(i32, (half, LANES), 1) < rank
    keys = jnp.where(low, top, pltpu.roll(bottom, rank, 1))
    values = jnp.where(low, pltpu.roll(top, rank, 1), bottom)
    for j in range(narrow_size):
        start = jnp.bitwise_xor(where_ref[1], j) * cols
        parts[j][...] = jnp.where(start >= KEY_VALUE_COLS, values, keys).astype(parts[j].dtype)


def down(where, blocks, weight, cols, narrow_size):
    features = weight.shape[-2]
    width = weight.size // features
    staged = weight.ndim == 2
    rows = sum(b.shape[0] for b in blocks)
    per_step = min(4, width // LANES)
    whole = pl.BlockSpec(memory_space=VMEM)
    scalar = pl.BlockSpec(memory_space=pltpu.SMEM)
    return pl.pallas_call(
        functools.partial(down_kernel, len(blocks), cols, narrow_size, per_step),
        out_shape=[
            jax.ShapeDtypeStruct((1, 1), i32),
            jax.ShapeDtypeStruct((rows, LANES), f32),
        ]
        + [jax.ShapeDtypeStruct((rows // 2, LANES), bf16 if j else f32) for j in range(narrow_size)],
        in_specs=[scalar]
        + [whole for _ in blocks]
        + [whole if staged else pl.BlockSpec(memory_space=pltpu.HBM)],
        out_specs=[scalar, whole] + [whole for _ in range(narrow_size)],
        scratch_shapes=[VMEM((rows, features), bf16)]
        + ([] if staged else [VMEM((features, width), bf16), pltpu.SemaphoreType.DMA((width // LANES,))]),
        compiler_params=params(18),
        cost_estimate=cost(2 * rows * features * width, 2 * features * (rows + width)),
        name="down_maps",
    )(where, *blocks, weight if staged else in_hbm(weight))


def up_kernel(narrow_size, ids_ref, *refs):
    parts, weight_ref, outs = refs[:narrow_size], refs[narrow_size], refs[narrow_size + 1 :]
    total = parts[0][...]
    for part in parts[1:]:
        total = total + part[...].astype(f32)
    low_rank = total.astype(bf16).astype(f32)
    rank = LANES // 2
    turned = pltpu.roll(low_rank, rank, 1)
    low = lax.broadcasted_iota(i32, low_rank.shape, 1) < rank
    twice = jnp.concatenate(
        [jnp.where(low, low_rank, turned), jnp.where(low, turned, low_rank)], axis=0
    )
    ids = ids_ref[...]
    second = (lax.broadcasted_iota(i32, ids.shape, 1) >= rank).astype(f32)
    adapters = weight_ref.shape[0] // rank
    left = [
        jnp.where(ids - second == 2.0 * pair + 1.0, twice, 0.0).astype(bf16)
        for pair in range(adapters // 2)
    ]
    found = jnp.dot(jnp.concatenate(left, axis=1), weight_ref[...], preferred_element_type=f32)
    offset = 0
    for out in outs:
        rows = out.shape[0]
        out[...] = found[offset : offset + rows].astype(bf16)
        offset += rows


def up(ids, parts, weight, counts):
    cols = weight.shape[1]
    return pl.pallas_call(
        functools.partial(up_kernel, len(parts)),
        out_shape=[jax.ShapeDtypeStruct((c, cols), bf16) for c in counts],
        compiler_params=params(10),
        cost_estimate=cost(2 * sum(counts) * weight.size, 2 * weight.size + 2 * sum(counts) * (cols + 512)),
        name="up_maps",
    )(ids, *parts, weight)


def base_kernel(act_ref, weight_ref, out_ref, act_held, weight_held, act_sem, weight_sem):
    parts = act_sem.shape[0]
    depth = act_held.shape[1] // parts

    def load(n):
        span = pl.ds(n * depth, depth)
        return (
            pltpu.make_async_copy(act_ref.at[:, span], act_held.at[:, span], act_sem.at[n]),
            pltpu.make_async_copy(weight_ref.at[span], weight_held.at[span], weight_sem.at[n]),
        )

    for n in range(parts):
        for copy in load(n):
            copy.start()
    total = None
    for n in range(parts):
        for copy in load(n):
            copy.wait()
        span = pl.ds(n * depth, depth)
        found = jnp.dot(act_held[:, span], weight_held[span, :], preferred_element_type=f32)
        total = found if total is None else total + found
    out_ref[...] = total


def base(acts, weight):
    rows, features = acts.shape
    cols = weight.shape[1]
    parts = 4
    return pl.pallas_call(
        base_kernel,
        out_shape=jax.ShapeDtypeStruct((rows, cols), f32),
        in_specs=[pl.BlockSpec(memory_space=pltpu.HBM)] * 2,
        out_specs=pl.BlockSpec(memory_space=VMEM),
        scratch_shapes=[
            VMEM(acts.shape, bf16),
            VMEM(weight.shape, bf16),
            pltpu.SemaphoreType.DMA((parts,)),
            pltpu.SemaphoreType.DMA((parts,)),
        ],
        compiler_params=params(18),
        cost_estimate=cost(2 * rows * features * cols, 2 * features * (cols + rows)),
        name="shared_projection",
    )(in_hbm(acts), in_hbm(weight))


def join_kernel(base_ref, place_ref, *refs):
    corrections, out_ref, held_ref, sem = refs[:-3], *refs[-3:]
    stacked = jnp.concatenate([c[...] for c in corrections], axis=0)
    rows, count = base_ref.shape[0], stacked.shape[0]
    parts = sem.shape[0]
    copies = []
    for n in range(parts):
        part = pl.ds(n * (rows // parts), rows // parts)
        place = place_ref[part, :1].astype(i32)
        perm = lax.broadcasted_iota(i32, (rows // parts, count), 1) == place
        found = jnp.dot(perm.astype(f32).astype(bf16), stacked, preferred_element_type=f32)
        held_ref[part, :] = (base_ref[part, :] + found).astype(out_ref.dtype)
        copy = pltpu.make_async_copy(held_ref.at[part, :], out_ref.at[part, :], sem.at[n])
        copy.start()
        copies.append(copy)
    for copy in copies:
        copy.wait()


def join(base_out, place, corrections, dtype):
    rows, cols = base_out.shape
    count = sum(c.shape[0] for c in corrections)
    parts = 2
    return pl.pallas_call(
        join_kernel,
        out_shape=pltpu.HBM((rows, cols), dtype),
        in_specs=[pl.BlockSpec(memory_space=VMEM)] * (2 + len(corrections)),
        out_specs=pl.BlockSpec(memory_space=pltpu.HBM),
        scratch_shapes=[VMEM((rows, cols), dtype), pltpu.SemaphoreType.DMA((parts,))],
        compiler_params=params(10),
        cost_estimate=cost(2 * rows * cols * count, 2 * cols * (count + 3 * rows)),
        name="join_corrections",
    )(base_out, place, *corrections)


def answers_for(where, blocks, staged, narrow_size):
    down_weight, up_weight = staged
    more, ids, *parts = down(where, blocks, down_weight, up_weight.shape[1], narrow_size)
    parts = [swap(p, "narrow", j) if j else p for j, p in enumerate(parts)]
    return up(ids, parts, up_weight, [b.shape[0] for b in blocks]), more


def later_turn(turn, axes, total, done, tenant, slot, activations, down_weight, up_weight):
    wide_size, narrow_size = lax.axis_size("wide"), lax.axis_size("narrow")
    where = jnp.stack([*axes, turn])
    layout = [(k, end, LATER_ROWS) for k, end in enumerate(done)]
    _, place, *sent = pack(
        where,
        tenant,
        slot,
        activations,
        down_weight.shape[0],
        wide_size,
        layout,
        (0, wide_size),
        LATER_ROWS - 1,
    )
    got = [swap(b, "wide", k) if k else b for k, b in enumerate(sent)]
    outs, more = answers_for(where, got, (down_weight, up_weight), narrow_size)
    answers = [swap(b, "wide", k) if k else b for k, b in enumerate(outs)]
    return join(total, place, answers, f32), more[0, 0]


def on_device(
    activations,
    request_tenants,
    adapter_slot,
    shared_weight,
    adapter_down_weight,
    adapter_up_weight,
):
    rows = activations.shape[0]
    wide_size, narrow_size = lax.axis_size("wide"), lax.axis_size("narrow")
    local_count = adapter_down_weight.shape[0]
    axes = (lax.axis_index("wide").astype(i32), lax.axis_index("narrow").astype(i32))
    where = jnp.stack([*axes, jnp.int32(0)])
    tenant = request_tenants.reshape(1, rows)
    slot = adapter_slot.reshape(1, -1)
    up_weight = adapter_up_weight.reshape(-1, adapter_up_weight.shape[-1])

    cols = up_weight.shape[1]
    first, second = first_turn(wide_size, local_count)
    layout = first + second
    routed = (local_count, wide_size, layout)
    begun, place, *sent = pack(
        where, tenant, slot, activations, *routed, (0, len(first)), 0
    )
    got = [swap(b, "wide", k) for (k, _, _), b in zip(first, sent)]
    def step(work, *operands):
        def never(*operands):
            return jax.tree.map(
                lambda s: jnp.zeros(s.shape, s.dtype), jax.eval_shape(work, *operands)
            )

        return lax.cond(begun[0, 0] > 0, work, never, *operands)

    def work_before(tenant, slot, activations):
        _, _, *sent = pack(
            where, tenant, slot, activations, *routed, (len(first), len(layout)), 0
        )
        return sent

    def work_on_first(blocks, maps):
        return answers_for(where, blocks, maps, narrow_size)

    def work_on_second(blocks, maps, acts, shared_weight):
        outs, more = [], jnp.zeros((1, 1), i32)
        if blocks:
            outs, more = answers_for(where, blocks, maps, narrow_size)
            acts = after(acts, *outs)
            outs = [swap(b, "wide", k) for (k, _, _), b in zip(second, outs)]
        return outs, more, base(acts, shared_weight)

    acts = lax.all_gather(after(activations, *sent), "narrow", axis=1, tiled=True)
    maps = after_all((adapter_down_weight, up_weight), *sent)
    sent = step(work_before, tenant, slot, activations)
    late = [swap(b, "wide", k) for (k, _, _), b in zip(second, sent[:-1])]
    staged = stage(*after_all(maps, sent))
    outs, more = step(work_on_first, [*got, sent[-1]], staged)
    late = after_all(late, *outs)
    outs = after_all(outs, *late)
    answers = [swap(b, "wide", k) for (k, _, _), b in zip(first, outs)]
    late_answers, late_more, base_out = step(work_on_second, late, maps, acts, shared_weight)
    answers = [*answers, *late_answers, outs[-1]]
    more = jnp.maximum(more, late_more)
    more = more[0, 0]

    def done(base_out):
        return join(base_out, place, answers, bf16)

    def go_on(base_out):
        def turn_of(state):
            turn, _, total = state
            total, more = later_turn(
                turn, axes, total, ends(layout, wide_size), tenant, slot, activations, adapter_down_weight, up_weight
            )
            return turn + 1, more, total

        state = (jnp.int32(0), jnp.int32(1), join(base_out, place, answers, f32))
        return lax.while_loop(lambda s: s[1] > 0, turn_of, state)[2].astype(bf16)

    return lax.cond(more > 0, go_on, done, base_out)


def solution(mesh):
    in_specs = (
        P(("groups", "wide"), "narrow"),
        P(("groups", "wide"), None),
        P(),
        P(None, "narrow"),
        P("wide", "narrow", None),
        P("wide", None, "narrow"),
    )
    out_specs = P(("groups", "wide"), "narrow")
    return jax.shard_map(
        on_device, mesh=mesh, in_specs=in_specs, out_specs=out_specs, check_vma=False
    )
```

```python
import functools

import jax
import jax.numpy as jnp
from jax import lax
from jax.experimental import pallas as pl
from jax.experimental.pallas import tpu as pltpu
from jax.sharding import PartitionSpec as P

KEY_VALUE_COLS = 1024
LANES = 128
MOST = 16
NEAR = 2
NEAR_ROWS = 112
FAR_ROWS = 96
LATER_ROWS = 32
VMEM = pltpu.VMEM
MIB = 1 << 20

f32, bf16, i32 = jnp.float32, jnp.bfloat16, jnp.int32


def first_turn(wide_size, local_count):
    most = -(-(local_count * MOST + 1) // 32) * 32
    blocks = [(k, 0, min(NEAR_ROWS if k < NEAR else FAR_ROWS, most)) for k in range(wide_size)]
    half = wide_size // 2
    return blocks[1 : half + 1][::-1], blocks[half + 1 :] + blocks[:1]


def ends(blocks, wide_size):
    return [max(start + count - 1 for j, start, count in blocks if j == k) for k in range(wide_size)]


def swap(x, axis, k):
    size = lax.axis_size(axis)
    return lax.ppermute(x, axis, [(i, i ^ k) for i in range(size)])


def after(x, *others):
    return lax.optimization_barrier((x, *others))[0]


def after_all(xs, *others):
    return lax.optimization_barrier((xs, others))[0]


def cost(flops, bytes_accessed, scale=0.001):
    return pl.CostEstimate(
        flops=int(flops * scale), bytes_accessed=int(bytes_accessed * scale), transcendentals=0
    )


def params(mib):
    return pltpu.CompilerParams(vmem_limit_bytes=mib * MIB)


def in_hbm(x):
    return pltpu.with_memory_space_constraint(x, pltpu.HBM)


def pack_kernel(
    local_count, wide_size, layout, span, per_turn, where_ref, tenant_ref, slot_ref, act_ref, *refs
):
    picked = range(*span)
    begun_ref, place_ref = refs[:2]
    blocks = dict(zip(picked, refs[2:-2]))
    act_held, in_sem = refs[-2:]
    rows, features = act_held.shape
    chunks = in_sem.shape[0]
    width = features // chunks

    def load(c):
        cols = pl.ds(c * width, width)
        return pltpu.make_async_copy(act_ref.at[:, cols], act_held.at[:, cols], in_sem.at[c])

    for c in range(chunks):
        load(c).start()
    begun_ref[0, 0] = jnp.int32(1)

    tenants = slot_ref.shape[1]
    tenant = tenant_ref[...]
    named = tenant == lax.broadcasted_iota(i32, (tenants, rows), 0)
    slots = jnp.broadcast_to(slot_ref[...].astype(f32), (8, tenants)).astype(bf16)
    slot = jnp.dot(slots, named.astype(f32).astype(bf16), preferred_element_type=f32)[:1]
    dest = jnp.floor((slot + 0.5) * (1.0 / local_count))
    adapter = slot - dest * local_count + 1.0
    leap = jnp.bitwise_xor(dest.astype(i32), where_ref[0])
    padded = max(8, wide_size)
    goes = (leap == lax.broadcasted_iota(i32, (padded, rows), 0)).astype(f32)
    earlier = lax.broadcasted_iota(i32, (rows, rows), 0) < lax.broadcasted_iota(
        i32, (rows, rows), 1
    )
    before = jnp.dot(
        goes.astype(bf16), earlier.astype(f32).astype(bf16), preferred_element_type=f32
    )
    position = jnp.sum(goes * before, axis=0, keepdims=True).astype(i32)
    adapters = jnp.broadcast_to(adapter, (8, rows)).astype(bf16)
    place = jnp.full((1, rows), -1, i32)
    more = jnp.zeros((1, rows), f32)
    position = position - where_ref[2] * per_turn
    for k, end in enumerate(ends(layout, wide_size)):
        more = jnp.where((leap == k) & (position >= end), 1.0, more)
    offset, here = 0, []
    for k, start, count in layout:
        mine = position - start
        mine = jnp.where((leap == k) & (mine >= 0) & (mine < count - 1), mine, -1)
        place = jnp.where(mine >= 0, mine + offset, place)
        offset += count
        here.append(mine)
    any_more = jnp.max(more, axis=1, keepdims=True)

    for n in picked:
        count = layout[n][2]
        perm = (lax.broadcasted_iota(i32, (count, rows), 0) == here[n]).astype(f32).astype(bf16)
        filler = jnp.zeros((LANES - count, rows), bf16)
        ids = lax.dot_general(
            adapters,
            jnp.concatenate([perm, filler], axis=0),
            (((1,), (1,)), ((), ())),
            preferred_element_type=f32,
        )[:1]
        lane = lax.broadcasted_iota(i32, (1, LANES), 1)
        ids = jnp.where(lane == LANES - 1, any_more, ids)
        last = lax.broadcasted_iota(i32, (count, LANES), 0) == count - 1
        for c in range(chunks):
            cols = pl.ds(c * width, width)
            if n == picked[0]:
                load(c).wait()
            body = jnp.dot(perm, act_held[:, cols], preferred_element_type=f32)
            if c == 0:
                first = jnp.where(last, ids, body[:, :LANES])
                body = jnp.concatenate([first, body[:, LANES:]], axis=1)
            blocks[n][:, cols] = body.astype(bf16)
    place_ref[...] = jnp.broadcast_to(place.astype(f32), (LANES, rows)).T

def pack(where, tenant, slot, activations, local_count, wide_size, layout, span, per_turn):
    rows, features = activations.shape
    counts = [count for _, _, count in layout[slice(*span)]]
    chunks = 4
    whole = pl.BlockSpec(memory_space=VMEM)
    scalar = pl.BlockSpec(memory_space=pltpu.SMEM)
    return pl.pallas_call(
        functools.partial(pack_kernel, local_count, wide_size, layout, span, per_turn),
        out_shape=[
            jax.ShapeDtypeStruct((1, 1), i32),
            jax.ShapeDtypeStruct((rows, LANES), f32),
        ]
        + [pltpu.VMEM((c, features), bf16) for c in counts],
        in_specs=[scalar, whole, whole, pl.BlockSpec(memory_space=pltpu.HBM)],
        out_specs=[scalar, whole] + [whole for _ in counts],
        scratch_shapes=[VMEM((rows, features), bf16), pltpu.SemaphoreType.DMA((chunks,))],
        compiler_params=params(12),
        cost_estimate=cost(2 * sum(counts) * rows * features, 2 * features * (rows + sum(counts))),
        name="pack_rows",
    )(where, tenant, slot, in_hbm(activations))


def stage_kernel(down_ref, up_ref, down_out, up_out, sem):
    adapters, _, width = down_ref.shape
    copies = [
        pltpu.make_async_copy(
            down_ref.at[j], down_out.at[:, pl.ds(j * width, width)], sem.at[j]
        )
        for j in range(adapters)
    ]
    copies.append(pltpu.make_async_copy(up_ref, up_out, sem.at[adapters]))
    for copy in copies:
        copy.start()
    for copy in copies:
        copy.wait()


def stage(down_weight, up_weight):
    adapters, features, width = down_weight.shape
    whole = pl.BlockSpec(memory_space=VMEM)
    return pl.pallas_call(
        stage_kernel,
        out_shape=[
            pltpu.VMEM((features, adapters * width), down_weight.dtype),
            pltpu.VMEM(up_weight.shape, up_weight.dtype),
        ],
        in_specs=[pl.BlockSpec(memory_space=pltpu.HBM)] * 2,
        out_specs=[whole, whole],
        scratch_shapes=[pltpu.SemaphoreType.DMA((adapters + 1,))],
        compiler_params=params(12),
        cost_estimate=cost(10, 10),
        name="stage_maps",
    )(in_hbm(down_weight), in_hbm(up_weight))


def down_kernel(count, cols, narrow_size, per_step, where_ref, *refs):
    xs, weight_ref = refs[:count], refs[count]
    flag_ref, ids_ref = refs[count + 1 : count + 3]
    parts = refs[count + 3 : count + 3 + narrow_size]
    (held_ref,) = refs[count + 3 + narrow_size :]
    steps = weight_ref.shape[1] // (per_step * LANES)

    offsets = [sum(x.shape[0] for x in xs[:n]) for n in range(count)]

    flag = jnp.zeros((1, LANES), f32)
    for n in range(count):
        rows = xs[n].shape[0]
        held_ref[pl.ds(offsets[n], rows), :] = xs[n][...]
        last = held_ref[pl.ds(offsets[n] + rows - 16, 16), :LANES].astype(f32)[15:]
        flag = jnp.maximum(flag, last)
        turned = jnp.broadcast_to(last, (LANES, LANES)).T[:rows]
        keep = lax.broadcasted_iota(i32, (rows, LANES), 0) < rows - 1
        ids_ref[pl.ds(offsets[n], rows), :] = jnp.where(keep, turned, 0.0)
    lane = lax.broadcasted_iota(i32, (1, LANES), 1)
    flag_ref[0, 0] = jnp.max(jnp.where(lane == LANES - 1, flag, 0.0)).astype(i32)

    ids = ids_ref[...]
    total = jnp.zeros(ids.shape, f32)
    for c in range(steps):
        weights = weight_ref[:, c * per_step * LANES : (c + 1) * per_step * LANES]
        found = jnp.dot(held_ref[...], weights, preferred_element_type=f32)
        for j in range(per_step):
            name = c * per_step + j + 1.0
            total = jnp.where(ids == name, found[:, j * LANES : (j + 1) * LANES], total)

    half = total.shape[0] // 2
    rank = LANES // 2
    top, bottom = total[:half], total[half:]
    low = lax.broadcasted_iota(i32, (half, LANES), 1) < rank
    keys = jnp.where(low, top, pltpu.roll(bottom, rank, 1))
    values = jnp.where(low, pltpu.roll(top, rank, 1), bottom)
    for j in range(narrow_size):
        start = jnp.bitwise_xor(where_ref[1], j) * cols
        parts[j][...] = jnp.where(start >= KEY_VALUE_COLS, values, keys).astype(parts[j].dtype)


def down(where, blocks, weight, cols, narrow_size, scale):
    features, width = weight.shape
    rows = sum(b.shape[0] for b in blocks)
    per_step = min(4, width // LANES)
    whole = pl.BlockSpec(memory_space=VMEM)
    scalar = pl.BlockSpec(memory_space=pltpu.SMEM)
    return pl.pallas_call(
        functools.partial(down_kernel, len(blocks), cols, narrow_size, per_step),
        out_shape=[
            jax.ShapeDtypeStruct((1, 1), i32),
            jax.ShapeDtypeStruct((rows, LANES), f32),
        ]
        + [jax.ShapeDtypeStruct((rows // 2, LANES), bf16 if j else f32) for j in range(narrow_size)],
        in_specs=[scalar] + [whole for _ in blocks] + [whole],
        out_specs=[scalar, whole] + [whole for _ in range(narrow_size)],
        scratch_shapes=[VMEM((rows, features), bf16)],
        compiler_params=params(18),
        cost_estimate=cost(2 * rows * features * width, 2 * features * (rows + width), scale),
        name="down_maps",
    )(where, *blocks, weight)


def up_kernel(narrow_size, ids_ref, *refs):
    parts, weight_ref, outs = refs[:narrow_size], refs[narrow_size], refs[narrow_size + 1 :]
    total = parts[0][...]
    for part in parts[1:]:
        total = total + part[...].astype(f32)
    low_rank = total.astype(bf16).astype(f32)
    rank = LANES // 2
    turned = pltpu.roll(low_rank, rank, 1)
    low = lax.broadcasted_iota(i32, low_rank.shape, 1) < rank
    twice = jnp.concatenate(
        [jnp.where(low, low_rank, turned), jnp.where(low, turned, low_rank)], axis=0
    )
    ids = ids_ref[...]
    second = (lax.broadcasted_iota(i32, ids.shape, 1) >= rank).astype(f32)
    adapters = weight_ref.shape[0] // rank
    left = [
        jnp.where(ids - second == 2.0 * pair + 1.0, twice, 0.0).astype(bf16)
        for pair in range(adapters // 2)
    ]
    found = jnp.dot(jnp.concatenate(left, axis=1), weight_ref[...], preferred_element_type=f32)
    offset = 0
    for out in outs:
        rows = out.shape[0]
        out[...] = found[offset : offset + rows].astype(bf16)
        offset += rows


def up(ids, parts, weight, counts):
    cols = weight.shape[1]
    return pl.pallas_call(
        functools.partial(up_kernel, len(parts)),
        out_shape=[jax.ShapeDtypeStruct((c, cols), bf16) for c in counts],
        compiler_params=params(10),
        cost_estimate=cost(2 * sum(counts) * weight.size, 2 * weight.size + 2 * sum(counts) * (cols + 512)),
        name="up_maps",
    )(ids, *parts, weight)


def base_kernel(count, where_ref, *refs):
    acts, weight_ref, so_far, out_ref = refs[:count], refs[count], refs[count + 1 : -1], refs[-1]
    step = pl.program_id(0)
    for j in range(count):

        @pl.when(step == j)
        def _(j=j):
            found = jnp.dot(acts[j][...], weight_ref[...], preferred_element_type=f32)
            if j:
                found = out_ref[...] + found
            elif so_far:
                found = so_far[0][...] + found
            out_ref[...] = found


def base(where, acts, first, weight, so_far):
    rows, features = acts[0].shape
    cols = weight.shape[1]
    count = len(acts)
    given = [] if so_far is None else [so_far]
    return pl.pallas_call(
        functools.partial(base_kernel, count),
        grid_spec=pltpu.PrefetchScalarGridSpec(
            num_scalar_prefetch=1,
            grid=(count,),
            in_specs=[pl.BlockSpec((rows, features), lambda i, where: (0, 0)) for _ in acts]
            + [
                pl.BlockSpec(
                    (features, cols),
                    lambda i, where: (jnp.bitwise_xor(where[1], first + i), 0),
                )
            ]
            + [pl.BlockSpec((rows, cols), lambda i, where: (0, 0)) for _ in given],
            out_specs=pl.BlockSpec((rows, cols), lambda i, where: (0, 0)),
        ),
        out_shape=jax.ShapeDtypeStruct((rows, cols), f32),
        compiler_params=params(14),
        cost_estimate=cost(2 * rows * features * count * cols, 2 * features * count * (cols + rows)),
        name="shared_projection",
    )(where, *acts, in_hbm(weight), *given)


def join_kernel(base_ref, place_ref, *refs):
    corrections, out_ref, held_ref, sem = refs[:-3], *refs[-3:]
    stacked = jnp.concatenate([c[...] for c in corrections], axis=0)
    rows, count = base_ref.shape[0], stacked.shape[0]
    parts = sem.shape[0]
    copies = []
    for n in range(parts):
        part = pl.ds(n * (rows // parts), rows // parts)
        place = place_ref[part, :1].astype(i32)
        perm = lax.broadcasted_iota(i32, (rows // parts, count), 1) == place
        found = jnp.dot(perm.astype(f32).astype(bf16), stacked, preferred_element_type=f32)
        held_ref[part, :] = (base_ref[part, :] + found).astype(out_ref.dtype)
        copy = pltpu.make_async_copy(held_ref.at[part, :], out_ref.at[part, :], sem.at[n])
        copy.start()
        copies.append(copy)
    for copy in copies:
        copy.wait()


def join(base_out, place, corrections, dtype):
    rows, cols = base_out.shape
    count = sum(c.shape[0] for c in corrections)
    parts = 2
    return pl.pallas_call(
        join_kernel,
        out_shape=pltpu.HBM((rows, cols), dtype),
        in_specs=[pl.BlockSpec(memory_space=VMEM)] * (2 + len(corrections)),
        out_specs=pl.BlockSpec(memory_space=pltpu.HBM),
        scratch_shapes=[VMEM((rows, cols), dtype), pltpu.SemaphoreType.DMA((parts,))],
        compiler_params=params(10),
        cost_estimate=cost(2 * rows * cols * count, 2 * cols * (count + 3 * rows)),
        name="join_corrections",
    )(base_out, place, *corrections)


def answers_for(where, blocks, staged, narrow_size, scale=0.001):
    down_weight, up_weight = staged
    more, ids, *parts = down(where, blocks, down_weight, up_weight.shape[1], narrow_size, scale)
    parts = [swap(p, "narrow", j) if j else p for j, p in enumerate(parts)]
    return up(ids, parts, up_weight, [b.shape[0] for b in blocks]), more


def later_turn(turn, axes, total, done, tenant, slot, activations, down_weight, up_weight):
    wide_size, narrow_size = lax.axis_size("wide"), lax.axis_size("narrow")
    where = jnp.stack([*axes, turn])
    layout = [(k, end, LATER_ROWS) for k, end in enumerate(done)]
    _, place, *sent = pack(
        where,
        tenant,
        slot,
        activations,
        down_weight.shape[0],
        wide_size,
        layout,
        (0, wide_size),
        LATER_ROWS - 1,
    )
    got = [swap(b, "wide", k) if k else b for k, b in enumerate(sent)]
    outs, more = answers_for(where, got, stage(down_weight, up_weight), narrow_size)
    answers = [swap(b, "wide", k) if k else b for k, b in enumerate(outs)]
    return join(total, place, answers, f32), more[0, 0]


def on_device(
    activations,
    request_tenants,
    adapter_slot,
    shared_weight,
    adapter_down_weight,
    adapter_up_weight,
):
    rows = activations.shape[0]
    wide_size, narrow_size = lax.axis_size("wide"), lax.axis_size("narrow")
    local_count = adapter_down_weight.shape[0]
    axes = (lax.axis_index("wide").astype(i32), lax.axis_index("narrow").astype(i32))
    where = jnp.stack([*axes, jnp.int32(0)])
    tenant = request_tenants.reshape(1, rows)
    slot = adapter_slot.reshape(1, -1)
    up_weight = adapter_up_weight.reshape(-1, adapter_up_weight.shape[-1])

    cols = up_weight.shape[1]
    first, second = first_turn(wide_size, local_count)
    layout = first + second
    routed = (local_count, wide_size, layout)
    begun, place, *sent = pack(
        where, tenant, slot, activations, *routed, (0, len(first)), 0
    )
    got = [swap(b, "wide", k) for (k, _, _), b in zip(first, sent)]
    half = narrow_size // 2

    def step(work, *operands):
        def never(*operands):
            return jax.tree.map(
                lambda s: jnp.zeros(s.shape, s.dtype), jax.eval_shape(work, *operands)
            )

        return lax.cond(begun[0, 0] > 0, work, never, *operands)

    def spread(act):
        acts, bit = {0: act}, half // 2
        while bit:
            acts.update({j ^ bit: swap(x, "narrow", bit) for j, x in list(acts.items())})
            bit //= 2
        return [acts[j] for j in sorted(acts)]

    def work_before(tenant, slot, activations, shared_weight, maps):
        _, _, *sent = pack(
            where, tenant, slot, activations, *routed, (len(first), len(layout)), 0
        )
        return sent, base(where, spread(activations), 0, shared_weight, None), stage(*maps)

    def work_on_first(blocks, staged, maps):
        outs, more = answers_for(where, blocks, staged, narrow_size)
        return outs, more, stage(*maps)

    def work_on_second(blocks, staged, acts, shared_weight, base_out):
        outs, more = [], jnp.zeros((1, 1), i32)
        if blocks:
            outs, more = answers_for(where, blocks, staged, narrow_size)
            acts = after_all(acts, *outs)
            outs = [swap(b, "wide", k) for (k, _, _), b in zip(second, outs)]
        acts = [x for act in acts for x in spread(act)]
        if acts:
            base_out = base(where, acts, half, shared_weight, base_out)
        return outs, more, base_out

    sent_first = sent
    shared_weight, maps = after_all((shared_weight, (adapter_down_weight, up_weight)), *sent)
    sent, base_out, staged = step(work_before, tenant, slot, activations, shared_weight, maps)
    late = [swap(b, "wide", k) for (k, _, _), b in zip(second, sent[:-1])]
    across = [swap(after(activations, *sent_first), "narrow", half)] if half else []
    outs, more, staged = step(work_on_first, [*got, sent[-1]], staged, maps)
    late = after_all(late, *outs)
    answers = [swap(b, "wide", k) for (k, _, _), b in zip(first, outs)]
    late_answers, late_more, base_out = step(
        work_on_second, late, staged, across, shared_weight, base_out
    )
    answers = [*answers, *late_answers, outs[-1]]
    more = jnp.maximum(more, late_more)
    more = more[0, 0]

    def done(base_out):
        return join(base_out, place, answers, bf16)

    def go_on(base_out):
        def turn_of(state):
            turn, _, total = state
            total, more = later_turn(
                turn, axes, total, ends(layout, wide_size), tenant, slot, activations, adapter_down_weight, up_weight
            )
            return turn + 1, more, total

        state = (jnp.int32(0), jnp.int32(1), join(base_out, place, answers, f32))
        return lax.while_loop(lambda s: s[1] > 0, turn_of, state)[2].astype(bf16)

    return lax.cond(more > 0, go_on, done, base_out)


def solution(mesh):
    in_specs = (
        P(("groups", "wide"), "narrow"),
        P(("groups", "wide"), None),
        P(),
        P(None, "narrow"),
        P("wide", "narrow", None),
        P("wide", None, "narrow"),
    )
    out_specs = P(("groups", "wide"), "narrow")
    return jax.shard_map(
        on_device, mesh=mesh, in_specs=in_specs, out_specs=out_specs, check_vma=False
    )
```

```python
import functools

import jax
import jax.numpy as jnp
from jax import lax
from jax.experimental import pallas as pl
from jax.experimental.pallas import tpu as pltpu
from jax.sharding import PartitionSpec as P

KEY_VALUE_COLS = 1024
LANES = 128
MOST = 16
NEAR = 2
NEAR_ROWS = 112
FAR_ROWS = 96
LATER_ROWS = 32
VMEM = pltpu.VMEM
MIB = 1 << 20

f32, bf16, i32 = jnp.float32, jnp.bfloat16, jnp.int32


def first_turn(wide_size, local_count):
    most = -(-(local_count * MOST + 1) // 32) * 32
    blocks = [(k, 0, min(NEAR_ROWS if k < NEAR else FAR_ROWS, most)) for k in range(wide_size)]
    half = wide_size // 2
    return blocks[1 : half + 1][::-1], blocks[half + 1 :] + blocks[:1]


def ends(blocks, wide_size):
    return [max(start + count - 1 for j, start, count in blocks if j == k) for k in range(wide_size)]


def swap(x, axis, k):
    size = lax.axis_size(axis)
    return lax.ppermute(x, axis, [(i, i ^ k) for i in range(size)])


def after(x, *others):
    return lax.optimization_barrier((x, *others))[0]


def after_all(xs, *others):
    return lax.optimization_barrier((xs, others))[0]


def cost(flops, bytes_accessed, scale=0.001):
    return pl.CostEstimate(
        flops=int(flops * scale), bytes_accessed=int(bytes_accessed * scale), transcendentals=0
    )


def params(mib):
    return pltpu.CompilerParams(vmem_limit_bytes=mib * MIB)


def in_hbm(x):
    return pltpu.with_memory_space_constraint(x, pltpu.HBM)


def pack_kernel(
    local_count, wide_size, layout, span, per_turn, where_ref, tenant_ref, slot_ref, act_ref, *refs
):
    picked = range(*span)
    begun_ref, place_ref = refs[:2]
    blocks = dict(zip(picked, refs[2:-2]))
    act_held, in_sem = refs[-2:]
    rows, features = act_held.shape
    chunks = in_sem.shape[0]
    width = features // chunks

    def load(c):
        cols = pl.ds(c * width, width)
        return pltpu.make_async_copy(act_ref.at[:, cols], act_held.at[:, cols], in_sem.at[c])

    for c in range(chunks):
        load(c).start()
    begun_ref[0, 0] = jnp.int32(1)

    tenants = slot_ref.shape[1]
    tenant = tenant_ref[...]
    named = tenant == lax.broadcasted_iota(i32, (tenants, rows), 0)
    slots = jnp.broadcast_to(slot_ref[...].astype(f32), (8, tenants)).astype(bf16)
    slot = jnp.dot(slots, named.astype(f32).astype(bf16), preferred_element_type=f32)[:1]
    dest = jnp.floor((slot + 0.5) * (1.0 / local_count))
    adapter = slot - dest * local_count + 1.0
    leap = jnp.bitwise_xor(dest.astype(i32), where_ref[0])
    padded = max(8, wide_size)
    goes = (leap == lax.broadcasted_iota(i32, (padded, rows), 0)).astype(f32)
    earlier = lax.broadcasted_iota(i32, (rows, rows), 0) < lax.broadcasted_iota(
        i32, (rows, rows), 1
    )
    before = jnp.dot(
        goes.astype(bf16), earlier.astype(f32).astype(bf16), preferred_element_type=f32
    )
    position = jnp.sum(goes * before, axis=0, keepdims=True).astype(i32)
    adapters = jnp.broadcast_to(adapter, (8, rows)).astype(bf16)
    place = jnp.full((1, rows), -1, i32)
    more = jnp.zeros((1, rows), f32)
    position = position - where_ref[2] * per_turn
    for k, end in enumerate(ends(layout, wide_size)):
        more = jnp.where((leap == k) & (position >= end), 1.0, more)
    offset, here = 0, []
    for k, start, count in layout:
        mine = position - start
        mine = jnp.where((leap == k) & (mine >= 0) & (mine < count - 1), mine, -1)
        place = jnp.where(mine >= 0, mine + offset, place)
        offset += count
        here.append(mine)
    any_more = jnp.max(more, axis=1, keepdims=True)

    for n in picked:
        count = layout[n][2]
        perm = (lax.broadcasted_iota(i32, (count, rows), 0) == here[n]).astype(f32).astype(bf16)
        filler = jnp.zeros((LANES - count, rows), bf16)
        ids = lax.dot_general(
            adapters,
            jnp.concatenate([perm, filler], axis=0),
            (((1,), (1,)), ((), ())),
            preferred_element_type=f32,
        )[:1]
        lane = lax.broadcasted_iota(i32, (1, LANES), 1)
        ids = jnp.where(lane == LANES - 1, any_more, ids)
        last = lax.broadcasted_iota(i32, (count, LANES), 0) == count - 1
        for c in range(chunks):
            cols = pl.ds(c * width, width)
            if n == picked[0]:
                load(c).wait()
            body = jnp.dot(perm, act_held[:, cols], preferred_element_type=f32)
            if c == 0:
                first = jnp.where(last, ids, body[:, :LANES])
                body = jnp.concatenate([first, body[:, LANES:]], axis=1)
            blocks[n][:, cols] = body.astype(bf16)
    place_ref[...] = jnp.broadcast_to(place.astype(f32), (LANES, rows)).T

def pack(where, tenant, slot, activations, local_count, wide_size, layout, span, per_turn):
    rows, features = activations.shape
    counts = [count for _, _, count in layout[slice(*span)]]
    chunks = 4
    whole = pl.BlockSpec(memory_space=VMEM)
    scalar = pl.BlockSpec(memory_space=pltpu.SMEM)
    return pl.pallas_call(
        functools.partial(pack_kernel, local_count, wide_size, layout, span, per_turn),
        out_shape=[
            jax.ShapeDtypeStruct((1, 1), i32),
            jax.ShapeDtypeStruct((rows, LANES), f32),
        ]
        + [pltpu.VMEM((c, features), bf16) for c in counts],
        in_specs=[scalar, whole, whole, pl.BlockSpec(memory_space=pltpu.HBM)],
        out_specs=[scalar, whole] + [whole for _ in counts],
        scratch_shapes=[VMEM((rows, features), bf16), pltpu.SemaphoreType.DMA((chunks,))],
        compiler_params=params(12),
        cost_estimate=cost(2 * sum(counts) * rows * features, 2 * features * (rows + sum(counts))),
        name="pack_rows",
    )(where, tenant, slot, in_hbm(activations))


def stage_kernel(down_ref, up_ref, down_out, up_out, sem):
    adapters, _, width = down_ref.shape
    copies = [
        pltpu.make_async_copy(
            down_ref.at[j], down_out.at[:, pl.ds(j * width, width)], sem.at[j]
        )
        for j in range(adapters)
    ]
    copies.append(pltpu.make_async_copy(up_ref, up_out, sem.at[adapters]))
    for copy in copies:
        copy.start()
    for copy in copies:
        copy.wait()


def stage(down_weight, up_weight):
    adapters, features, width = down_weight.shape
    whole = pl.BlockSpec(memory_space=VMEM)
    return pl.pallas_call(
        stage_kernel,
        out_shape=[
            pltpu.VMEM((features, adapters * width), down_weight.dtype),
            pltpu.VMEM(up_weight.shape, up_weight.dtype),
        ],
        in_specs=[pl.BlockSpec(memory_space=pltpu.HBM)] * 2,
        out_specs=[whole, whole],
        scratch_shapes=[pltpu.SemaphoreType.DMA((adapters + 1,))],
        compiler_params=params(12),
        cost_estimate=cost(10, 10),
        name="stage_maps",
    )(in_hbm(down_weight), in_hbm(up_weight))


def down_kernel(count, cols, narrow_size, per_step, where_ref, *refs):
    xs, weight_ref = refs[:count], refs[count]
    flag_ref, ids_ref = refs[count + 1 : count + 3]
    parts = refs[count + 3 : count + 3 + narrow_size]
    (held_ref,) = refs[count + 3 + narrow_size :]
    steps = weight_ref.shape[1] // (per_step * LANES)

    offsets = [sum(x.shape[0] for x in xs[:n]) for n in range(count)]

    flag = jnp.zeros((1, LANES), f32)
    for n in range(count):
        rows = xs[n].shape[0]
        held_ref[pl.ds(offsets[n], rows), :] = xs[n][...]
        last = held_ref[pl.ds(offsets[n] + rows - 16, 16), :LANES].astype(f32)[15:]
        flag = jnp.maximum(flag, last)
        turned = jnp.broadcast_to(last, (LANES, LANES)).T[:rows]
        keep = lax.broadcasted_iota(i32, (rows, LANES), 0) < rows - 1
        ids_ref[pl.ds(offsets[n], rows), :] = jnp.where(keep, turned, 0.0)
    lane = lax.broadcasted_iota(i32, (1, LANES), 1)
    flag_ref[0, 0] = jnp.max(jnp.where(lane == LANES - 1, flag, 0.0)).astype(i32)

    ids = ids_ref[...]
    total = jnp.zeros(ids.shape, f32)
    for c in range(steps):
        weights = weight_ref[:, c * per_step * LANES : (c + 1) * per_step * LANES]
        found = jnp.dot(held_ref[...], weights, preferred_element_type=f32)
        for j in range(per_step):
            name = c * per_step + j + 1.0
            total = jnp.where(ids == name, found[:, j * LANES : (j + 1) * LANES], total)

    half = total.shape[0] // 2
    rank = LANES // 2
    top, bottom = total[:half], total[half:]
    low = lax.broadcasted_iota(i32, (half, LANES), 1) < rank
    keys = jnp.where(low, top, pltpu.roll(bottom, rank, 1))
    values = jnp.where(low, pltpu.roll(top, rank, 1), bottom)
    for j in range(narrow_size):
        start = jnp.bitwise_xor(where_ref[1], j) * cols
        parts[j][...] = jnp.where(start >= KEY_VALUE_COLS, values, keys).astype(parts[j].dtype)


def down(where, blocks, weight, cols, narrow_size, scale):
    features, width = weight.shape
    rows = sum(b.shape[0] for b in blocks)
    per_step = min(4, width // LANES)
    whole = pl.BlockSpec(memory_space=VMEM)
    scalar = pl.BlockSpec(memory_space=pltpu.SMEM)
    return pl.pallas_call(
        functools.partial(down_kernel, len(blocks), cols, narrow_size, per_step),
        out_shape=[
            jax.ShapeDtypeStruct((1, 1), i32),
            jax.ShapeDtypeStruct((rows, LANES), f32),
        ]
        + [jax.ShapeDtypeStruct((rows // 2, LANES), bf16 if j else f32) for j in range(narrow_size)],
        in_specs=[scalar] + [whole for _ in blocks] + [whole],
        out_specs=[scalar, whole] + [whole for _ in range(narrow_size)],
        scratch_shapes=[VMEM((rows, features), bf16)],
        compiler_params=params(18),
        cost_estimate=cost(2 * rows * features * width, 2 * features * (rows + width), scale),
        name="down_maps",
    )(where, *blocks, weight)


def up_kernel(narrow_size, ids_ref, *refs):
    parts, weight_ref, outs = refs[:narrow_size], refs[narrow_size], refs[narrow_size + 1 :]
    total = parts[0][...]
    for part in parts[1:]:
        total = total + part[...].astype(f32)
    low_rank = total.astype(bf16).astype(f32)
    rank = LANES // 2
    turned = pltpu.roll(low_rank, rank, 1)
    low = lax.broadcasted_iota(i32, low_rank.shape, 1) < rank
    twice = jnp.concatenate(
        [jnp.where(low, low_rank, turned), jnp.where(low, turned, low_rank)], axis=0
    )
    ids = ids_ref[...]
    second = (lax.broadcasted_iota(i32, ids.shape, 1) >= rank).astype(f32)
    adapters = weight_ref.shape[0] // rank
    left = [
        jnp.where(ids - second == 2.0 * pair + 1.0, twice, 0.0).astype(bf16)
        for pair in range(adapters // 2)
    ]
    found = jnp.dot(jnp.concatenate(left, axis=1), weight_ref[...], preferred_element_type=f32)
    offset = 0
    for out in outs:
        rows = out.shape[0]
        out[...] = found[offset : offset + rows].astype(bf16)
        offset += rows


def up(ids, parts, weight, counts):
    cols = weight.shape[1]
    return pl.pallas_call(
        functools.partial(up_kernel, len(parts)),
        out_shape=[jax.ShapeDtypeStruct((c, cols), bf16) for c in counts],
        compiler_params=params(10),
        cost_estimate=cost(2 * sum(counts) * weight.size, 2 * weight.size + 2 * sum(counts) * (cols + 512)),
        name="up_maps",
    )(ids, *parts, weight)


def base_kernel(count, where_ref, *refs):
    acts, weight_ref, so_far, out_ref = refs[:count], refs[count], refs[count + 1 : -1], refs[-1]
    step = pl.program_id(0)
    for j in range(count):

        @pl.when(step == j)
        def _(j=j):
            found = jnp.dot(acts[j][...], weight_ref[...], preferred_element_type=f32)
            if j:
                found = out_ref[...] + found
            elif so_far:
                found = so_far[0][...] + found
            out_ref[...] = found


def base(where, acts, first, weight, so_far):
    rows, features = acts[0].shape
    cols = weight.shape[1]
    count = len(acts)
    given = [] if so_far is None else [so_far]
    return pl.pallas_call(
        functools.partial(base_kernel, count),
        grid_spec=pltpu.PrefetchScalarGridSpec(
            num_scalar_prefetch=1,
            grid=(count,),
            in_specs=[pl.BlockSpec((rows, features), lambda i, where: (0, 0)) for _ in acts]
            + [
                pl.BlockSpec(
                    (features, cols),
                    lambda i, where: (jnp.bitwise_xor(where[1], first + i), 0),
                )
            ]
            + [pl.BlockSpec((rows, cols), lambda i, where: (0, 0)) for _ in given],
            out_specs=pl.BlockSpec((rows, cols), lambda i, where: (0, 0)),
        ),
        out_shape=jax.ShapeDtypeStruct((rows, cols), f32),
        compiler_params=params(14),
        cost_estimate=cost(2 * rows * features * count * cols, 2 * features * count * (cols + rows)),
        name="shared_projection",
    )(where, *acts, in_hbm(weight), *given)


def join_kernel(base_ref, place_ref, *refs):
    corrections, out_ref, held_ref, sem = refs[:-3], *refs[-3:]
    stacked = jnp.concatenate([c[...] for c in corrections], axis=0)
    rows, count = base_ref.shape[0], stacked.shape[0]
    parts = sem.shape[0]
    copies = []
    for n in range(parts):
        part = pl.ds(n * (rows // parts), rows // parts)
        place = place_ref[part, :1].astype(i32)
        perm = lax.broadcasted_iota(i32, (rows // parts, count), 1) == place
        found = jnp.dot(perm.astype(f32).astype(bf16), stacked, preferred_element_type=f32)
        held_ref[part, :] = (base_ref[part, :] + found).astype(out_ref.dtype)
        copy = pltpu.make_async_copy(held_ref.at[part, :], out_ref.at[part, :], sem.at[n])
        copy.start()
        copies.append(copy)
    for copy in copies:
        copy.wait()


def join(base_out, place, corrections, dtype):
    rows, cols = base_out.shape
    count = sum(c.shape[0] for c in corrections)
    parts = 2
    return pl.pallas_call(
        join_kernel,
        out_shape=pltpu.HBM((rows, cols), dtype),
        in_specs=[pl.BlockSpec(memory_space=VMEM)] * (2 + len(corrections)),
        out_specs=pl.BlockSpec(memory_space=pltpu.HBM),
        scratch_shapes=[VMEM((rows, cols), dtype), pltpu.SemaphoreType.DMA((parts,))],
        compiler_params=params(10),
        cost_estimate=cost(2 * rows * cols * count, 2 * cols * (count + 3 * rows)),
        name="join_corrections",
    )(base_out, place, *corrections)


def raise_parts(ids, parts, up_weight, counts):
    parts = [swap(p, "narrow", j) if j else p for j, p in enumerate(parts)]
    return up(ids, parts, up_weight, counts)


def answers_for(where, blocks, maps, narrow_size):
    down_weight, up_weight = maps
    more, ids, *parts = down(where, blocks, down_weight, up_weight.shape[1], narrow_size, 0.001)
    return raise_parts(ids, parts, up_weight, [b.shape[0] for b in blocks]), more


def later_turn(turn, axes, total, done, tenant, slot, activations, down_weight, up_weight):
    wide_size, narrow_size = lax.axis_size("wide"), lax.axis_size("narrow")
    where = jnp.stack([*axes, turn])
    layout = [(k, end, LATER_ROWS) for k, end in enumerate(done)]
    _, place, *sent = pack(
        where,
        tenant,
        slot,
        activations,
        down_weight.shape[0],
        wide_size,
        layout,
        (0, wide_size),
        LATER_ROWS - 1,
    )
    got = [swap(b, "wide", k) if k else b for k, b in enumerate(sent)]
    outs, more = answers_for(where, got, stage(down_weight, up_weight), narrow_size)
    answers = [swap(b, "wide", k) if k else b for k, b in enumerate(outs)]
    return join(total, place, answers, f32), more[0, 0]


def on_device(
    activations,
    request_tenants,
    adapter_slot,
    shared_weight,
    adapter_down_weight,
    adapter_up_weight,
):
    rows = activations.shape[0]
    wide_size, narrow_size = lax.axis_size("wide"), lax.axis_size("narrow")
    local_count = adapter_down_weight.shape[0]
    axes = (lax.axis_index("wide").astype(i32), lax.axis_index("narrow").astype(i32))
    where = jnp.stack([*axes, jnp.int32(0)])
    tenant = request_tenants.reshape(1, rows)
    slot = adapter_slot.reshape(1, -1)
    up_weight = adapter_up_weight.reshape(-1, adapter_up_weight.shape[-1])

    cols = up_weight.shape[1]
    first, second = first_turn(wide_size, local_count)
    layout = first + second
    routed = (local_count, wide_size, layout)
    begun, place, *sent = pack(
        where, tenant, slot, activations, *routed, (0, len(first)), 0
    )
    got = [swap(b, "wide", k) for (k, _, _), b in zip(first, sent)]
    half = narrow_size // 2

    def step(work, *operands):
        def never(*operands):
            return jax.tree.map(
                lambda s: jnp.zeros(s.shape, s.dtype), jax.eval_shape(work, *operands)
            )

        return lax.cond(begun[0, 0] > 0, work, never, *operands)

    def spread(act):
        acts, bit = {0: act}, half // 2
        while bit:
            acts.update({j ^ bit: swap(x, "narrow", bit) for j, x in list(acts.items())})
            bit //= 2
        return [acts[j] for j in sorted(acts)]

    def work_before(tenant, slot, activations, shared_weight, maps):
        _, _, *sent = pack(
            where, tenant, slot, activations, *routed, (len(first), len(layout)), 0
        )
        return sent, base(where, spread(activations), 0, shared_weight, None), stage(*maps)

    def work_on_first(ids, parts, up_weight, maps):
        counts = [count for _, _, count in [*first, layout[-1]]]
        return raise_parts(ids, parts, up_weight, counts), stage(*maps)

    def work_on_second(blocks, maps):
        return answers_for(where, blocks, maps, narrow_size)

    def work_after(across, shared_weight, base_out):
        return base(where, spread(across), half, shared_weight, base_out)

    shared_weight, maps = after_all((shared_weight, (adapter_down_weight, up_weight)), *sent)
    sent, base_out, staged = step(work_before, tenant, slot, activations, shared_weight, maps)
    across = swap(after(activations, base_out), "narrow", half) if half else None
    late = [swap(b, "wide", k) for (k, _, _), b in zip(second, sent[:-1])]
    more, ids, *parts = down(
        where, [*got, sent[-1]], staged[0], up_weight.shape[1], narrow_size, 20
    )
    outs, staged = step(work_on_first, ids, parts, staged[1], maps)
    if late:
        late_outs, late_more = step(work_on_second, after_all(late, *outs), staged)
        more = jnp.maximum(more, late_more)
        outs = after_all(outs, *late_outs)
        outs = [*outs[:-1], *late_outs, outs[-1]]
    answers = [swap(b, "wide", k) if k else b for (k, _, _), b in zip(layout, outs)]
    if half:
        base_out = step(work_after, *after_all((across, shared_weight, base_out), *outs))
    more = more[0, 0]

    def done(base_out):
        return join(base_out, place, answers, bf16)

    def go_on(base_out):
        def turn_of(state):
            turn, _, total = state
            total, more = later_turn(
                turn, axes, total, ends(layout, wide_size), tenant, slot, activations, adapter_down_weight, up_weight
            )
            return turn + 1, more, total

        state = (jnp.int32(0), jnp.int32(1), join(base_out, place, answers, f32))
        return lax.while_loop(lambda s: s[1] > 0, turn_of, state)[2].astype(bf16)

    return lax.cond(more > 0, go_on, done, base_out)


def solution(mesh):
    in_specs = (
        P(("groups", "wide"), "narrow"),
        P(("groups", "wide"), None),
        P(),
        P(None, "narrow"),
        P("wide", "narrow", None),
        P("wide", None, "narrow"),
    )
    out_specs = P(("groups", "wide"), "narrow")
    return jax.shard_map(
        on_device, mesh=mesh, in_specs=in_specs, out_specs=out_specs, check_vma=False
    )
```

```python
import functools

import jax
import jax.numpy as jnp
from jax import lax
from jax.experimental import pallas as pl
from jax.experimental.pallas import tpu as pltpu
from jax.sharding import PartitionSpec as P

KEY_VALUE_COLS = 1024
LANES = 128
MOST = 16
OWN_ROWS = 112
AWAY_ROWS = 96
LATER_ROWS = 32
VMEM = pltpu.VMEM
MIB = 1 << 20

f32, bf16, i32 = jnp.float32, jnp.bfloat16, jnp.int32


def first_turn(wide_size, local_count):
    most = -(-(local_count * MOST + 1) // 32) * 32
    return [(k, 0, min(AWAY_ROWS if k else OWN_ROWS, most)) for k in reversed(range(wide_size))]


def ends(blocks, wide_size):
    return [max(start + count - 1 for j, start, count in blocks if j == k) for k in range(wide_size)]


def swap(x, axis, k):
    size = lax.axis_size(axis)
    return lax.ppermute(x, axis, [(i, i ^ k) for i in range(size)])


def after(x, *others):
    return lax.optimization_barrier((x, *others))[0]


def after_all(xs, *others):
    return lax.optimization_barrier((xs, others))[0]


def cost(flops, bytes_accessed, scale=0.001):
    return pl.CostEstimate(
        flops=int(flops * scale), bytes_accessed=int(bytes_accessed * scale), transcendentals=0
    )


def params(mib):
    return pltpu.CompilerParams(vmem_limit_bytes=mib * MIB)


def in_hbm(x):
    return pltpu.with_memory_space_constraint(x, pltpu.HBM)


def pack_kernel(
    local_count, wide_size, layout, span, per_turn, where_ref, tenant_ref, slot_ref, act_ref, *refs
):
    picked = range(*span)
    begun_ref, place_ref = refs[:2]
    blocks = dict(zip(picked, refs[2:-2]))
    act_held, in_sem = refs[-2:]
    rows, features = act_held.shape
    chunks = in_sem.shape[0]
    width = features // chunks

    def load(c):
        cols = pl.ds(c * width, width)
        return pltpu.make_async_copy(act_ref.at[:, cols], act_held.at[:, cols], in_sem.at[c])

    for c in range(chunks):
        load(c).start()
    begun_ref[0, 0] = jnp.int32(1)

    tenants = slot_ref.shape[1]
    tenant = tenant_ref[...]
    named = tenant == lax.broadcasted_iota(i32, (tenants, rows), 0)
    slots = jnp.broadcast_to(slot_ref[...].astype(f32), (8, tenants)).astype(bf16)
    slot = jnp.dot(slots, named.astype(f32).astype(bf16), preferred_element_type=f32)[:1]
    dest = jnp.floor((slot + 0.5) * (1.0 / local_count))
    adapter = slot - dest * local_count + 1.0
    leap = jnp.bitwise_xor(dest.astype(i32), where_ref[0])
    padded = max(8, wide_size)
    goes = (leap == lax.broadcasted_iota(i32, (padded, rows), 0)).astype(f32)
    earlier = lax.broadcasted_iota(i32, (rows, rows), 0) < lax.broadcasted_iota(
        i32, (rows, rows), 1
    )
    before = jnp.dot(
        goes.astype(bf16), earlier.astype(f32).astype(bf16), preferred_element_type=f32
    )
    position = jnp.sum(goes * before, axis=0, keepdims=True).astype(i32)
    adapters = jnp.broadcast_to(adapter, (8, rows)).astype(bf16)
    place = jnp.full((1, rows), -1, i32)
    more = jnp.zeros((1, rows), f32)
    position = position - where_ref[2] * per_turn
    for k, end in enumerate(ends(layout, wide_size)):
        more = jnp.where((leap == k) & (position >= end), 1.0, more)
    offset, here = 0, []
    for k, start, count in layout:
        mine = position - start
        mine = jnp.where((leap == k) & (mine >= 0) & (mine < count - 1), mine, -1)
        place = jnp.where(mine >= 0, mine + offset, place)
        offset += count
        here.append(mine)
    any_more = jnp.max(more, axis=1, keepdims=True)

    for n in picked:
        count = layout[n][2]
        perm = (lax.broadcasted_iota(i32, (count, rows), 0) == here[n]).astype(f32).astype(bf16)
        filler = jnp.zeros((LANES - count, rows), bf16)
        ids = lax.dot_general(
            adapters,
            jnp.concatenate([perm, filler], axis=0),
            (((1,), (1,)), ((), ())),
            preferred_element_type=f32,
        )[:1]
        lane = lax.broadcasted_iota(i32, (1, LANES), 1)
        ids = jnp.where(lane == LANES - 1, any_more, ids)
        last = lax.broadcasted_iota(i32, (count, LANES), 0) == count - 1
        for c in range(chunks):
            cols = pl.ds(c * width, width)
            if n == picked[0]:
                load(c).wait()
            body = jnp.dot(perm, act_held[:, cols], preferred_element_type=f32)
            if c == 0:
                first = jnp.where(last, ids, body[:, :LANES])
                body = jnp.concatenate([first, body[:, LANES:]], axis=1)
            blocks[n][:, cols] = body.astype(bf16)
    place_ref[...] = jnp.broadcast_to(place.astype(f32), (LANES, rows)).T

def pack(where, tenant, slot, activations, local_count, wide_size, layout, span, per_turn):
    rows, features = activations.shape
    counts = [count for _, _, count in layout[slice(*span)]]
    chunks = 4
    whole = pl.BlockSpec(memory_space=VMEM)
    scalar = pl.BlockSpec(memory_space=pltpu.SMEM)
    return pl.pallas_call(
        functools.partial(pack_kernel, local_count, wide_size, layout, span, per_turn),
        out_shape=[
            jax.ShapeDtypeStruct((1, 1), i32),
            jax.ShapeDtypeStruct((rows, LANES), f32),
        ]
        + [pltpu.VMEM((c, features), bf16) for c in counts],
        in_specs=[scalar, whole, whole, pl.BlockSpec(memory_space=pltpu.HBM)],
        out_specs=[scalar, whole] + [whole for _ in counts],
        scratch_shapes=[VMEM((rows, features), bf16), pltpu.SemaphoreType.DMA((chunks,))],
        compiler_params=params(12),
        cost_estimate=cost(2 * sum(counts) * rows * features, 2 * features * (rows + sum(counts))),
        name="pack_rows",
    )(where, tenant, slot, in_hbm(activations))


def stage_kernel(down_ref, up_ref, down_out, up_out, sem):
    adapters, _, width = down_ref.shape
    copies = [
        pltpu.make_async_copy(
            down_ref.at[j], down_out.at[:, pl.ds(j * width, width)], sem.at[j]
        )
        for j in range(adapters)
    ]
    copies.append(pltpu.make_async_copy(up_ref, up_out, sem.at[adapters]))
    for copy in copies:
        copy.start()
    for copy in copies:
        copy.wait()


def stage(down_weight, up_weight):
    adapters, features, width = down_weight.shape
    whole = pl.BlockSpec(memory_space=VMEM)
    return pl.pallas_call(
        stage_kernel,
        out_shape=[
            pltpu.VMEM((features, adapters * width), down_weight.dtype),
            pltpu.VMEM(up_weight.shape, up_weight.dtype),
        ],
        in_specs=[pl.BlockSpec(memory_space=pltpu.HBM)] * 2,
        out_specs=[whole, whole],
        scratch_shapes=[pltpu.SemaphoreType.DMA((adapters + 1,))],
        compiler_params=params(12),
        cost_estimate=cost(10, 10),
        name="stage_maps",
    )(in_hbm(down_weight), in_hbm(up_weight))


def down_kernel(count, cols, narrow_size, per_step, where_ref, weight_ref, *refs):
    xs, refs = refs[:count], refs[count:]
    before, refs = (refs[:3], refs[3:]) if narrow_size else ((), refs)
    flag_ref, ids_ref, *outs, held_ref = refs
    steps = weight_ref.shape[1] // (per_step * LANES)

    flag = jnp.zeros((1, LANES), f32)
    ids = []
    offset = 0
    for x in xs:
        rows = x.shape[0]
        held_ref[pl.ds(offset, rows), :] = x[...]
        last = x[pl.ds(rows - 16, 16), :LANES].astype(f32)[15:]
        flag = jnp.maximum(flag, last)
        turned = jnp.broadcast_to(last, (LANES, LANES)).T[:rows]
        keep = lax.broadcasted_iota(i32, (rows, LANES), 0) < rows - 1
        ids.append(jnp.where(keep, turned, 0.0))
        offset += rows
    ids = jnp.concatenate(ids, axis=0)
    lane = lax.broadcasted_iota(i32, (1, LANES), 1)
    flag = jnp.max(jnp.where(lane == LANES - 1, flag, 0.0)).astype(i32)

    total = jnp.zeros(ids.shape, f32)
    for c in range(steps):
        weights = weight_ref[:, c * per_step * LANES : (c + 1) * per_step * LANES]
        found = jnp.dot(held_ref[...], weights, preferred_element_type=f32)
        for j in range(per_step):
            name = c * per_step + j + 1.0
            total = jnp.where(ids == name, found[:, j * LANES : (j + 1) * LANES], total)

    if not narrow_size:
        flag_ref[0, 0] = flag
        ids_ref[...] = ids
        outs[0][...] = total
        return
    if before:
        flag = jnp.maximum(flag, before[0][0, 0])
        ids = jnp.concatenate([before[1][...], ids], axis=0)
        total = jnp.concatenate([before[2][...], total], axis=0)
    flag_ref[0, 0] = flag
    padding = jnp.zeros((ids_ref.shape[0] - ids.shape[0], LANES), f32)
    if padding.shape[0]:
        ids = jnp.concatenate([ids, padding], axis=0)
        total = jnp.concatenate([total, padding], axis=0)
    ids_ref[...] = ids
    half = total.shape[0] // 2
    rank = LANES // 2
    top, bottom = total[:half], total[half:]
    low = lax.broadcasted_iota(i32, (half, LANES), 1) < rank
    keys = jnp.where(low, top, pltpu.roll(bottom, rank, 1))
    values = jnp.where(low, pltpu.roll(top, rank, 1), bottom)
    for j in range(narrow_size):
        start = jnp.bitwise_xor(where_ref[1], j) * cols
        outs[j][...] = jnp.where(start >= KEY_VALUE_COLS, values, keys).astype(outs[j].dtype)


def down(where, blocks, weight, cols, before, narrow_size, scale):
    features, width = weight.shape
    new_rows = sum(b.shape[0] for b in blocks)
    per_step = min(4, width // LANES)
    whole = pl.BlockSpec(memory_space=VMEM)
    scalar = pl.BlockSpec(memory_space=pltpu.SMEM)
    if narrow_size:
        rows = -(-(new_rows + before[1].shape[0]) // 32) * 32
        sums = [((rows // 2, LANES), bf16 if j else f32) for j in range(narrow_size)]
    else:
        rows = new_rows
        sums = [((rows, LANES), f32)]
    return pl.pallas_call(
        functools.partial(down_kernel, len(blocks), cols, narrow_size, per_step),
        out_shape=[
            jax.ShapeDtypeStruct((1, 1), i32),
            jax.ShapeDtypeStruct((rows, LANES), f32),
        ]
        + [jax.ShapeDtypeStruct(*s) for s in sums],
        in_specs=[scalar, whole]
        + [whole for _ in blocks]
        + ([scalar, whole, whole] if narrow_size else []),
        out_specs=[scalar, whole] + [whole for _ in sums],
        scratch_shapes=[VMEM((new_rows, features), bf16)],
        compiler_params=params(18),
        cost_estimate=cost(
            2 * new_rows * features * width, 2 * features * (new_rows + width), scale
        ),
        name="down_maps",
    )(where, weight, *blocks, *(before if narrow_size else []))


def up_kernel(narrow_size, ids_ref, *refs):
    parts, weight_ref, outs = refs[:narrow_size], refs[narrow_size], refs[narrow_size + 1 :]
    total = parts[0][...]
    for part in parts[1:]:
        total = total + part[...].astype(f32)
    low_rank = total.astype(bf16).astype(f32)
    rank = LANES // 2
    turned = pltpu.roll(low_rank, rank, 1)
    low = lax.broadcasted_iota(i32, low_rank.shape, 1) < rank
    twice = jnp.concatenate(
        [jnp.where(low, low_rank, turned), jnp.where(low, turned, low_rank)], axis=0
    )
    ids = ids_ref[...]
    second = (lax.broadcasted_iota(i32, ids.shape, 1) >= rank).astype(f32)
    adapters = weight_ref.shape[0] // rank
    left = [
        jnp.where(ids - second == 2.0 * pair + 1.0, twice, 0.0).astype(bf16)
        for pair in range(adapters // 2)
    ]
    found = jnp.dot(jnp.concatenate(left, axis=1), weight_ref[...], preferred_element_type=f32)
    offset = 0
    for out in outs:
        rows = out.shape[0]
        out[...] = found[offset : offset + rows].astype(bf16)
        offset += rows


def up(ids, parts, weight, counts):
    cols = weight.shape[1]
    return pl.pallas_call(
        functools.partial(up_kernel, len(parts)),
        out_shape=[jax.ShapeDtypeStruct((c, cols), bf16) for c in counts],
        compiler_params=params(10),
        cost_estimate=cost(2 * sum(counts) * weight.size, 2 * weight.size + 2 * sum(counts) * (cols + 512)),
        name="up_maps",
    )(ids, *parts, weight)


def base_kernel(count, where_ref, *refs):
    acts, weight_ref, so_far, out_ref = refs[:count], refs[count], refs[count + 1 : -1], refs[-1]
    step = pl.program_id(0)
    for j in range(count):

        @pl.when(step == j)
        def _(j=j):
            found = jnp.dot(acts[j][...], weight_ref[...], preferred_element_type=f32)
            if j:
                found = out_ref[...] + found
            elif so_far:
                found = so_far[0][...] + found
            out_ref[...] = found


def base(where, acts, first, weight, so_far):
    rows, features = acts[0].shape
    cols = weight.shape[1]
    count = len(acts)
    given = [] if so_far is None else [so_far]
    return pl.pallas_call(
        functools.partial(base_kernel, count),
        grid_spec=pltpu.PrefetchScalarGridSpec(
            num_scalar_prefetch=1,
            grid=(count,),
            in_specs=[pl.BlockSpec((rows, features), lambda i, where: (0, 0)) for _ in acts]
            + [
                pl.BlockSpec(
                    (features, cols),
                    lambda i, where: (jnp.bitwise_xor(where[1], first + i), 0),
                )
            ]
            + [pl.BlockSpec((rows, cols), lambda i, where: (0, 0)) for _ in given],
            out_specs=pl.BlockSpec((rows, cols), lambda i, where: (0, 0)),
        ),
        out_shape=jax.ShapeDtypeStruct((rows, cols), f32),
        compiler_params=params(14),
        cost_estimate=cost(2 * rows * features * count * cols, 2 * features * count * (cols + rows)),
        name="shared_projection",
    )(where, *acts, in_hbm(weight), *given)


def join_kernel(base_ref, place_ref, *refs):
    corrections, out_ref, held_ref, sem = refs[:-3], *refs[-3:]
    stacked = jnp.concatenate([c[...] for c in corrections], axis=0)
    rows, count = base_ref.shape[0], stacked.shape[0]
    parts = sem.shape[0]
    copies = []
    for n in range(parts):
        part = pl.ds(n * (rows // parts), rows // parts)
        place = place_ref[part, :1].astype(i32)
        perm = lax.broadcasted_iota(i32, (rows // parts, count), 1) == place
        found = jnp.dot(perm.astype(f32).astype(bf16), stacked, preferred_element_type=f32)
        held_ref[part, :] = (base_ref[part, :] + found).astype(out_ref.dtype)
        copy = pltpu.make_async_copy(held_ref.at[part, :], out_ref.at[part, :], sem.at[n])
        copy.start()
        copies.append(copy)
    for copy in copies:
        copy.wait()


def join(base_out, place, corrections, dtype):
    rows, cols = base_out.shape
    count = sum(c.shape[0] for c in corrections)
    parts = 2
    return pl.pallas_call(
        join_kernel,
        out_shape=pltpu.HBM((rows, cols), dtype),
        in_specs=[pl.BlockSpec(memory_space=VMEM)] * (2 + len(corrections)),
        out_specs=pl.BlockSpec(memory_space=pltpu.HBM),
        scratch_shapes=[VMEM((rows, cols), dtype), pltpu.SemaphoreType.DMA((parts,))],
        compiler_params=params(10),
        cost_estimate=cost(2 * rows * cols * count, 2 * cols * (count + 3 * rows)),
        name="join_corrections",
    )(base_out, place, *corrections)


def raise_sums(ids, sums, up_weight, counts):
    sums = [swap(part, "narrow", j) if j else part for j, part in enumerate(sums)]
    return up(ids, sums, up_weight, counts)


def later_turn(turn, axes, total, done, tenant, slot, activations, down_weight, up_weight):
    wide_size, narrow_size = lax.axis_size("wide"), lax.axis_size("narrow")
    where = jnp.stack([*axes, turn])
    layout = [(k, end, LATER_ROWS) for k, end in enumerate(done)]
    _, place, *sent = pack(
        where,
        tenant,
        slot,
        activations,
        down_weight.shape[0],
        wide_size,
        layout,
        (0, wide_size),
        LATER_ROWS - 1,
    )
    got = [swap(b, "wide", k) if k else b for k, b in enumerate(sent)]
    cols = up_weight.shape[1]
    down_weight, up_weight = stage(down_weight, up_weight)
    before = down(where, got[:1], down_weight, cols, None, 0, 0.001)
    more, ids, *sums = down(where, got[1:], down_weight, cols, before, narrow_size, 0.001)
    outs = raise_sums(ids, sums, up_weight, [b.shape[0] for b in got])
    answers = [swap(b, "wide", k) if k else b for k, b in enumerate(outs)]
    return join(total, place, answers, f32), more[0, 0]


def on_device(
    activations,
    request_tenants,
    adapter_slot,
    shared_weight,
    adapter_down_weight,
    adapter_up_weight,
):
    rows = activations.shape[0]
    wide_size, narrow_size = lax.axis_size("wide"), lax.axis_size("narrow")
    local_count = adapter_down_weight.shape[0]
    axes = (lax.axis_index("wide").astype(i32), lax.axis_index("narrow").astype(i32))
    where = jnp.stack([*axes, jnp.int32(0)])
    tenant = request_tenants.reshape(1, rows)
    slot = adapter_slot.reshape(1, -1)
    up_weight = adapter_up_weight.reshape(-1, adapter_up_weight.shape[-1])

    cols = up_weight.shape[1]
    layout = first_turn(wide_size, local_count)
    own = len(layout) - 1
    routed = (local_count, wide_size, layout)
    begun, place, *sent = pack(where, tenant, slot, activations, *routed, (0, own), 0)
    got = [swap(b, "wide", k) for (k, _, _), b in zip(layout, sent)]
    half = narrow_size // 2

    def step(work, *operands):
        def never(*operands):
            return jax.tree.map(
                lambda s: jnp.zeros(s.shape, s.dtype), jax.eval_shape(work, *operands)
            )

        return lax.cond(begun[0, 0] > 0, work, never, *operands)

    def spread(act):
        acts, bit = {0: act}, half // 2
        while bit:
            acts.update({j ^ bit: swap(x, "narrow", bit) for j, x in list(acts.items())})
            bit //= 2
        return [acts[j] for j in sorted(acts)]

    def pack_own(tenant, slot, activations):
        return pack(where, tenant, slot, activations, *routed, (own, own + 1), 0)[2]

    def work_before(activations, shared_weight, maps):
        return base(where, spread(activations), 0, shared_weight, None), stage(*maps)

    def work_after(across, shared_weight, base_out):
        return base(where, spread(across), half, shared_weight, base_out)

    shared_weight, maps = after_all((shared_weight, (adapter_down_weight, up_weight)), *sent)
    own_block = step(pack_own, tenant, slot, activations)
    across = swap(after(activations, own_block), "narrow", half) if half else None
    base_out, (down_beside, up_beside) = step(
        work_before, *after_all((activations, shared_weight, maps), own_block)
    )
    before = down(where, [got[-1], after(own_block, base_out)], down_beside, cols, None, 0, 0.001)
    more, ids, *sums = down(
        where, after_all(got[:-1], *before), down_beside, cols, before, narrow_size, 20
    )
    counts = [layout[n][2] for n in (own - 1, own, *range(own - 1))]
    outs = raise_sums(ids, sums, up_beside, counts)
    outs = [*outs[2:], *outs[:2]]
    answers = [swap(b, "wide", k) if k else b for (k, _, _), b in zip(layout, outs)]
    if half:
        base_out = step(work_after, *after_all((across, shared_weight, base_out), *outs))
    more = more[0, 0]

    def done(base_out):
        return join(base_out, place, answers, bf16)

    def go_on(base_out):
        def turn_of(state):
            turn, _, total = state
            total, more = later_turn(
                turn, axes, total, ends(layout, wide_size), tenant, slot, activations, adapter_down_weight, up_weight
            )
            return turn + 1, more, total

        state = (jnp.int32(0), jnp.int32(1), join(base_out, place, answers, f32))
        return lax.while_loop(lambda s: s[1] > 0, turn_of, state)[2].astype(bf16)

    return lax.cond(more > 0, go_on, done, base_out)


def solution(mesh):
    in_specs = (
        P(("groups", "wide"), "narrow"),
        P(("groups", "wide"), None),
        P(),
        P(None, "narrow"),
        P("wide", "narrow", None),
        P("wide", None, "narrow"),
    )
    out_specs = P(("groups", "wide"), "narrow")
    return jax.shard_map(
        on_device, mesh=mesh, in_specs=in_specs, out_specs=out_specs, check_vma=False
    )
```

```python
import functools

import jax
import jax.numpy as jnp
from jax import lax
from jax.experimental import pallas as pl
from jax.experimental.pallas import tpu as pltpu
from jax.sharding import PartitionSpec as P

KEY_VALUE_COLS = 1024
LANES = 128
MOST = 16
OWN_ROWS = 112
AWAY_ROWS = 96
LATER_ROWS = 32
VMEM = pltpu.VMEM
MIB = 1 << 20

f32, bf16, i32 = jnp.float32, jnp.bfloat16, jnp.int32


def first_turn(wide_size, local_count):
    most = -(-(local_count * MOST + 1) // 32) * 32
    return [(k, 0, min(AWAY_ROWS if k else OWN_ROWS, most)) for k in reversed(range(wide_size))]


def ends(blocks, wide_size):
    return [max(start + count - 1 for j, start, count in blocks if j == k) for k in range(wide_size)]


def swap(x, axis, k):
    size = lax.axis_size(axis)
    return lax.ppermute(x, axis, [(i, i ^ k) for i in range(size)])


def after(x, *others):
    return lax.optimization_barrier((x, *others))[0]


def after_all(xs, *others):
    return lax.optimization_barrier((xs, others))[0]


def cost(flops, bytes_accessed, scale=0.001):
    return pl.CostEstimate(
        flops=int(flops * scale), bytes_accessed=int(bytes_accessed * scale), transcendentals=0
    )


def params(mib):
    return pltpu.CompilerParams(vmem_limit_bytes=mib * MIB)


def in_hbm(x):
    return pltpu.with_memory_space_constraint(x, pltpu.HBM)


def pack_kernel(
    local_count, wide_size, layout, span, per_turn, where_ref, tenant_ref, slot_ref, act_ref, *refs
):
    picked = range(*span)
    begun_ref, refs = refs[0], refs[1:]
    last_span = span[1] == len(layout)
    place_ref, refs = (refs[0], refs[1:]) if last_span else (None, refs)
    blocks = dict(zip(picked, refs[:-2]))
    act_held, in_sem = refs[-2:]
    rows, features = act_held.shape
    chunks = in_sem.shape[0]
    width = features // chunks

    def load(c):
        cols = pl.ds(c * width, width)
        return pltpu.make_async_copy(act_ref.at[:, cols], act_held.at[:, cols], in_sem.at[c])

    for c in range(chunks):
        load(c).start()
    begun_ref[0, 0] = jnp.int32(1)

    tenants = slot_ref.shape[1]
    tenant = tenant_ref[...]
    named = tenant == lax.broadcasted_iota(i32, (tenants, rows), 0)
    slots = jnp.broadcast_to(slot_ref[...].astype(f32), (8, tenants)).astype(bf16)
    slot = jnp.dot(slots, named.astype(f32).astype(bf16), preferred_element_type=f32)[:1]
    dest = jnp.floor((slot + 0.5) * (1.0 / local_count))
    adapter = slot - dest * local_count + 1.0
    leap = jnp.bitwise_xor(dest.astype(i32), where_ref[0])
    padded = max(8, wide_size)
    goes = (leap == lax.broadcasted_iota(i32, (padded, rows), 0)).astype(f32)
    earlier = lax.broadcasted_iota(i32, (rows, rows), 0) < lax.broadcasted_iota(
        i32, (rows, rows), 1
    )
    before = jnp.dot(
        goes.astype(bf16), earlier.astype(f32).astype(bf16), preferred_element_type=f32
    )
    position = jnp.sum(goes * before, axis=0, keepdims=True).astype(i32)
    adapters = jnp.broadcast_to(adapter, (8, rows)).astype(bf16)
    place = jnp.full((1, rows), -1, i32)
    more = jnp.zeros((1, rows), f32)
    position = position - where_ref[2] * per_turn
    for k, end in enumerate(ends(layout, wide_size)):
        more = jnp.where((leap == k) & (position >= end), 1.0, more)
    offset, here = 0, []
    for k, start, count in layout:
        mine = position - start
        mine = jnp.where((leap == k) & (mine >= 0) & (mine < count - 1), mine, -1)
        place = jnp.where(mine >= 0, mine + offset, place)
        offset += count
        here.append(mine)
    any_more = jnp.max(more, axis=1, keepdims=True)

    perm = jnp.concatenate(
        [
            (lax.broadcasted_iota(i32, (LANES, rows), 0) == here[n]).astype(f32).astype(bf16)
            for n in picked
        ],
        axis=0,
    )
    all_ids = lax.dot_general(
        adapters, perm, (((1,), (1,)), ((), ())), preferred_element_type=f32
    )
    lane = lax.broadcasted_iota(i32, (1, LANES), 1)
    for c in range(chunks):
        cols = pl.ds(c * width, width)
        load(c).wait()
        body = jnp.dot(perm, act_held[:, cols], preferred_element_type=f32)
        for m, n in enumerate(picked):
            count = layout[n][2]
            part = body[m * LANES : m * LANES + count]
            if c == 0:
                ids = all_ids[:1, m * LANES : (m + 1) * LANES]
                ids = jnp.where(lane == LANES - 1, any_more, ids)
                last = lax.broadcasted_iota(i32, (count, LANES), 0) == count - 1
                first = jnp.where(last, ids, part[:, :LANES])
                part = jnp.concatenate([first, part[:, LANES:]], axis=1)
            blocks[n][:, cols] = part.astype(bf16)
    if last_span:
        place_ref[...] = jnp.broadcast_to(place.astype(f32), (LANES, rows)).T


def pack(where, tenant, slot, activations, local_count, wide_size, layout, span, per_turn):
    rows, features = activations.shape
    counts = [count for _, _, count in layout[slice(*span)]]
    places = [jax.ShapeDtypeStruct((rows, LANES), f32)] if span[1] == len(layout) else []
    chunks = 4
    whole = pl.BlockSpec(memory_space=VMEM)
    scalar = pl.BlockSpec(memory_space=pltpu.SMEM)
    return pl.pallas_call(
        functools.partial(pack_kernel, local_count, wide_size, layout, span, per_turn),
        out_shape=[
            jax.ShapeDtypeStruct((1, 1), i32),
            *places,
        ]
        + [pltpu.VMEM((c, features), bf16) for c in counts],
        in_specs=[scalar, whole, whole, pl.BlockSpec(memory_space=pltpu.HBM)],
        out_specs=[scalar] + [whole for _ in [*places, *counts]],
        scratch_shapes=[VMEM((rows, features), bf16), pltpu.SemaphoreType.DMA((chunks,))],
        compiler_params=params(12),
        cost_estimate=cost(2 * sum(counts) * rows * features, 2 * features * (rows + sum(counts))),
        name="pack_rows",
    )(where, tenant, slot, in_hbm(activations))


def stage_kernel(down_ref, up_ref, down_out, up_out, sem):
    adapters, _, width = down_ref.shape
    copies = [
        pltpu.make_async_copy(
            down_ref.at[j], down_out.at[:, pl.ds(j * width, width)], sem.at[j]
        )
        for j in range(adapters)
    ]
    copies.append(pltpu.make_async_copy(up_ref, up_out, sem.at[adapters]))
    for copy in copies:
        copy.start()
    for copy in copies:
        copy.wait()


def stage(down_weight, up_weight):
    adapters, features, width = down_weight.shape
    whole = pl.BlockSpec(memory_space=VMEM)
    return pl.pallas_call(
        stage_kernel,
        out_shape=[
            pltpu.VMEM((features, adapters * width), down_weight.dtype),
            pltpu.VMEM(up_weight.shape, up_weight.dtype),
        ],
        in_specs=[pl.BlockSpec(memory_space=pltpu.HBM)] * 2,
        out_specs=[whole, whole],
        scratch_shapes=[pltpu.SemaphoreType.DMA((adapters + 1,))],
        compiler_params=params(12),
        cost_estimate=cost(10, 10),
        name="stage_maps",
    )(in_hbm(down_weight), in_hbm(up_weight))


def down_kernel(count, cols, narrow_size, per_step, where_ref, weight_ref, *refs):
    xs, refs = refs[:count], refs[count:]
    before, refs = (refs[:3], refs[3:]) if narrow_size else ((), refs)
    flag_ref, ids_ref, *outs, held_ref = refs
    steps = weight_ref.shape[1] // (per_step * LANES)

    flag = jnp.zeros((1, LANES), f32)
    ids = []
    offset = 0
    for x in xs:
        rows = x.shape[0]
        held_ref[pl.ds(offset, rows), :] = x[...]
        last = x[pl.ds(rows - 16, 16), :LANES].astype(f32)[15:]
        flag = jnp.maximum(flag, last)
        turned = jnp.broadcast_to(last, (LANES, LANES)).T[:rows]
        keep = lax.broadcasted_iota(i32, (rows, LANES), 0) < rows - 1
        ids.append(jnp.where(keep, turned, 0.0))
        offset += rows
    ids = jnp.concatenate(ids, axis=0)
    lane = lax.broadcasted_iota(i32, (1, LANES), 1)
    flag = jnp.max(jnp.where(lane == LANES - 1, flag, 0.0)).astype(i32)

    total = jnp.zeros(ids.shape, f32)
    for c in range(steps):
        weights = weight_ref[:, c * per_step * LANES : (c + 1) * per_step * LANES]
        found = jnp.dot(held_ref[...], weights, preferred_element_type=f32)
        for j in range(per_step):
            name = c * per_step + j + 1.0
            total = jnp.where(ids == name, found[:, j * LANES : (j + 1) * LANES], total)

    if not narrow_size:
        flag_ref[0, 0] = flag
        ids_ref[...] = ids
        outs[0][...] = total
        return
    if before:
        flag = jnp.maximum(flag, before[0][0, 0])
        ids = jnp.concatenate([before[1][...], ids], axis=0)
        total = jnp.concatenate([before[2][...], total], axis=0)
    flag_ref[0, 0] = flag
    padding = jnp.zeros((ids_ref.shape[0] - ids.shape[0], LANES), f32)
    if padding.shape[0]:
        ids = jnp.concatenate([ids, padding], axis=0)
        total = jnp.concatenate([total, padding], axis=0)
    ids_ref[...] = ids
    half = total.shape[0] // 2
    rank = LANES // 2
    top, bottom = total[:half], total[half:]
    low = lax.broadcasted_iota(i32, (half, LANES), 1) < rank
    keys = jnp.where(low, top, pltpu.roll(bottom, rank, 1))
    values = jnp.where(low, pltpu.roll(top, rank, 1), bottom)
    for j in range(narrow_size):
        start = jnp.bitwise_xor(where_ref[1], j) * cols
        outs[j][...] = jnp.where(start >= KEY_VALUE_COLS, values, keys).astype(outs[j].dtype)


def down(where, blocks, weight, cols, before, narrow_size, scale):
    features, width = weight.shape
    new_rows = sum(b.shape[0] for b in blocks)
    per_step = min(4, width // LANES)
    whole = pl.BlockSpec(memory_space=VMEM)
    scalar = pl.BlockSpec(memory_space=pltpu.SMEM)
    if narrow_size:
        rows = -(-(new_rows + before[1].shape[0]) // 32) * 32
        sums = [((rows // 2, LANES), bf16 if j else f32) for j in range(narrow_size)]
    else:
        rows = new_rows
        sums = [((rows, LANES), f32)]
    return pl.pallas_call(
        functools.partial(down_kernel, len(blocks), cols, narrow_size, per_step),
        out_shape=[
            jax.ShapeDtypeStruct((1, 1), i32),
            jax.ShapeDtypeStruct((rows, LANES), f32),
        ]
        + [jax.ShapeDtypeStruct(*s) for s in sums],
        in_specs=[scalar, whole]
        + [whole for _ in blocks]
        + ([scalar, whole, whole] if narrow_size else []),
        out_specs=[scalar, whole] + [whole for _ in sums],
        scratch_shapes=[VMEM((new_rows, features), bf16)],
        compiler_params=params(18),
        cost_estimate=cost(
            2 * new_rows * features * width, 2 * features * (new_rows + width), scale
        ),
        name="down_maps",
    )(where, weight, *blocks, *(before if narrow_size else []))


def up_kernel(narrow_size, ids_ref, *refs):
    parts, weight_ref, outs = refs[:narrow_size], refs[narrow_size], refs[narrow_size + 1 :]
    total = parts[0][...]
    for part in parts[1:]:
        total = total + part[...].astype(f32)
    low_rank = total.astype(bf16).astype(f32)
    rank = LANES // 2
    turned = pltpu.roll(low_rank, rank, 1)
    low = lax.broadcasted_iota(i32, low_rank.shape, 1) < rank
    twice = jnp.concatenate(
        [jnp.where(low, low_rank, turned), jnp.where(low, turned, low_rank)], axis=0
    )
    ids = ids_ref[...]
    second = (lax.broadcasted_iota(i32, ids.shape, 1) >= rank).astype(f32)
    adapters = weight_ref.shape[0] // rank
    left = [
        jnp.where(ids - second == 2.0 * pair + 1.0, twice, 0.0).astype(bf16)
        for pair in range(adapters // 2)
    ]
    found = jnp.dot(jnp.concatenate(left, axis=1), weight_ref[...], preferred_element_type=f32)
    offset = 0
    for out in outs:
        rows = out.shape[0]
        out[...] = found[offset : offset + rows].astype(bf16)
        offset += rows


def up(ids, parts, weight, counts):
    cols = weight.shape[1]
    return pl.pallas_call(
        functools.partial(up_kernel, len(parts)),
        out_shape=[jax.ShapeDtypeStruct((c, cols), bf16) for c in counts],
        compiler_params=params(10),
        cost_estimate=cost(2 * sum(counts) * weight.size, 2 * weight.size + 2 * sum(counts) * (cols + 512)),
        name="up_maps",
    )(ids, *parts, weight)


def base_kernel(count, where_ref, *refs):
    acts, weight_ref, so_far, out_ref = refs[:count], refs[count], refs[count + 1 : -1], refs[-1]
    step = pl.program_id(0)
    for j in range(count):

        @pl.when(step == j)
        def _(j=j):
            found = jnp.dot(acts[j][...], weight_ref[...], preferred_element_type=f32)
            if j:
                found = out_ref[...] + found
            elif so_far:
                found = so_far[0][...] + found
            out_ref[...] = found


def base(where, acts, first, weight, so_far):
    rows, features = acts[0].shape
    cols = weight.shape[1]
    count = len(acts)
    given = [] if so_far is None else [so_far]
    return pl.pallas_call(
        functools.partial(base_kernel, count),
        grid_spec=pltpu.PrefetchScalarGridSpec(
            num_scalar_prefetch=1,
            grid=(count,),
            in_specs=[pl.BlockSpec((rows, features), lambda i, where: (0, 0)) for _ in acts]
            + [
                pl.BlockSpec(
                    (features, cols),
                    lambda i, where: (jnp.bitwise_xor(where[1], first + i), 0),
                )
            ]
            + [pl.BlockSpec((rows, cols), lambda i, where: (0, 0)) for _ in given],
            out_specs=pl.BlockSpec((rows, cols), lambda i, where: (0, 0)),
        ),
        out_shape=jax.ShapeDtypeStruct((rows, cols), f32),
        compiler_params=params(14),
        cost_estimate=cost(2 * rows * features * count * cols, 2 * features * count * (cols + rows)),
        name="shared_projection",
    )(where, *acts, in_hbm(weight), *given)


def join_kernel(base_ref, place_ref, *refs):
    corrections, out_ref, held_ref, sem = refs[:-3], *refs[-3:]
    stacked = jnp.concatenate([c[...] for c in corrections], axis=0)
    rows, count = base_ref.shape[0], stacked.shape[0]
    parts = sem.shape[0]
    copies = []
    for n in range(parts):
        part = pl.ds(n * (rows // parts), rows // parts)
        place = place_ref[part, :1].astype(i32)
        perm = lax.broadcasted_iota(i32, (rows // parts, count), 1) == place
        found = jnp.dot(perm.astype(f32).astype(bf16), stacked, preferred_element_type=f32)
        held_ref[part, :] = (base_ref[part, :] + found).astype(out_ref.dtype)
        copy = pltpu.make_async_copy(held_ref.at[part, :], out_ref.at[part, :], sem.at[n])
        copy.start()
        copies.append(copy)
    for copy in copies:
        copy.wait()


def join(base_out, place, corrections, dtype):
    rows, cols = base_out.shape
    count = sum(c.shape[0] for c in corrections)
    parts = 2
    return pl.pallas_call(
        join_kernel,
        out_shape=pltpu.HBM((rows, cols), dtype),
        in_specs=[pl.BlockSpec(memory_space=VMEM)] * (2 + len(corrections)),
        out_specs=pl.BlockSpec(memory_space=pltpu.HBM),
        scratch_shapes=[VMEM((rows, cols), dtype), pltpu.SemaphoreType.DMA((parts,))],
        compiler_params=params(10),
        cost_estimate=cost(2 * rows * cols * count, 2 * cols * (count + 3 * rows)),
        name="join_corrections",
    )(base_out, place, *corrections)


def raise_sums(ids, sums, up_weight, counts):
    sums = [swap(part, "narrow", j) if j else part for j, part in enumerate(sums)]
    return up(ids, sums, up_weight, counts)


def later_turn(turn, axes, total, done, tenant, slot, activations, down_weight, up_weight):
    wide_size, narrow_size = lax.axis_size("wide"), lax.axis_size("narrow")
    where = jnp.stack([*axes, turn])
    layout = [(k, end, LATER_ROWS) for k, end in enumerate(done)]
    _, place, *sent = pack(
        where,
        tenant,
        slot,
        activations,
        down_weight.shape[0],
        wide_size,
        layout,
        (0, wide_size),
        LATER_ROWS - 1,
    )
    got = [swap(b, "wide", k) if k else b for k, b in enumerate(sent)]
    cols = up_weight.shape[1]
    down_weight, up_weight = stage(down_weight, up_weight)
    before = down(where, got[:1], down_weight, cols, None, 0, 0.001)
    more, ids, *sums = down(where, got[1:], down_weight, cols, before, narrow_size, 0.001)
    outs = raise_sums(ids, sums, up_weight, [b.shape[0] for b in got])
    answers = [swap(b, "wide", k) if k else b for k, b in enumerate(outs)]
    return join(total, place, answers, f32), more[0, 0]


def on_device(
    activations,
    request_tenants,
    adapter_slot,
    shared_weight,
    adapter_down_weight,
    adapter_up_weight,
):
    rows = activations.shape[0]
    wide_size, narrow_size = lax.axis_size("wide"), lax.axis_size("narrow")
    local_count = adapter_down_weight.shape[0]
    axes = (lax.axis_index("wide").astype(i32), lax.axis_index("narrow").astype(i32))
    where = jnp.stack([*axes, jnp.int32(0)])
    tenant = request_tenants.reshape(1, rows)
    slot = adapter_slot.reshape(1, -1)
    up_weight = adapter_up_weight.reshape(-1, adapter_up_weight.shape[-1])

    cols = up_weight.shape[1]
    layout = first_turn(wide_size, local_count)
    own = len(layout) - 1
    routed = (local_count, wide_size, layout)
    begun, *sent = pack(where, tenant, slot, activations, *routed, (0, 1), 0)
    if own > 1:
        sent += pack(where, tenant, slot, after(activations, *sent), *routed, (1, own), 0)[1:]
    got = [swap(b, "wide", k) for (k, _, _), b in zip(layout, sent)]
    half = narrow_size // 2

    def step(work, *operands):
        def never(*operands):
            return jax.tree.map(
                lambda s: jnp.zeros(s.shape, s.dtype), jax.eval_shape(work, *operands)
            )

        return lax.cond(begun[0, 0] > 0, work, never, *operands)

    def spread(act):
        acts, bit = {0: act}, half // 2
        while bit:
            acts.update({j ^ bit: swap(x, "narrow", bit) for j, x in list(acts.items())})
            bit //= 2
        return [acts[j] for j in sorted(acts)]

    def pack_own(tenant, slot, activations):
        return pack(where, tenant, slot, activations, *routed, (own, own + 1), 0)[1:]

    def work_before(activations, shared_weight, maps):
        return base(where, spread(activations), 0, shared_weight, None), stage(*maps)

    def work_after(across, shared_weight, base_out):
        return base(where, spread(across), half, shared_weight, base_out)

    shared_weight, maps = after_all((shared_weight, (adapter_down_weight, up_weight)), *sent)
    place, own_block = step(pack_own, tenant, slot, after(activations, *sent))
    across = swap(after(activations, own_block), "narrow", half) if half else None
    base_out, (down_beside, up_beside) = step(
        work_before, *after_all((activations, shared_weight, maps), own_block)
    )
    before = down(where, [got[0], after(own_block, base_out)], down_beside, cols, None, 0, 0.001)
    more, ids, *sums = down(
        where, after_all(got[1:], *before), down_beside, cols, before, narrow_size, 20
    )
    counts = [layout[n][2] for n in (0, own, *range(1, own))]
    outs = raise_sums(ids, sums, up_beside, counts)
    outs = [outs[0], *outs[2:], outs[1]]
    answers = [swap(b, "wide", k) if k else b for (k, _, _), b in zip(layout, outs)]
    if half:
        base_out = step(work_after, *after_all((across, shared_weight, base_out), *outs))
    more = more[0, 0]

    def done(base_out):
        return join(base_out, place, answers, bf16)

    def go_on(base_out):
        def turn_of(state):
            turn, _, total = state
            total, more = later_turn(
                turn, axes, total, ends(layout, wide_size), tenant, slot, activations, adapter_down_weight, up_weight
            )
            return turn + 1, more, total

        state = (jnp.int32(0), jnp.int32(1), join(base_out, place, answers, f32))
        return lax.while_loop(lambda s: s[1] > 0, turn_of, state)[2].astype(bf16)

    return lax.cond(more > 0, go_on, done, base_out)


def solution(mesh):
    in_specs = (
        P(("groups", "wide"), "narrow"),
        P(("groups", "wide"), None),
        P(),
        P(None, "narrow"),
        P("wide", "narrow", None),
        P("wide", None, "narrow"),
    )
    out_specs = P(("groups", "wide"), "narrow")
    return jax.shard_map(
        on_device, mesh=mesh, in_specs=in_specs, out_specs=out_specs, check_vma=False
    )
```

```python
import functools

import jax
import jax.numpy as jnp
from jax import lax
from jax.experimental import pallas as pl
from jax.experimental.pallas import tpu as pltpu
from jax.sharding import PartitionSpec as P

KEY_VALUE_COLS = 1024
LANES = 128
MOST = 16
OWN_ROWS = 112
AWAY_ROWS = 96
LATER_ROWS = 32
VMEM = pltpu.VMEM
MIB = 1 << 20

f32, bf16, i32 = jnp.float32, jnp.bfloat16, jnp.int32


def first_turn(wide_size, local_count):
    most = -(-(local_count * MOST + 1) // 32) * 32
    return [(k, 0, min(AWAY_ROWS if k else OWN_ROWS, most)) for k in reversed(range(wide_size))]


def ends(blocks, wide_size):
    return [max(start + count - 1 for j, start, count in blocks if j == k) for k in range(wide_size)]


def swap(x, axis, k):
    size = lax.axis_size(axis)
    return lax.ppermute(x, axis, [(i, i ^ k) for i in range(size)])


def after(x, *others):
    return lax.optimization_barrier((x, *others))[0]


def after_all(xs, *others):
    return lax.optimization_barrier((xs, others))[0]


def cost(flops, bytes_accessed, scale=0.001):
    return pl.CostEstimate(
        flops=int(flops * scale), bytes_accessed=int(bytes_accessed * scale), transcendentals=0
    )


def params(mib):
    return pltpu.CompilerParams(vmem_limit_bytes=mib * MIB)


def in_hbm(x):
    return pltpu.with_memory_space_constraint(x, pltpu.HBM)


def pack_kernel(
    local_count, wide_size, layout, span, per_turn, where_ref, tenant_ref, slot_ref, act_ref, *refs
):
    picked = range(*span)
    begun_ref, refs = refs[0], refs[1:]
    last_span = span[1] == len(layout)
    place_ref, refs = (refs[0], refs[1:]) if last_span else (None, refs)
    blocks = dict(zip(picked, refs[:-2]))
    act_held, in_sem = refs[-2:]
    rows, features = act_held.shape
    chunks = 4
    width = features // chunks
    loads = in_sem.shape[0]

    def load(n):
        part = pl.ds(n * (rows // loads), rows // loads)
        return pltpu.make_async_copy(act_ref.at[part, :], act_held.at[part, :], in_sem.at[n])

    for n in range(loads):
        load(n).start()
    begun_ref[0, 0] = jnp.int32(1)

    tenants = slot_ref.shape[1]
    tenant = tenant_ref[...]
    named = tenant == lax.broadcasted_iota(i32, (tenants, rows), 0)
    slots = jnp.broadcast_to(slot_ref[...].astype(f32), (8, tenants)).astype(bf16)
    slot = jnp.dot(slots, named.astype(f32).astype(bf16), preferred_element_type=f32)[:1]
    dest = jnp.floor((slot + 0.5) * (1.0 / local_count))
    adapter = slot - dest * local_count + 1.0
    leap = jnp.bitwise_xor(dest.astype(i32), where_ref[0])
    padded = max(8, wide_size)
    goes = (leap == lax.broadcasted_iota(i32, (padded, rows), 0)).astype(f32)
    earlier = lax.broadcasted_iota(i32, (rows, rows), 0) < lax.broadcasted_iota(
        i32, (rows, rows), 1
    )
    before = jnp.dot(
        goes.astype(bf16), earlier.astype(f32).astype(bf16), preferred_element_type=f32
    )
    position = jnp.sum(goes * before, axis=0, keepdims=True).astype(i32)
    adapters = jnp.broadcast_to(adapter, (8, rows)).astype(bf16)
    place = jnp.full((1, rows), -1, i32)
    more = jnp.zeros((1, rows), f32)
    position = position - where_ref[2] * per_turn
    for k, end in enumerate(ends(layout, wide_size)):
        more = jnp.where((leap == k) & (position >= end), 1.0, more)
    offset, here = 0, []
    for k, start, count in layout:
        mine = position - start
        mine = jnp.where((leap == k) & (mine >= 0) & (mine < count - 1), mine, -1)
        place = jnp.where(mine >= 0, mine + offset, place)
        offset += count
        here.append(mine)
    any_more = jnp.max(more, axis=1, keepdims=True)

    perm = jnp.concatenate(
        [
            (lax.broadcasted_iota(i32, (LANES, rows), 0) == here[n]).astype(f32).astype(bf16)
            for n in picked
        ],
        axis=0,
    )
    all_ids = lax.dot_general(
        adapters, perm, (((1,), (1,)), ((), ())), preferred_element_type=f32
    )
    lane = lax.broadcasted_iota(i32, (1, LANES), 1)
    for n in range(loads):
        load(n).wait()
    for c in range(chunks):
        cols = pl.ds(c * width, width)
        body = jnp.dot(perm, act_held[:, cols], preferred_element_type=f32)
        for m, n in enumerate(picked):
            count = layout[n][2]
            part = body[m * LANES : m * LANES + count]
            if c == 0:
                ids = all_ids[:1, m * LANES : (m + 1) * LANES]
                ids = jnp.where(lane == LANES - 1, any_more, ids)
                last = lax.broadcasted_iota(i32, (count, LANES), 0) == count - 1
                first = jnp.where(last, ids, part[:, :LANES])
                part = jnp.concatenate([first, part[:, LANES:]], axis=1)
            blocks[n][:, cols] = part.astype(bf16)
    if last_span:
        place_ref[...] = jnp.broadcast_to(place.astype(f32), (LANES, rows)).T


def pack(where, tenant, slot, activations, local_count, wide_size, layout, span, per_turn):
    rows, features = activations.shape
    counts = [count for _, _, count in layout[slice(*span)]]
    places = [jax.ShapeDtypeStruct((rows, LANES), f32)] if span[1] == len(layout) else []
    loads = 4
    whole = pl.BlockSpec(memory_space=VMEM)
    scalar = pl.BlockSpec(memory_space=pltpu.SMEM)
    return pl.pallas_call(
        functools.partial(pack_kernel, local_count, wide_size, layout, span, per_turn),
        out_shape=[
            jax.ShapeDtypeStruct((1, 1), i32),
            *places,
        ]
        + [pltpu.VMEM((c, features), bf16) for c in counts],
        in_specs=[scalar, whole, whole, pl.BlockSpec(memory_space=pltpu.HBM)],
        out_specs=[scalar] + [whole for _ in [*places, *counts]],
        scratch_shapes=[VMEM((rows, features), bf16), pltpu.SemaphoreType.DMA((loads,))],
        compiler_params=params(12),
        cost_estimate=cost(2 * sum(counts) * rows * features, 2 * features * (rows + sum(counts))),
        name="pack_rows",
    )(where, tenant, slot, in_hbm(activations))


def stage_kernel(down_ref, up_ref, down_out, up_out, sem):
    adapters, _, width = down_ref.shape
    copies = [
        pltpu.make_async_copy(
            down_ref.at[j], down_out.at[:, pl.ds(j * width, width)], sem.at[j]
        )
        for j in range(adapters)
    ]
    copies.append(pltpu.make_async_copy(up_ref, up_out, sem.at[adapters]))
    for copy in copies:
        copy.start()
    for copy in copies:
        copy.wait()


def stage(down_weight, up_weight):
    adapters, features, width = down_weight.shape
    whole = pl.BlockSpec(memory_space=VMEM)
    return pl.pallas_call(
        stage_kernel,
        out_shape=[
            pltpu.VMEM((features, adapters * width), down_weight.dtype),
            pltpu.VMEM(up_weight.shape, up_weight.dtype),
        ],
        in_specs=[pl.BlockSpec(memory_space=pltpu.HBM)] * 2,
        out_specs=[whole, whole],
        scratch_shapes=[pltpu.SemaphoreType.DMA((adapters + 1,))],
        compiler_params=params(12),
        cost_estimate=cost(10, 10),
        name="stage_maps",
    )(in_hbm(down_weight), in_hbm(up_weight))


def down_kernel(count, cols, narrow_size, per_step, where_ref, weight_ref, *refs):
    xs, refs = refs[:count], refs[count:]
    before, refs = (refs[:3], refs[3:]) if narrow_size else ((), refs)
    flag_ref, ids_ref, *outs, held_ref = refs
    steps = weight_ref.shape[1] // (per_step * LANES)

    flag = jnp.zeros((1, LANES), f32)
    ids = []
    offset = 0
    for x in xs:
        rows = x.shape[0]
        held_ref[pl.ds(offset, rows), :] = x[...]
        last = x[pl.ds(rows - 16, 16), :LANES].astype(f32)[15:]
        flag = jnp.maximum(flag, last)
        turned = jnp.broadcast_to(last, (LANES, LANES)).T[:rows]
        keep = lax.broadcasted_iota(i32, (rows, LANES), 0) < rows - 1
        ids.append(jnp.where(keep, turned, 0.0))
        offset += rows
    ids = jnp.concatenate(ids, axis=0)
    lane = lax.broadcasted_iota(i32, (1, LANES), 1)
    flag = jnp.max(jnp.where(lane == LANES - 1, flag, 0.0)).astype(i32)

    total = jnp.zeros(ids.shape, f32)
    for c in range(steps):
        weights = weight_ref[:, c * per_step * LANES : (c + 1) * per_step * LANES]
        found = jnp.dot(held_ref[...], weights, preferred_element_type=f32)
        for j in range(per_step):
            name = c * per_step + j + 1.0
            total = jnp.where(ids == name, found[:, j * LANES : (j + 1) * LANES], total)

    if not narrow_size:
        flag_ref[0, 0] = flag
        ids_ref[...] = ids
        outs[0][...] = total
        return
    if before:
        flag = jnp.maximum(flag, before[0][0, 0])
        ids = jnp.concatenate([before[1][...], ids], axis=0)
        total = jnp.concatenate([before[2][...], total], axis=0)
    flag_ref[0, 0] = flag
    padding = jnp.zeros((ids_ref.shape[0] - ids.shape[0], LANES), f32)
    if padding.shape[0]:
        ids = jnp.concatenate([ids, padding], axis=0)
        total = jnp.concatenate([total, padding], axis=0)
    ids_ref[...] = ids
    half = total.shape[0] // 2
    rank = LANES // 2
    top, bottom = total[:half], total[half:]
    low = lax.broadcasted_iota(i32, (half, LANES), 1) < rank
    keys = jnp.where(low, top, pltpu.roll(bottom, rank, 1))
    values = jnp.where(low, pltpu.roll(top, rank, 1), bottom)
    for j in range(narrow_size):
        start = jnp.bitwise_xor(where_ref[1], j) * cols
        outs[j][...] = jnp.where(start >= KEY_VALUE_COLS, values, keys).astype(outs[j].dtype)


def down(where, blocks, weight, cols, before, narrow_size, scale):
    features, width = weight.shape
    new_rows = sum(b.shape[0] for b in blocks)
    per_step = min(4, width // LANES)
    whole = pl.BlockSpec(memory_space=VMEM)
    scalar = pl.BlockSpec(memory_space=pltpu.SMEM)
    if narrow_size:
        rows = -(-(new_rows + before[1].shape[0]) // 32) * 32
        sums = [((rows // 2, LANES), bf16 if j else f32) for j in range(narrow_size)]
    else:
        rows = new_rows
        sums = [((rows, LANES), f32)]
    return pl.pallas_call(
        functools.partial(down_kernel, len(blocks), cols, narrow_size, per_step),
        out_shape=[
            jax.ShapeDtypeStruct((1, 1), i32),
            jax.ShapeDtypeStruct((rows, LANES), f32),
        ]
        + [jax.ShapeDtypeStruct(*s) for s in sums],
        in_specs=[scalar, whole]
        + [whole for _ in blocks]
        + ([scalar, whole, whole] if narrow_size else []),
        out_specs=[scalar, whole] + [whole for _ in sums],
        scratch_shapes=[VMEM((new_rows, features), bf16)],
        compiler_params=params(18),
        cost_estimate=cost(
            2 * new_rows * features * width, 2 * features * (new_rows + width), scale
        ),
        name="down_maps",
    )(where, weight, *blocks, *(before if narrow_size else []))


def up_kernel(narrow_size, ids_ref, *refs):
    parts, weight_ref, outs = refs[:narrow_size], refs[narrow_size], refs[narrow_size + 1 :]
    total = parts[0][...]
    for part in parts[1:]:
        total = total + part[...].astype(f32)
    low_rank = total.astype(bf16).astype(f32)
    rank = LANES // 2
    turned = pltpu.roll(low_rank, rank, 1)
    low = lax.broadcasted_iota(i32, low_rank.shape, 1) < rank
    twice = jnp.concatenate(
        [jnp.where(low, low_rank, turned), jnp.where(low, turned, low_rank)], axis=0
    )
    ids = ids_ref[...]
    second = (lax.broadcasted_iota(i32, ids.shape, 1) >= rank).astype(f32)
    adapters = weight_ref.shape[0] // rank
    left = [
        jnp.where(ids - second == 2.0 * pair + 1.0, twice, 0.0).astype(bf16)
        for pair in range(adapters // 2)
    ]
    found = jnp.dot(jnp.concatenate(left, axis=1), weight_ref[...], preferred_element_type=f32)
    offset = 0
    for out in outs:
        rows = out.shape[0]
        out[...] = found[offset : offset + rows].astype(bf16)
        offset += rows


def up(ids, parts, weight, counts):
    cols = weight.shape[1]
    return pl.pallas_call(
        functools.partial(up_kernel, len(parts)),
        out_shape=[jax.ShapeDtypeStruct((c, cols), bf16) for c in counts],
        compiler_params=params(10),
        cost_estimate=cost(2 * sum(counts) * weight.size, 2 * weight.size + 2 * sum(counts) * (cols + 512)),
        name="up_maps",
    )(ids, *parts, weight)


def base_kernel(count, where_ref, *refs):
    acts, weight_ref, so_far, out_ref = refs[:count], refs[count], refs[count + 1 : -1], refs[-1]
    step = pl.program_id(0)
    for j in range(count):

        @pl.when(step == j)
        def _(j=j):
            found = jnp.dot(acts[j][...], weight_ref[...], preferred_element_type=f32)
            if j:
                found = out_ref[...] + found
            elif so_far:
                found = so_far[0][...] + found
            out_ref[...] = found


def base(where, acts, first, weight, so_far):
    rows, features = acts[0].shape
    cols = weight.shape[1]
    count = len(acts)
    given = [] if so_far is None else [so_far]
    return pl.pallas_call(
        functools.partial(base_kernel, count),
        grid_spec=pltpu.PrefetchScalarGridSpec(
            num_scalar_prefetch=1,
            grid=(count,),
            in_specs=[pl.BlockSpec((rows, features), lambda i, where: (0, 0)) for _ in acts]
            + [
                pl.BlockSpec(
                    (features, cols),
                    lambda i, where: (jnp.bitwise_xor(where[1], first + i), 0),
                )
            ]
            + [pl.BlockSpec((rows, cols), lambda i, where: (0, 0)) for _ in given],
            out_specs=pl.BlockSpec((rows, cols), lambda i, where: (0, 0)),
        ),
        out_shape=jax.ShapeDtypeStruct((rows, cols), f32),
        compiler_params=params(14),
        cost_estimate=cost(2 * rows * features * count * cols, 2 * features * count * (cols + rows)),
        name="shared_projection",
    )(where, *acts, in_hbm(weight), *given)


def join_kernel(base_ref, place_ref, *refs):
    corrections, out_ref, held_ref, sem = refs[:-3], *refs[-3:]
    stacked = jnp.concatenate([c[...] for c in corrections], axis=0)
    rows, count = base_ref.shape[0], stacked.shape[0]
    parts = sem.shape[0]
    copies = []
    for n in range(parts):
        part = pl.ds(n * (rows // parts), rows // parts)
        place = place_ref[part, :1].astype(i32)
        perm = lax.broadcasted_iota(i32, (rows // parts, count), 1) == place
        found = jnp.dot(perm.astype(f32).astype(bf16), stacked, preferred_element_type=f32)
        held_ref[part, :] = (base_ref[part, :] + found).astype(out_ref.dtype)
        copy = pltpu.make_async_copy(held_ref.at[part, :], out_ref.at[part, :], sem.at[n])
        copy.start()
        copies.append(copy)
    for copy in copies:
        copy.wait()


def join(base_out, place, corrections, dtype):
    rows, cols = base_out.shape
    count = sum(c.shape[0] for c in corrections)
    parts = 2
    return pl.pallas_call(
        join_kernel,
        out_shape=pltpu.HBM((rows, cols), dtype),
        in_specs=[pl.BlockSpec(memory_space=VMEM)] * (2 + len(corrections)),
        out_specs=pl.BlockSpec(memory_space=pltpu.HBM),
        scratch_shapes=[VMEM((rows, cols), dtype), pltpu.SemaphoreType.DMA((parts,))],
        compiler_params=params(10),
        cost_estimate=cost(2 * rows * cols * count, 2 * cols * (count + 3 * rows)),
        name="join_corrections",
    )(base_out, place, *corrections)


def raise_sums(ids, sums, up_weight, counts):
    sums = [swap(part, "narrow", j) if j else part for j, part in enumerate(sums)]
    return up(ids, sums, up_weight, counts)


def later_turn(turn, axes, total, done, tenant, slot, activations, down_weight, up_weight):
    wide_size, narrow_size = lax.axis_size("wide"), lax.axis_size("narrow")
    where = jnp.stack([*axes, turn])
    layout = [(k, end, LATER_ROWS) for k, end in enumerate(done)]
    _, place, *sent = pack(
        where,
        tenant,
        slot,
        activations,
        down_weight.shape[0],
        wide_size,
        layout,
        (0, wide_size),
        LATER_ROWS - 1,
    )
    got = [swap(b, "wide", k) if k else b for k, b in enumerate(sent)]
    cols = up_weight.shape[1]
    down_weight, up_weight = stage(down_weight, up_weight)
    before = down(where, got[:1], down_weight, cols, None, 0, 0.001)
    more, ids, *sums = down(where, got[1:], down_weight, cols, before, narrow_size, 0.001)
    outs = raise_sums(ids, sums, up_weight, [b.shape[0] for b in got])
    answers = [swap(b, "wide", k) if k else b for k, b in enumerate(outs)]
    return join(total, place, answers, f32), more[0, 0]


def on_device(
    activations,
    request_tenants,
    adapter_slot,
    shared_weight,
    adapter_down_weight,
    adapter_up_weight,
):
    rows = activations.shape[0]
    wide_size, narrow_size = lax.axis_size("wide"), lax.axis_size("narrow")
    local_count = adapter_down_weight.shape[0]
    axes = (lax.axis_index("wide").astype(i32), lax.axis_index("narrow").astype(i32))
    where = jnp.stack([*axes, jnp.int32(0)])
    tenant = request_tenants.reshape(1, rows)
    slot = adapter_slot.reshape(1, -1)
    up_weight = adapter_up_weight.reshape(-1, adapter_up_weight.shape[-1])

    cols = up_weight.shape[1]
    layout = first_turn(wide_size, local_count)
    own = len(layout) - 1
    routed = (local_count, wide_size, layout)
    begun, *sent = pack(where, tenant, slot, activations, *routed, (0, 1), 0)
    if own > 1:
        sent += pack(where, tenant, slot, after(activations, *sent), *routed, (1, own), 0)[1:]
    got = [swap(b, "wide", k) for (k, _, _), b in zip(layout, sent)]
    half = narrow_size // 2

    def step(work, *operands):
        def never(*operands):
            return jax.tree.map(
                lambda s: jnp.zeros(s.shape, s.dtype), jax.eval_shape(work, *operands)
            )

        return lax.cond(begun[0, 0] > 0, work, never, *operands)

    def spread(act):
        acts, bit = {0: act}, half // 2
        while bit:
            acts.update({j ^ bit: swap(x, "narrow", bit) for j, x in list(acts.items())})
            bit //= 2
        return [acts[j] for j in sorted(acts)]

    def pack_own(tenant, slot, activations):
        return pack(where, tenant, slot, activations, *routed, (own, own + 1), 0)[1:]

    def work_before(activations, shared_weight, maps):
        return base(where, spread(activations), 0, shared_weight, None), stage(*maps)

    def work_after(across, shared_weight, base_out):
        for n, act in enumerate(spread(across)):
            base_out = base(where, [act], half + n, shared_weight, base_out)
        return base_out

    shared_weight, maps = after_all((shared_weight, (adapter_down_weight, up_weight)), *sent)
    place, own_block = step(pack_own, tenant, slot, after(activations, *sent))
    across = swap(after(activations, own_block), "narrow", half) if half else None
    base_out, (down_beside, up_beside) = step(
        work_before, *after_all((activations, shared_weight, maps), own_block)
    )
    before = down(where, [got[0], after(own_block, base_out)], down_beside, cols, None, 0, 0.001)
    more, ids, *sums = down(
        where, after_all(got[1:], *before), down_beside, cols, before, narrow_size, 20
    )
    counts = [layout[n][2] for n in (0, own, *range(1, own))]
    outs = raise_sums(ids, sums, up_beside, counts)
    outs = [outs[0], *outs[2:], outs[1]]
    answers = [swap(b, "wide", k) if k else b for (k, _, _), b in zip(layout, outs)]
    if half:
        base_out = step(work_after, *after_all((across, shared_weight, base_out), *outs))
    more = more[0, 0]

    def done(base_out):
        return join(base_out, place, answers, bf16)

    def go_on(base_out):
        def turn_of(state):
            turn, _, total = state
            total, more = later_turn(
                turn, axes, total, ends(layout, wide_size), tenant, slot, activations, adapter_down_weight, up_weight
            )
            return turn + 1, more, total

        state = (jnp.int32(0), jnp.int32(1), join(base_out, place, answers, f32))
        return lax.while_loop(lambda s: s[1] > 0, turn_of, state)[2].astype(bf16)

    return lax.cond(more > 0, go_on, done, base_out)


def solution(mesh):
    in_specs = (
        P(("groups", "wide"), "narrow"),
        P(("groups", "wide"), None),
        P(),
        P(None, "narrow"),
        P("wide", "narrow", None),
        P("wide", None, "narrow"),
    )
    out_specs = P(("groups", "wide"), "narrow")
    return jax.shard_map(
        on_device, mesh=mesh, in_specs=in_specs, out_specs=out_specs, check_vma=False
    )
```

```python
import functools

import jax
import jax.numpy as jnp
from jax import lax
from jax.experimental import pallas as pl
from jax.experimental.pallas import tpu as pltpu
from jax.sharding import PartitionSpec as P

KEY_VALUE_COLS = 1024
LANES = 128
MOST = 16
OWN_ROWS = 112
NEAR_ROWS = 112
FAR_ROWS = 64
SHARED_ROWS = 48
LATER_ROWS = 32
VMEM = pltpu.VMEM
MIB = 1 << 20

f32, bf16, i32 = jnp.float32, jnp.bfloat16, jnp.int32


def first_turn(wide_size, local_count):
    most = -(-(local_count * MOST + 1) // 32) * 32
    plain = {k: min(FAR_ROWS if k > 1 else NEAR_ROWS if k else OWN_ROWS, most) for k in range(wide_size)}
    far = range(2, wide_size)
    shares = FAR_ROWS - 1 < local_count * MOST

    def rows_for(k):
        return [(k, True, SHARED_ROWS)] * shares * (k > 1) + [(k, False, plain[k])]

    leaving = [(k, True, SHARED_ROWS) for k in far[::2]] if shares else []
    leaving += [(k, False, plain[k]) for k in [*range(1, min(2, wide_size)), *far, 0]]
    early = [entry for k in [*far[:1], 0] for entry in rows_for(k)]
    rest = [entry for k in [*far[1:], *range(1, min(2, wide_size))] for entry in rows_for(k)]
    return leaving, early, rest


def swap(x, axis, k):
    size = lax.axis_size(axis)
    return lax.ppermute(x, axis, [(i, i ^ k) for i in range(size)])


def after(x, *others):
    return lax.optimization_barrier((x, *others))[0]


def after_all(xs, *others):
    return lax.optimization_barrier((xs, others))[0]


def cost(flops, bytes_accessed, scale=0.001):
    return pl.CostEstimate(
        flops=int(flops * scale), bytes_accessed=int(bytes_accessed * scale), transcendentals=0
    )


def params(mib):
    return pltpu.CompilerParams(vmem_limit_bytes=mib * MIB)


def in_hbm(x):
    return pltpu.with_memory_space_constraint(x, pltpu.HBM)


def pack_kernel(
    local_count, wide_size, turns, span, later, where_ref, tenant_ref, slot_ref, act_ref, *refs
):
    leaving, early, rest = turns
    layout = [(k, False, LATER_ROWS) for k in range(wide_size)] if later else leaving
    answers = layout if later else early + rest
    picked = range(*span)
    begun_ref, refs = refs[0], refs[1:]
    last_span = span[1] == len(layout)
    place_ref, refs = (refs[0], refs[1:]) if last_span else (None, refs)
    blocks = dict(zip(picked, refs[:-2]))
    act_held, in_sem = refs[-2:]
    rows, features = act_held.shape
    chunks = 4
    width = features // chunks
    loads = in_sem.shape[0]

    def load(n):
        part = pl.ds(n * (rows // loads), rows // loads)
        return pltpu.make_async_copy(act_ref.at[part, :], act_held.at[part, :], in_sem.at[n])

    for n in range(loads):
        load(n).start()
    begun_ref[0, 0] = jnp.int32(1)

    tenants = slot_ref.shape[1]
    tenant = tenant_ref[...]
    named = tenant == lax.broadcasted_iota(i32, (tenants, rows), 0)
    slots = jnp.broadcast_to(slot_ref[...].astype(f32), (8, tenants)).astype(bf16)
    slot = jnp.dot(slots, named.astype(f32).astype(bf16), preferred_element_type=f32)[:1]
    dest = jnp.floor((slot + 0.5) * (1.0 / local_count))
    adapter = slot - dest * local_count + 1.0
    leap = jnp.bitwise_xor(dest.astype(i32), where_ref[0])
    padded = max(8, wide_size)
    goes = (leap == lax.broadcasted_iota(i32, (padded, rows), 0)).astype(f32)
    earlier = lax.broadcasted_iota(i32, (rows, rows), 0) < lax.broadcasted_iota(
        i32, (rows, rows), 1
    )
    before = jnp.dot(
        goes.astype(bf16), earlier.astype(f32).astype(bf16), preferred_element_type=f32
    )
    position = jnp.sum(goes * before, axis=0, keepdims=True).astype(i32)
    held = {k: count - 1 for k, shared, count in leaving if not shared}
    end, extra = dict(held), {}
    for k, shared, count in leaving:
        if shared:
            named_k = jnp.sum(goes[k : k + 1], axis=1, keepdims=True).astype(i32)
            extra[k] = jnp.maximum(named_k - held[k], 0)
            end[k] = held[k] + count - 1
            end[k ^ 1] = held[k ^ 1] + count - 1 - jnp.minimum(extra[k], count - 1)
    offsets, offset = {}, 0
    for k, shared, count in answers:
        offsets[k, shared] = offset
        offset += count
    place = jnp.full((1, rows), -1, i32)
    more = jnp.zeros((1, rows), f32)
    here, adapters = [], []
    for k, shared, count in layout:
        numbers = adapter
        if later:
            mine = position - end[k] - where_ref[2] * (count - 1)
            mine = jnp.where(leap == k, mine, -1)
            more = jnp.where(mine >= count - 1, 1.0, more)
        elif shared:
            mine = jnp.where(leap == k, position - held[k], -1)
            other = jnp.where(position >= held[k ^ 1], position - held[k ^ 1] + extra[k], -1)
            mine = jnp.where(leap == k ^ 1, other, mine)
            numbers = adapter + jnp.where(leap == k ^ 1, 1.0 * local_count, 0.0)
        else:
            mine = jnp.where(leap == k, position, -1)
            more = jnp.where((leap == k) & (position >= end[k]), 1.0, more)
        mine = jnp.where((mine >= 0) & (mine < count - 1), mine, -1)
        for j in (k, k ^ 1) if shared else (k,):
            place = jnp.where((mine >= 0) & (leap == j), mine + offsets[j, shared], place)
        here.append(mine)
        adapters.append(jnp.broadcast_to(numbers, (8, rows)).astype(bf16))
    any_more = jnp.max(more, axis=1, keepdims=True)

    perm = jnp.concatenate(
        [
            (lax.broadcasted_iota(i32, (LANES, rows), 0) == here[n]).astype(f32).astype(bf16)
            for n in picked
        ],
        axis=0,
    )
    all_ids = [
        lax.dot_general(
            adapters[n],
            perm[m * LANES : (m + 1) * LANES],
            (((1,), (1,)), ((), ())),
            preferred_element_type=f32,
        )[:1]
        for m, n in enumerate(picked)
    ]
    lane = lax.broadcasted_iota(i32, (1, LANES), 1)
    for n in range(loads):
        load(n).wait()
    for c in range(chunks):
        cols = pl.ds(c * width, width)
        body = jnp.dot(perm, act_held[:, cols], preferred_element_type=f32)
        for m, n in enumerate(picked):
            count = layout[n][2]
            part = body[m * LANES : m * LANES + count]
            if c == 0:
                ids = jnp.where(lane == LANES - 1, any_more, all_ids[m])
                last = lax.broadcasted_iota(i32, (count, LANES), 0) == count - 1
                first = jnp.where(last, ids, part[:, :LANES])
                part = jnp.concatenate([first, part[:, LANES:]], axis=1)
            blocks[n][:, cols] = part.astype(bf16)
    if last_span:
        place_ref[...] = jnp.broadcast_to(place.astype(f32), (LANES, rows)).T


def pack(where, tenant, slot, activations, local_count, wide_size, turns, span, later):
    rows, features = activations.shape
    total = wide_size if later else len(turns[0])
    counts = [LATER_ROWS if later else turns[0][n][2] for n in range(*span)]
    places = [jax.ShapeDtypeStruct((rows, LANES), f32)] if span[1] == total else []
    loads = 4
    whole = pl.BlockSpec(memory_space=VMEM)
    scalar = pl.BlockSpec(memory_space=pltpu.SMEM)
    return pl.pallas_call(
        functools.partial(pack_kernel, local_count, wide_size, turns, span, later),
        out_shape=[
            jax.ShapeDtypeStruct((1, 1), i32),
            *places,
        ]
        + [pltpu.VMEM((c, features), bf16) for c in counts],
        in_specs=[scalar, whole, whole, pl.BlockSpec(memory_space=pltpu.HBM)],
        out_specs=[scalar] + [whole for _ in [*places, *counts]],
        scratch_shapes=[VMEM((rows, features), bf16), pltpu.SemaphoreType.DMA((loads,))],
        compiler_params=params(12),
        cost_estimate=cost(2 * sum(counts) * rows * features, 2 * features * (rows + sum(counts))),
        name="pack_rows",
    )(where, tenant, slot, in_hbm(activations))


def stage_kernel(down_ref, up_ref, down_out, up_out, sem):
    adapters, _, width = down_ref.shape
    copies = [
        pltpu.make_async_copy(
            down_ref.at[j], down_out.at[:, pl.ds(j * width, width)], sem.at[j]
        )
        for j in range(adapters)
    ]
    copies.append(pltpu.make_async_copy(up_ref, up_out, sem.at[adapters]))
    for copy in copies:
        copy.start()
    for copy in copies:
        copy.wait()


def stage(down_weight, up_weight):
    adapters, features, width = down_weight.shape
    whole = pl.BlockSpec(memory_space=VMEM)
    return pl.pallas_call(
        stage_kernel,
        out_shape=[
            pltpu.VMEM((features, adapters * width), down_weight.dtype),
            pltpu.VMEM(up_weight.shape, up_weight.dtype),
        ],
        in_specs=[pl.BlockSpec(memory_space=pltpu.HBM)] * 2,
        out_specs=[whole, whole],
        scratch_shapes=[pltpu.SemaphoreType.DMA((adapters + 1,))],
        compiler_params=params(12),
        cost_estimate=cost(10, 10),
        name="stage_maps",
    )(in_hbm(down_weight), in_hbm(up_weight))


def down_kernel(shifts, cols, narrow_size, per_step, where_ref, weight_ref, *refs):
    count = len(shifts)
    xs, refs = refs[:count], refs[count:]
    before, refs = (refs[:3], refs[3:]) if narrow_size else ((), refs)
    flag_ref, ids_ref, *outs, held_ref = refs
    steps = weight_ref.shape[1] // (per_step * LANES)

    flag = jnp.zeros((1, LANES), f32)
    ids = []
    offset = 0
    for x, shift in zip(xs, shifts):
        rows = x.shape[0]
        held_ref[pl.ds(offset, rows), :] = x[...]
        last = x[pl.ds(rows - 16, 16), :LANES].astype(f32)[15:]
        flag = jnp.maximum(flag, last)
        turned = jnp.broadcast_to(last, (LANES, LANES)).T[:rows]
        keep = lax.broadcasted_iota(i32, (rows, LANES), 0) < rows - 1
        ids.append(jnp.where(keep, turned - shift, 0.0))
        offset += rows
    ids = jnp.concatenate(ids, axis=0)
    lane = lax.broadcasted_iota(i32, (1, LANES), 1)
    flag = jnp.max(jnp.where(lane == LANES - 1, flag, 0.0)).astype(i32)

    total = jnp.zeros(ids.shape, f32)
    for c in range(steps):
        weights = weight_ref[:, c * per_step * LANES : (c + 1) * per_step * LANES]
        found = jnp.dot(held_ref[...], weights, preferred_element_type=f32)
        for j in range(per_step):
            name = c * per_step + j + 1.0
            total = jnp.where(ids == name, found[:, j * LANES : (j + 1) * LANES], total)

    if not narrow_size:
        flag_ref[0, 0] = flag
        ids_ref[...] = ids
        outs[0][...] = total
        return
    if before:
        flag = jnp.maximum(flag, before[0][0, 0])
        ids = jnp.concatenate([before[1][...], ids], axis=0)
        total = jnp.concatenate([before[2][...], total], axis=0)
    flag_ref[0, 0] = flag
    padding = jnp.zeros((ids_ref.shape[0] - ids.shape[0], LANES), f32)
    if padding.shape[0]:
        ids = jnp.concatenate([ids, padding], axis=0)
        total = jnp.concatenate([total, padding], axis=0)
    ids_ref[...] = ids
    half = total.shape[0] // 2
    rank = LANES // 2
    top, bottom = total[:half], total[half:]
    low = lax.broadcasted_iota(i32, (half, LANES), 1) < rank
    keys = jnp.where(low, top, pltpu.roll(bottom, rank, 1))
    values = jnp.where(low, pltpu.roll(top, rank, 1), bottom)
    for j in range(narrow_size):
        start = jnp.bitwise_xor(where_ref[1], j) * cols
        outs[j][...] = jnp.where(start >= KEY_VALUE_COLS, values, keys).astype(outs[j].dtype)


def down(where, blocks, shifts, weight, cols, before, narrow_size, scale):
    features, width = weight.shape
    new_rows = sum(b.shape[0] for b in blocks)
    per_step = min(4, width // LANES)
    whole = pl.BlockSpec(memory_space=VMEM)
    scalar = pl.BlockSpec(memory_space=pltpu.SMEM)
    if narrow_size:
        rows = -(-(new_rows + before[1].shape[0]) // 32) * 32
        sums = [((rows // 2, LANES), bf16 if j else f32) for j in range(narrow_size)]
    else:
        rows = new_rows
        sums = [((rows, LANES), f32)]
    return pl.pallas_call(
        functools.partial(down_kernel, shifts, cols, narrow_size, per_step),
        out_shape=[
            jax.ShapeDtypeStruct((1, 1), i32),
            jax.ShapeDtypeStruct((rows, LANES), f32),
        ]
        + [jax.ShapeDtypeStruct(*s) for s in sums],
        in_specs=[scalar, whole]
        + [whole for _ in blocks]
        + ([scalar, whole, whole] if narrow_size else []),
        out_specs=[scalar, whole] + [whole for _ in sums],
        scratch_shapes=[VMEM((new_rows, features), bf16)],
        compiler_params=params(18),
        cost_estimate=cost(
            2 * new_rows * features * width, 2 * features * (new_rows + width), scale
        ),
        name="down_maps",
    )(where, weight, *blocks, *(before if narrow_size else []))


def up_kernel(narrow_size, ids_ref, *refs):
    parts, weight_ref, outs = refs[:narrow_size], refs[narrow_size], refs[narrow_size + 1 :]
    total = parts[0][...]
    for part in parts[1:]:
        total = total + part[...].astype(f32)
    low_rank = total.astype(bf16).astype(f32)
    rank = LANES // 2
    turned = pltpu.roll(low_rank, rank, 1)
    low = lax.broadcasted_iota(i32, low_rank.shape, 1) < rank
    twice = jnp.concatenate(
        [jnp.where(low, low_rank, turned), jnp.where(low, turned, low_rank)], axis=0
    )
    ids = ids_ref[...]
    second = (lax.broadcasted_iota(i32, ids.shape, 1) >= rank).astype(f32)
    adapters = weight_ref.shape[0] // rank
    left = [
        jnp.where(ids - second == 2.0 * pair + 1.0, twice, 0.0).astype(bf16)
        for pair in range(adapters // 2)
    ]
    found = jnp.dot(jnp.concatenate(left, axis=1), weight_ref[...], preferred_element_type=f32)
    offset = 0
    for out in outs:
        rows = out.shape[0]
        out[...] = found[offset : offset + rows].astype(bf16)
        offset += rows


def up(ids, parts, weight, counts):
    cols = weight.shape[1]
    return pl.pallas_call(
        functools.partial(up_kernel, len(parts)),
        out_shape=[jax.ShapeDtypeStruct((c, cols), bf16) for c in counts],
        compiler_params=params(10),
        cost_estimate=cost(2 * sum(counts) * weight.size, 2 * weight.size + 2 * sum(counts) * (cols + 512)),
        name="up_maps",
    )(ids, *parts, weight)


def base_kernel(count, where_ref, *refs):
    acts, weight_ref, so_far, out_ref = refs[:count], refs[count], refs[count + 1 : -1], refs[-1]
    step = pl.program_id(0)
    for j in range(count):

        @pl.when(step == j)
        def _(j=j):
            found = jnp.dot(acts[j][...], weight_ref[...], preferred_element_type=f32)
            if j:
                found = out_ref[...] + found
            elif so_far:
                found = so_far[0][...] + found
            out_ref[...] = found


def base(where, acts, first, weight, so_far):
    rows, features = acts[0].shape
    cols = weight.shape[1]
    count = len(acts)
    given = [] if so_far is None else [so_far]
    return pl.pallas_call(
        functools.partial(base_kernel, count),
        grid_spec=pltpu.PrefetchScalarGridSpec(
            num_scalar_prefetch=1,
            grid=(count,),
            in_specs=[pl.BlockSpec((rows, features), lambda i, where: (0, 0)) for _ in acts]
            + [
                pl.BlockSpec(
                    (features, cols),
                    lambda i, where: (jnp.bitwise_xor(where[1], first + i), 0),
                )
            ]
            + [pl.BlockSpec((rows, cols), lambda i, where: (0, 0)) for _ in given],
            out_specs=pl.BlockSpec((rows, cols), lambda i, where: (0, 0)),
        ),
        out_shape=jax.ShapeDtypeStruct((rows, cols), f32),
        compiler_params=params(14),
        cost_estimate=cost(2 * rows * features * count * cols, 2 * features * count * (cols + rows)),
        name="shared_projection",
    )(where, *acts, in_hbm(weight), *given)


def join_kernel(base_ref, place_ref, *refs):
    corrections, out_ref, held_ref, sem = refs[:-3], *refs[-3:]
    stacked = jnp.concatenate([c[...] for c in corrections], axis=0)
    rows, count = base_ref.shape[0], stacked.shape[0]
    parts = sem.shape[0]
    copies = []
    for n in range(parts):
        part = pl.ds(n * (rows // parts), rows // parts)
        place = place_ref[part, :1].astype(i32)
        perm = lax.broadcasted_iota(i32, (rows // parts, count), 1) == place
        found = jnp.dot(perm.astype(f32).astype(bf16), stacked, preferred_element_type=f32)
        held_ref[part, :] = (base_ref[part, :] + found).astype(out_ref.dtype)
        copy = pltpu.make_async_copy(held_ref.at[part, :], out_ref.at[part, :], sem.at[n])
        copy.start()
        copies.append(copy)
    for copy in copies:
        copy.wait()


def join(base_out, place, corrections, dtype):
    rows, cols = base_out.shape
    count = sum(c.shape[0] for c in corrections)
    parts = 2
    return pl.pallas_call(
        join_kernel,
        out_shape=pltpu.HBM((rows, cols), dtype),
        in_specs=[pl.BlockSpec(memory_space=VMEM)] * (2 + len(corrections)),
        out_specs=pl.BlockSpec(memory_space=pltpu.HBM),
        scratch_shapes=[VMEM((rows, cols), dtype), pltpu.SemaphoreType.DMA((parts,))],
        compiler_params=params(10),
        cost_estimate=cost(2 * rows * cols * count, 2 * cols * (count + 3 * rows)),
        name="join_corrections",
    )(base_out, place, *corrections)


def raise_sums(ids, sums, up_weight, counts):
    sums = [swap(part, "narrow", j) if j else part for j, part in enumerate(sums)]
    return up(ids, sums, up_weight, counts)


def later_turn(turn, axes, total, turns, tenant, slot, activations, down_weight, up_weight):
    wide_size, narrow_size = lax.axis_size("wide"), lax.axis_size("narrow")
    where = jnp.stack([*axes, turn])
    _, place, *sent = pack(
        where,
        tenant,
        slot,
        activations,
        down_weight.shape[0],
        wide_size,
        turns,
        (0, wide_size),
        True,
    )
    got = [swap(b, "wide", k) if k else b for k, b in enumerate(sent)]
    cols = up_weight.shape[1]
    down_weight, up_weight = stage(down_weight, up_weight)
    shifts = [0] * wide_size
    before = down(where, got[:1], shifts[:1], down_weight, cols, None, 0, 0.001)
    more, ids, *sums = down(
        where, got[1:], shifts[1:], down_weight, cols, before, narrow_size, 0.001
    )
    outs = raise_sums(ids, sums, up_weight, [b.shape[0] for b in got])
    answers = [swap(b, "wide", k) if k else b for k, b in enumerate(outs)]
    return join(total, place, answers, f32), more[0, 0]


def on_device(
    activations,
    request_tenants,
    adapter_slot,
    shared_weight,
    adapter_down_weight,
    adapter_up_weight,
):
    rows = activations.shape[0]
    wide_size, narrow_size = lax.axis_size("wide"), lax.axis_size("narrow")
    local_count = adapter_down_weight.shape[0]
    axes = (lax.axis_index("wide").astype(i32), lax.axis_index("narrow").astype(i32))
    where = jnp.stack([*axes, jnp.int32(0)])
    tenant = request_tenants.reshape(1, rows)
    slot = adapter_slot.reshape(1, -1)
    up_weight = adapter_up_weight.reshape(-1, adapter_up_weight.shape[-1])

    cols = up_weight.shape[1]
    turns = first_turn(wide_size, local_count)
    leaving, early, rest = turns
    own = len(leaving) - 1
    routed = (local_count, wide_size, turns)
    ahead = min(own, 1 + sum(shared for _, shared, _ in leaving))
    begun, *sent = pack(where, tenant, slot, activations, *routed, (0, ahead), False)
    half = narrow_size // 2

    def step(work, *operands):
        def never(*operands):
            return jax.tree.map(
                lambda s: jnp.zeros(s.shape, s.dtype), jax.eval_shape(work, *operands)
            )

        return lax.cond(begun[0, 0] > 0, work, never, *operands)

    def spread(act):
        acts, bit = {0: act}, half // 2
        while bit:
            acts.update({j ^ bit: swap(x, "narrow", bit) for j, x in list(acts.items())})
            bit //= 2
        return [acts[j] for j in sorted(acts)]

    def pack_away(tenant, slot, activations):
        blocks = pack(where, tenant, slot, activations, *routed, (ahead, own), False)[1:]
        return blocks, spread(activations)[1:]

    def pack_own(tenant, slot, activations):
        return pack(where, tenant, slot, activations, *routed, (own, own + 1), False)[1:]

    def work_before(acts, shared_weight, maps):
        return base(where, acts, 0, shared_weight, None), stage(*maps)

    def work_after(across, shared_weight, base_out):
        for n, act in enumerate(spread(across)):
            base_out = base(where, [act], half + n, shared_weight, base_out)
        return base_out

    if own == ahead:
        acts = spread(activations)[1:]
    else:
        away, acts = step(pack_away, tenant, slot, after(activations, *sent))
        sent += away
    acts = [activations, *acts]
    got = {}
    for (k, shared, _), block in zip(leaving, sent):
        got[k, shared] = swap(block, "wide", k)
    shared_weight, maps = after_all((shared_weight, (adapter_down_weight, up_weight)), *sent)
    place, own_block = step(pack_own, tenant, slot, after(activations, *sent))
    got[0, False] = own_block
    across = swap(after(activations, own_block), "narrow", half) if half else None
    for k, shared, _ in leaving:
        if shared:
            got[k ^ 1, True] = swap(got[k, True], "wide", 1)
    base_out, (down_beside, up_beside) = step(
        work_before, *after_all((acts, shared_weight, maps), own_block)
    )

    def blocks_of(entries):
        shifts = [local_count if shared and k % 2 else 0 for k, shared, _ in entries]
        return [got[k, shared] for k, shared, _ in entries], shifts

    blocks, shifts = blocks_of(early)
    blocks[-1] = after(blocks[-1], base_out)
    before = down(where, blocks, shifts, down_beside, cols, None, 0, 0.001)
    blocks, shifts = blocks_of(rest)
    more, ids, *sums = down(
        where, after_all(blocks, *before), shifts, down_beside, cols, before, narrow_size, 20
    )
    counts = {}
    for k, _, count in early + rest:
        counts[k] = counts.get(k, 0) + count
    outs = raise_sums(ids, sums, up_beside, list(counts.values()))
    answers = [swap(b, "wide", k) if k else b for k, b in zip(counts, outs)]
    if half:
        base_out = step(work_after, *after_all((across, shared_weight, base_out), *outs))
    more = more[0, 0]

    def done(base_out):
        return join(base_out, place, answers, bf16)

    def go_on(base_out):
        def turn_of(state):
            turn, _, total = state
            total, more = later_turn(
                turn, axes, total, turns, tenant, slot, activations, adapter_down_weight, up_weight
            )
            return turn + 1, more, total

        state = (jnp.int32(0), jnp.int32(1), join(base_out, place, answers, f32))
        return lax.while_loop(lambda s: s[1] > 0, turn_of, state)[2].astype(bf16)

    return lax.cond(more > 0, go_on, done, base_out)


def solution(mesh):
    in_specs = (
        P(("groups", "wide"), "narrow"),
        P(("groups", "wide"), None),
        P(),
        P(None, "narrow"),
        P("wide", "narrow", None),
        P("wide", None, "narrow"),
    )
    out_specs = P(("groups", "wide"), "narrow")
    return jax.shard_map(
        on_device, mesh=mesh, in_specs=in_specs, out_specs=out_specs, check_vma=False
    )
```

```python
import functools

import jax
import jax.numpy as jnp
from jax import lax
from jax.experimental import pallas as pl
from jax.experimental.pallas import tpu as pltpu
from jax.sharding import PartitionSpec as P

KEY_VALUE_COLS = 1024
LANES = 128
MOST = 16
OWN_ROWS = 112
NEAR_ROWS = 112
FAR_ROWS = 64
SHARED_ROWS = 48
LATER_ROWS = 32
VMEM = pltpu.VMEM
MIB = 1 << 20

f32, bf16, i32 = jnp.float32, jnp.bfloat16, jnp.int32


def first_turn(wide_size, local_count):
    most = -(-(local_count * MOST + 1) // 32) * 32
    plain = {k: min(FAR_ROWS if k > 1 else NEAR_ROWS if k else OWN_ROWS, most) for k in range(wide_size)}
    far = range(2, wide_size)
    shares = FAR_ROWS - 1 < local_count * MOST

    def rows_for(k):
        return [(k, True, SHARED_ROWS)] * shares * (k > 1) + [(k, False, plain[k])]

    leaving = [(k, True, SHARED_ROWS) for k in far[::2]] if shares else []
    leaving += [(k, False, plain[k]) for k in [*range(1, min(2, wide_size)), *far, 0]]
    early = [entry for k in [*far[:1], 0] for entry in rows_for(k)]
    rest = [entry for k in [*far[1:], *range(1, min(2, wide_size))] for entry in rows_for(k)]
    return leaving, early, rest


def swap(x, axis, k):
    size = lax.axis_size(axis)
    return lax.ppermute(x, axis, [(i, i ^ k) for i in range(size)])


def after(x, *others):
    return lax.optimization_barrier((x, *others))[0]


def after_all(xs, *others):
    return lax.optimization_barrier((xs, others))[0]


def cost(flops, bytes_accessed, scale=0.001):
    return pl.CostEstimate(
        flops=int(flops * scale), bytes_accessed=int(bytes_accessed * scale), transcendentals=0
    )


def params(mib):
    return pltpu.CompilerParams(vmem_limit_bytes=mib * MIB)


def in_hbm(x):
    return pltpu.with_memory_space_constraint(x, pltpu.HBM)


def pack_kernel(
    local_count, wide_size, turns, span, later, where_ref, tenant_ref, slot_ref, act_ref, *refs
):
    leaving, early, rest = turns
    layout = [(k, False, LATER_ROWS) for k in range(wide_size)] if later else leaving
    answers = layout if later else early + rest
    picked = range(*span)
    begun_ref, refs = refs[0], refs[1:]
    last_span = span[1] == len(layout)
    place_ref, refs = (refs[0], refs[1:]) if last_span else (None, refs)
    blocks = dict(zip(picked, refs[:-2]))
    act_held, in_sem = refs[-2:]
    rows, features = act_held.shape
    chunks = 4
    width = features // chunks
    loads = in_sem.shape[0]

    def load(n):
        part = pl.ds(n * (rows // loads), rows // loads)
        return pltpu.make_async_copy(act_ref.at[part, :], act_held.at[part, :], in_sem.at[n])

    for n in range(loads):
        load(n).start()
    begun_ref[0, 0] = jnp.int32(1)

    tenants = slot_ref.shape[1]
    tenant = tenant_ref[...]
    named = tenant == lax.broadcasted_iota(i32, (tenants, rows), 0)
    slots = jnp.broadcast_to(slot_ref[...].astype(f32), (8, tenants)).astype(bf16)
    slot = jnp.dot(slots, named.astype(f32).astype(bf16), preferred_element_type=f32)[:1]
    dest = jnp.floor((slot + 0.5) * (1.0 / local_count))
    adapter = slot - dest * local_count + 1.0
    leap = jnp.bitwise_xor(dest.astype(i32), where_ref[0])
    padded = max(8, wide_size)
    goes = (leap == lax.broadcasted_iota(i32, (padded, rows), 0)).astype(f32)
    earlier = lax.broadcasted_iota(i32, (rows, rows), 0) < lax.broadcasted_iota(
        i32, (rows, rows), 1
    )
    before = jnp.dot(
        goes.astype(bf16), earlier.astype(f32).astype(bf16), preferred_element_type=f32
    )
    position = jnp.sum(goes * before, axis=0, keepdims=True).astype(i32)
    held = {k: count - 1 for k, shared, count in leaving if not shared}
    end, extra = dict(held), {}
    for k, shared, count in leaving:
        if shared:
            named_k = jnp.sum(goes[k : k + 1], axis=1, keepdims=True).astype(i32)
            extra[k] = jnp.maximum(named_k - held[k], 0)
            end[k] = held[k] + count - 1
            end[k ^ 1] = held[k ^ 1] + count - 1 - jnp.minimum(extra[k], count - 1)
    offsets, offset = {}, 0
    for k, shared, count in answers:
        offsets[k, shared] = offset
        offset += count
    place = jnp.full((1, rows), -1, i32)
    more = jnp.zeros((1, rows), f32)
    here, adapters = [], []
    for k, shared, count in layout:
        numbers = adapter
        if later:
            mine = position - end[k] - where_ref[2] * (count - 1)
            mine = jnp.where(leap == k, mine, -1)
            more = jnp.where(mine >= count - 1, 1.0, more)
        elif shared:
            mine = jnp.where(leap == k, position - held[k], -1)
            other = jnp.where(position >= held[k ^ 1], position - held[k ^ 1] + extra[k], -1)
            mine = jnp.where(leap == k ^ 1, other, mine)
            numbers = adapter + jnp.where(leap == k ^ 1, 1.0 * local_count, 0.0)
        else:
            mine = jnp.where(leap == k, position, -1)
            more = jnp.where((leap == k) & (position >= end[k]), 1.0, more)
        mine = jnp.where((mine >= 0) & (mine < count - 1), mine, -1)
        for j in (k, k ^ 1) if shared else (k,):
            place = jnp.where((mine >= 0) & (leap == j), mine + offsets[j, shared], place)
        here.append(mine)
        adapters.append(jnp.broadcast_to(numbers, (8, rows)).astype(bf16))
    any_more = jnp.max(more, axis=1, keepdims=True)

    perm = jnp.concatenate(
        [
            (lax.broadcasted_iota(i32, (LANES, rows), 0) == here[n]).astype(f32).astype(bf16)
            for n in picked
        ],
        axis=0,
    )
    all_ids = [
        lax.dot_general(
            adapters[n],
            perm[m * LANES : (m + 1) * LANES],
            (((1,), (1,)), ((), ())),
            preferred_element_type=f32,
        )[:1]
        for m, n in enumerate(picked)
    ]
    lane = lax.broadcasted_iota(i32, (1, LANES), 1)
    for n in range(loads):
        load(n).wait()
    for c in range(chunks):
        cols = pl.ds(c * width, width)
        body = jnp.dot(perm, act_held[:, cols], preferred_element_type=f32)
        for m, n in enumerate(picked):
            count = layout[n][2]
            part = body[m * LANES : m * LANES + count]
            if c == 0:
                ids = jnp.where(lane == LANES - 1, any_more, all_ids[m])
                last = lax.broadcasted_iota(i32, (count, LANES), 0) == count - 1
                first = jnp.where(last, ids, part[:, :LANES])
                part = jnp.concatenate([first, part[:, LANES:]], axis=1)
            blocks[n][:, cols] = part.astype(bf16)
    if last_span:
        place_ref[...] = jnp.broadcast_to(place.astype(f32), (LANES, rows)).T


def pack(where, tenant, slot, activations, local_count, wide_size, turns, span, later):
    rows, features = activations.shape
    total = wide_size if later else len(turns[0])
    counts = [LATER_ROWS if later else turns[0][n][2] for n in range(*span)]
    places = [jax.ShapeDtypeStruct((rows, LANES), f32)] if span[1] == total else []
    loads = 4
    whole = pl.BlockSpec(memory_space=VMEM)
    scalar = pl.BlockSpec(memory_space=pltpu.SMEM)
    return pl.pallas_call(
        functools.partial(pack_kernel, local_count, wide_size, turns, span, later),
        out_shape=[
            jax.ShapeDtypeStruct((1, 1), i32),
            *places,
        ]
        + [pltpu.VMEM((c, features), bf16) for c in counts],
        in_specs=[scalar, whole, whole, pl.BlockSpec(memory_space=pltpu.HBM)],
        out_specs=[scalar] + [whole for _ in [*places, *counts]],
        scratch_shapes=[VMEM((rows, features), bf16), pltpu.SemaphoreType.DMA((loads,))],
        compiler_params=params(12),
        cost_estimate=cost(2 * sum(counts) * rows * features, 2 * features * (rows + sum(counts))),
        name="pack_rows",
    )(where, tenant, slot, in_hbm(activations))


def stage_kernel(down_ref, up_ref, down_out, up_out, sem):
    adapters, _, width = down_ref.shape
    copies = [
        pltpu.make_async_copy(
            down_ref.at[j], down_out.at[:, pl.ds(j * width, width)], sem.at[j]
        )
        for j in range(adapters)
    ]
    copies.append(pltpu.make_async_copy(up_ref, up_out, sem.at[adapters]))
    for copy in copies:
        copy.start()
    for copy in copies:
        copy.wait()


def stage(down_weight, up_weight):
    adapters, features, width = down_weight.shape
    whole = pl.BlockSpec(memory_space=VMEM)
    return pl.pallas_call(
        stage_kernel,
        out_shape=[
            pltpu.VMEM((features, adapters * width), down_weight.dtype),
            pltpu.VMEM(up_weight.shape, up_weight.dtype),
        ],
        in_specs=[pl.BlockSpec(memory_space=pltpu.HBM)] * 2,
        out_specs=[whole, whole],
        scratch_shapes=[pltpu.SemaphoreType.DMA((adapters + 1,))],
        compiler_params=params(12),
        cost_estimate=cost(10, 10),
        name="stage_maps",
    )(in_hbm(down_weight), in_hbm(up_weight))


def down_kernel(shifts, cols, narrow_size, per_step, where_ref, weight_ref, *refs):
    count = len(shifts)
    xs, refs = refs[:count], refs[count:]
    before, refs = (refs[:3], refs[3:]) if narrow_size else ((), refs)
    flag_ref, ids_ref, *outs, held_ref = refs
    steps = weight_ref.shape[1] // (per_step * LANES)

    flag = jnp.zeros((1, LANES), f32)
    ids = []
    offset = 0
    for x, shift in zip(xs, shifts):
        rows = x.shape[0]
        held_ref[pl.ds(offset, rows), :] = x[...]
        last = x[pl.ds(rows - 16, 16), :LANES].astype(f32)[15:]
        flag = jnp.maximum(flag, last)
        turned = jnp.broadcast_to(last, (LANES, LANES)).T[:rows]
        keep = lax.broadcasted_iota(i32, (rows, LANES), 0) < rows - 1
        ids.append(jnp.where(keep, turned - shift, 0.0))
        offset += rows
    ids = jnp.concatenate(ids, axis=0)
    lane = lax.broadcasted_iota(i32, (1, LANES), 1)
    flag = jnp.max(jnp.where(lane == LANES - 1, flag, 0.0)).astype(i32)

    total = jnp.zeros(ids.shape, f32)
    for c in range(steps):
        weights = weight_ref[:, c * per_step * LANES : (c + 1) * per_step * LANES]
        found = jnp.dot(held_ref[...], weights, preferred_element_type=f32)
        for j in range(per_step):
            name = c * per_step + j + 1.0
            total = jnp.where(ids == name, found[:, j * LANES : (j + 1) * LANES], total)

    if not narrow_size:
        flag_ref[0, 0] = flag
        ids_ref[...] = ids
        outs[0][...] = total
        return
    if before:
        flag = jnp.maximum(flag, before[0][0, 0])
        ids = jnp.concatenate([before[1][...], ids], axis=0)
        total = jnp.concatenate([before[2][...], total], axis=0)
    flag_ref[0, 0] = flag
    padding = jnp.zeros((ids_ref.shape[0] - ids.shape[0], LANES), f32)
    if padding.shape[0]:
        ids = jnp.concatenate([ids, padding], axis=0)
        total = jnp.concatenate([total, padding], axis=0)
    ids_ref[...] = ids
    half = total.shape[0] // 2
    rank = LANES // 2
    top, bottom = total[:half], total[half:]
    low = lax.broadcasted_iota(i32, (half, LANES), 1) < rank
    keys = jnp.where(low, top, pltpu.roll(bottom, rank, 1))
    values = jnp.where(low, pltpu.roll(top, rank, 1), bottom)
    for j in range(narrow_size):
        start = jnp.bitwise_xor(where_ref[1], j) * cols
        outs[j][...] = jnp.where(start >= KEY_VALUE_COLS, values, keys).astype(outs[j].dtype)


def down(where, blocks, shifts, weight, cols, before, narrow_size, scale):
    features, width = weight.shape
    new_rows = sum(b.shape[0] for b in blocks)
    per_step = min(4, width // LANES)
    whole = pl.BlockSpec(memory_space=VMEM)
    scalar = pl.BlockSpec(memory_space=pltpu.SMEM)
    if narrow_size:
        rows = -(-(new_rows + before[1].shape[0]) // 32) * 32
        sums = [((rows // 2, LANES), bf16 if j else f32) for j in range(narrow_size)]
    else:
        rows = new_rows
        sums = [((rows, LANES), f32)]
    return pl.pallas_call(
        functools.partial(down_kernel, shifts, cols, narrow_size, per_step),
        out_shape=[
            jax.ShapeDtypeStruct((1, 1), i32),
            jax.ShapeDtypeStruct((rows, LANES), f32),
        ]
        + [jax.ShapeDtypeStruct(*s) for s in sums],
        in_specs=[scalar, whole]
        + [whole for _ in blocks]
        + ([scalar, whole, whole] if narrow_size else []),
        out_specs=[scalar, whole] + [whole for _ in sums],
        scratch_shapes=[VMEM((new_rows, features), bf16)],
        compiler_params=params(18),
        cost_estimate=cost(
            2 * new_rows * features * width, 2 * features * (new_rows + width), scale
        ),
        name="down_maps",
    )(where, weight, *blocks, *(before if narrow_size else []))


def up_kernel(narrow_size, ids_ref, *refs):
    parts, weight_ref, outs = refs[:narrow_size], refs[narrow_size], refs[narrow_size + 1 :]
    total = parts[0][...]
    for part in parts[1:]:
        total = total + part[...].astype(f32)
    low_rank = total.astype(bf16).astype(f32)
    rank = LANES // 2
    turned = pltpu.roll(low_rank, rank, 1)
    low = lax.broadcasted_iota(i32, low_rank.shape, 1) < rank
    twice = jnp.concatenate(
        [jnp.where(low, low_rank, turned), jnp.where(low, turned, low_rank)], axis=0
    )
    ids = ids_ref[...]
    second = (lax.broadcasted_iota(i32, ids.shape, 1) >= rank).astype(f32)
    adapters = weight_ref.shape[0] // rank
    left = [
        jnp.where(ids - second == 2.0 * pair + 1.0, twice, 0.0).astype(bf16)
        for pair in range(adapters // 2)
    ]
    found = jnp.dot(jnp.concatenate(left, axis=1), weight_ref[...], preferred_element_type=f32)
    offset = 0
    for out in outs:
        rows = out.shape[0]
        out[...] = found[offset : offset + rows].astype(bf16)
        offset += rows


def up(ids, parts, weight, counts):
    cols = weight.shape[1]
    return pl.pallas_call(
        functools.partial(up_kernel, len(parts)),
        out_shape=[jax.ShapeDtypeStruct((c, cols), bf16) for c in counts],
        compiler_params=params(10),
        cost_estimate=cost(2 * sum(counts) * weight.size, 2 * weight.size + 2 * sum(counts) * (cols + 512)),
        name="up_maps",
    )(ids, *parts, weight)


def base_kernel(count, where_ref, *refs):
    acts, weight_ref, so_far, out_ref = refs[:count], refs[count], refs[count + 1 : -1], refs[-1]
    step = pl.program_id(0)
    for j in range(count):

        @pl.when(step == j)
        def _(j=j):
            found = jnp.dot(acts[j][...], weight_ref[...], preferred_element_type=f32)
            if j:
                found = out_ref[...] + found
            elif so_far:
                found = so_far[0][...] + found
            out_ref[...] = found


def base(where, acts, first, weight, so_far):
    rows, features = acts[0].shape
    cols = weight.shape[1]
    count = len(acts)
    given = [] if so_far is None else [so_far]
    return pl.pallas_call(
        functools.partial(base_kernel, count),
        grid_spec=pltpu.PrefetchScalarGridSpec(
            num_scalar_prefetch=1,
            grid=(count,),
            in_specs=[pl.BlockSpec((rows, features), lambda i, where: (0, 0)) for _ in acts]
            + [
                pl.BlockSpec(
                    (features, cols),
                    lambda i, where: (jnp.bitwise_xor(where[1], first + i), 0),
                )
            ]
            + [pl.BlockSpec((rows, cols), lambda i, where: (0, 0)) for _ in given],
            out_specs=pl.BlockSpec((rows, cols), lambda i, where: (0, 0)),
        ),
        out_shape=jax.ShapeDtypeStruct((rows, cols), f32),
        compiler_params=params(14),
        cost_estimate=cost(2 * rows * features * count * cols, 2 * features * count * (cols + rows)),
        name="shared_projection",
    )(where, *acts, in_hbm(weight), *given)


def join_kernel(base_ref, place_ref, *refs):
    corrections, out_ref, held_ref, sem = refs[:-3], *refs[-3:]
    stacked = jnp.concatenate([c[...] for c in corrections], axis=0)
    rows, count = base_ref.shape[0], stacked.shape[0]
    parts = sem.shape[0]
    copies = []
    for n in range(parts):
        part = pl.ds(n * (rows // parts), rows // parts)
        place = place_ref[part, :1].astype(i32)
        perm = lax.broadcasted_iota(i32, (rows // parts, count), 1) == place
        found = jnp.dot(perm.astype(f32).astype(bf16), stacked, preferred_element_type=f32)
        held_ref[part, :] = (base_ref[part, :] + found).astype(out_ref.dtype)
        copy = pltpu.make_async_copy(held_ref.at[part, :], out_ref.at[part, :], sem.at[n])
        copy.start()
        copies.append(copy)
    for copy in copies:
        copy.wait()


def join(base_out, place, corrections, dtype):
    rows, cols = base_out.shape
    count = sum(c.shape[0] for c in corrections)
    parts = 2
    return pl.pallas_call(
        join_kernel,
        out_shape=pltpu.HBM((rows, cols), dtype),
        in_specs=[pl.BlockSpec(memory_space=VMEM)] * (2 + len(corrections)),
        out_specs=pl.BlockSpec(memory_space=pltpu.HBM),
        scratch_shapes=[VMEM((rows, cols), dtype), pltpu.SemaphoreType.DMA((parts,))],
        compiler_params=params(10),
        cost_estimate=cost(2 * rows * cols * count, 2 * cols * (count + 3 * rows)),
        name="join_corrections",
    )(base_out, place, *corrections)


def raise_sums(ids, sums, up_weight, counts):
    sums = [swap(part, "narrow", j) if j else part for j, part in enumerate(sums)]
    return up(ids, sums, up_weight, counts)


def later_turn(turn, axes, total, turns, tenant, slot, activations, down_weight, up_weight):
    wide_size, narrow_size = lax.axis_size("wide"), lax.axis_size("narrow")
    where = jnp.stack([*axes, turn])
    _, place, *sent = pack(
        where,
        tenant,
        slot,
        activations,
        down_weight.shape[0],
        wide_size,
        turns,
        (0, wide_size),
        True,
    )
    got = [swap(b, "wide", k) if k else b for k, b in enumerate(sent)]
    cols = up_weight.shape[1]
    down_weight, up_weight = stage(down_weight, up_weight)
    shifts = [0] * wide_size
    before = down(where, got[:1], shifts[:1], down_weight, cols, None, 0, 0.001)
    more, ids, *sums = down(
        where, got[1:], shifts[1:], down_weight, cols, before, narrow_size, 0.001
    )
    outs = raise_sums(ids, sums, up_weight, [b.shape[0] for b in got])
    answers = [swap(b, "wide", k) if k else b for k, b in enumerate(outs)]
    return join(total, place, answers, f32), more[0, 0]


def on_device(
    activations,
    request_tenants,
    adapter_slot,
    shared_weight,
    adapter_down_weight,
    adapter_up_weight,
):
    rows = activations.shape[0]
    wide_size, narrow_size = lax.axis_size("wide"), lax.axis_size("narrow")
    local_count = adapter_down_weight.shape[0]
    axes = (lax.axis_index("wide").astype(i32), lax.axis_index("narrow").astype(i32))
    where = jnp.stack([*axes, jnp.int32(0)])
    tenant = request_tenants.reshape(1, rows)
    slot = adapter_slot.reshape(1, -1)
    up_weight = adapter_up_weight.reshape(-1, adapter_up_weight.shape[-1])

    cols = up_weight.shape[1]
    turns = first_turn(wide_size, local_count)
    leaving, early, rest = turns
    own = len(leaving) - 1
    routed = (local_count, wide_size, turns)
    ahead = min(own, 1 + sum(shared for _, shared, _ in leaving))
    begun, *sent = pack(where, tenant, slot, activations, *routed, (0, ahead), False)
    half = narrow_size // 2

    def step(work, *operands):
        def never(*operands):
            return jax.tree.map(
                lambda s: jnp.zeros(s.shape, s.dtype), jax.eval_shape(work, *operands)
            )

        return lax.cond(begun[0, 0] > 0, work, never, *operands)

    def spread(act):
        acts, bit = {0: act}, half // 2
        while bit:
            acts.update({j ^ bit: swap(x, "narrow", bit) for j, x in list(acts.items())})
            bit //= 2
        return [acts[j] for j in sorted(acts)]

    def pack_away(tenant, slot, activations):
        blocks = pack(where, tenant, slot, activations, *routed, (ahead, own), False)[1:]
        return blocks, spread(activations)[1:]

    def pack_own(tenant, slot, activations):
        return pack(where, tenant, slot, activations, *routed, (own, own + 1), False)[1:]

    def work_before(acts, shared_weight, maps):
        return base(where, acts, 0, shared_weight, None), stage(*maps)

    def work_after(across, shared_weight, base_out):
        for n, act in enumerate(spread(across)):
            base_out = base(where, [act], half + n, shared_weight, base_out)
        return base_out

    if own == ahead:
        acts = spread(activations)[1:]
    else:
        away, acts = step(pack_away, tenant, slot, after(activations, *sent))
        sent += away
    acts = [activations, *acts]
    got = {}
    for (k, shared, _), block in zip(leaving, sent):
        got[k, shared] = swap(block, "wide", k)
    shared_weight, maps = after_all((shared_weight, (adapter_down_weight, up_weight)), *sent)
    place, own_block = step(pack_own, tenant, slot, after(activations, *sent))
    got[0, False] = own_block
    across = swap(after(activations, *sent[:ahead]), "narrow", half) if half else None
    base_out, (down_beside, up_beside) = step(
        work_before, *after_all((acts, shared_weight, maps), own_block)
    )

    for k, shared, _ in leaving:
        if shared:
            got[k ^ 1, True] = swap(after(got[k, True], base_out), "wide", 1)

    def blocks_of(entries):
        shifts = [local_count if shared and k % 2 else 0 for k, shared, _ in entries]
        return [got[k, shared] for k, shared, _ in entries], shifts

    blocks, shifts = blocks_of(early)
    blocks[-1] = after(blocks[-1], base_out)
    before = down(where, blocks, shifts, down_beside, cols, None, 0, 0.001)
    blocks, shifts = blocks_of(rest)
    more, ids, *sums = down(
        where, after_all(blocks, *before), shifts, down_beside, cols, before, narrow_size, 0.001
    )
    counts = {}
    for k, _, count in early + rest:
        counts[k] = counts.get(k, 0) + count
    outs = raise_sums(ids, sums, up_beside, list(counts.values()))
    answers = [swap(b, "wide", k) if k else b for k, b in zip(counts, outs)]
    if half:
        base_out = step(work_after, *after_all((across, shared_weight, base_out), *outs))
    more = more[0, 0]

    def done(base_out):
        return join(base_out, place, answers, bf16)

    def go_on(base_out):
        def turn_of(state):
            turn, _, total = state
            total, more = later_turn(
                turn, axes, total, turns, tenant, slot, activations, adapter_down_weight, up_weight
            )
            return turn + 1, more, total

        state = (jnp.int32(0), jnp.int32(1), join(base_out, place, answers, f32))
        return lax.while_loop(lambda s: s[1] > 0, turn_of, state)[2].astype(bf16)

    return lax.cond(more > 0, go_on, done, base_out)


def solution(mesh):
    in_specs = (
        P(("groups", "wide"), "narrow"),
        P(("groups", "wide"), None),
        P(),
        P(None, "narrow"),
        P("wide", "narrow", None),
        P("wide", None, "narrow"),
    )
    out_specs = P(("groups", "wide"), "narrow")
    return jax.shard_map(
        on_device, mesh=mesh, in_specs=in_specs, out_specs=out_specs, check_vma=False
    )
```

```python
import functools

import jax
import jax.numpy as jnp
from jax import lax
from jax.experimental import pallas as pl
from jax.experimental.pallas import tpu as pltpu
from jax.sharding import PartitionSpec as P

KEY_VALUE_COLS = 1024
LANES = 128
MOST = 16
OWN_ROWS = 112
NEAR_ROWS = 112
FAR_ROWS = 64
SHARED_ROWS = 48
LATER_ROWS = 32
VMEM = pltpu.VMEM
MIB = 1 << 20

f32, bf16, i32 = jnp.float32, jnp.bfloat16, jnp.int32


def first_turn(wide_size, local_count):
    most = -(-(local_count * MOST + 1) // 32) * 32
    plain = {k: min(FAR_ROWS if k > 1 else NEAR_ROWS if k else OWN_ROWS, most) for k in range(wide_size)}
    far = range(2, wide_size)
    shares = FAR_ROWS - 1 < local_count * MOST

    near = [(k, False, plain[k]) for k in range(min(2, wide_size))][::-1]
    direct = [(k, True, SHARED_ROWS) for k in far[::2]] if shares else []
    passed = [(k, True, SHARED_ROWS) for k in far[1::2]] if shares else []
    apart = [(k, False, plain[k]) for k in far]
    leaving = [*direct, *near[:-1], *apart, near[-1]]
    return leaving, [*direct, *near], [*apart, *passed]


def answer_order(early, rest):
    return sorted(early + rest, key=lambda entry: (-entry[0], entry[1]))


def swap(x, axis, k):
    size = lax.axis_size(axis)
    return lax.ppermute(x, axis, [(i, i ^ k) for i in range(size)])


def after(x, *others):
    return lax.optimization_barrier((x, *others))[0]


def after_all(xs, *others):
    return lax.optimization_barrier((xs, others))[0]


def cost(flops, bytes_accessed, scale=0.001):
    return pl.CostEstimate(
        flops=int(flops * scale), bytes_accessed=int(bytes_accessed * scale), transcendentals=0
    )


def params(mib):
    return pltpu.CompilerParams(vmem_limit_bytes=mib * MIB)


def in_hbm(x):
    return pltpu.with_memory_space_constraint(x, pltpu.HBM)


def pack_kernel(
    local_count, wide_size, turns, span, later, where_ref, tenant_ref, slot_ref, act_ref, *refs
):
    leaving, early, rest = turns
    layout = [(k, False, LATER_ROWS) for k in range(wide_size)] if later else leaving
    answers = layout if later else answer_order(early, rest)
    picked = range(*span)
    begun_ref, refs = refs[0], refs[1:]
    last_span = span[1] == len(layout)
    place_ref, refs = (refs[0], refs[1:]) if last_span else (None, refs)
    blocks = dict(zip(picked, refs[:-2]))
    act_held, in_sem = refs[-2:]
    rows, features = act_held.shape
    chunks = 4
    width = features // chunks
    loads = in_sem.shape[0]

    def load(n):
        part = pl.ds(n * (rows // loads), rows // loads)
        return pltpu.make_async_copy(act_ref.at[part, :], act_held.at[part, :], in_sem.at[n])

    for n in range(loads):
        load(n).start()
    begun_ref[0, 0] = jnp.int32(1)

    tenants = slot_ref.shape[1]
    tenant = tenant_ref[...]
    named = tenant == lax.broadcasted_iota(i32, (tenants, rows), 0)
    slots = jnp.broadcast_to(slot_ref[...].astype(f32), (8, tenants)).astype(bf16)
    slot = jnp.dot(slots, named.astype(f32).astype(bf16), preferred_element_type=f32)[:1]
    dest = jnp.floor((slot + 0.5) * (1.0 / local_count))
    adapter = slot - dest * local_count + 1.0
    leap = jnp.bitwise_xor(dest.astype(i32), where_ref[0])
    padded = max(8, wide_size)
    goes = (leap == lax.broadcasted_iota(i32, (padded, rows), 0)).astype(f32)
    earlier = lax.broadcasted_iota(i32, (rows, rows), 0) < lax.broadcasted_iota(
        i32, (rows, rows), 1
    )
    before = jnp.dot(
        goes.astype(bf16), earlier.astype(f32).astype(bf16), preferred_element_type=f32
    )
    position = jnp.sum(goes * before, axis=0, keepdims=True).astype(i32)
    held = {k: count - 1 for k, shared, count in leaving if not shared}
    end, extra = dict(held), {}
    for k, shared, count in leaving:
        if shared:
            named_k = jnp.sum(goes[k : k + 1], axis=1, keepdims=True).astype(i32)
            extra[k] = jnp.maximum(named_k - held[k], 0)
            end[k] = held[k] + count - 1
            end[k ^ 1] = held[k ^ 1] + count - 1 - jnp.minimum(extra[k], count - 1)
    offsets, offset = {}, 0
    for k, shared, count in answers:
        offsets[k, shared] = offset
        offset += count
    place = jnp.full((1, rows), -1, i32)
    more = jnp.zeros((1, rows), f32)
    here, adapters = [], []
    for k, shared, count in layout:
        numbers = adapter
        if later:
            mine = position - end[k] - where_ref[2] * (count - 1)
            mine = jnp.where(leap == k, mine, -1)
            more = jnp.where(mine >= count - 1, 1.0, more)
        elif shared:
            mine = jnp.where(leap == k, position - held[k], -1)
            other = jnp.where(position >= held[k ^ 1], position - held[k ^ 1] + extra[k], -1)
            mine = jnp.where(leap == k ^ 1, other, mine)
            numbers = adapter + jnp.where(leap == k ^ 1, 1.0 * local_count, 0.0)
        else:
            mine = jnp.where(leap == k, position, -1)
            more = jnp.where((leap == k) & (position >= end[k]), 1.0, more)
        mine = jnp.where((mine >= 0) & (mine < count - 1), mine, -1)
        for j in (k, k ^ 1) if shared else (k,):
            place = jnp.where((mine >= 0) & (leap == j), mine + offsets[j, shared], place)
        here.append(mine)
        adapters.append(jnp.broadcast_to(numbers, (8, rows)).astype(bf16))
    any_more = jnp.max(more, axis=1, keepdims=True)

    perm = jnp.concatenate(
        [
            (lax.broadcasted_iota(i32, (LANES, rows), 0) == here[n]).astype(f32).astype(bf16)
            for n in picked
        ],
        axis=0,
    )
    all_ids = [
        lax.dot_general(
            adapters[n],
            perm[m * LANES : (m + 1) * LANES],
            (((1,), (1,)), ((), ())),
            preferred_element_type=f32,
        )[:1]
        for m, n in enumerate(picked)
    ]
    lane = lax.broadcasted_iota(i32, (1, LANES), 1)
    for n in range(loads):
        load(n).wait()
    for c in range(chunks):
        cols = pl.ds(c * width, width)
        body = jnp.dot(perm, act_held[:, cols], preferred_element_type=f32)
        for m, n in enumerate(picked):
            count = layout[n][2]
            part = body[m * LANES : m * LANES + count]
            if c == 0:
                ids = jnp.where(lane == LANES - 1, any_more, all_ids[m])
                last = lax.broadcasted_iota(i32, (count, LANES), 0) == count - 1
                first = jnp.where(last, ids, part[:, :LANES])
                part = jnp.concatenate([first, part[:, LANES:]], axis=1)
            blocks[n][:, cols] = part.astype(bf16)
    if last_span:
        place_ref[...] = jnp.broadcast_to(place.astype(f32), (LANES, rows)).T


def pack(where, tenant, slot, activations, local_count, wide_size, turns, span, later):
    rows, features = activations.shape
    total = wide_size if later else len(turns[0])
    counts = [LATER_ROWS if later else turns[0][n][2] for n in range(*span)]
    places = [jax.ShapeDtypeStruct((rows, LANES), f32)] if span[1] == total else []
    loads = 4
    whole = pl.BlockSpec(memory_space=VMEM)
    scalar = pl.BlockSpec(memory_space=pltpu.SMEM)
    return pl.pallas_call(
        functools.partial(pack_kernel, local_count, wide_size, turns, span, later),
        out_shape=[
            jax.ShapeDtypeStruct((1, 1), i32),
            *places,
        ]
        + [pltpu.VMEM((c, features), bf16) for c in counts],
        in_specs=[scalar, whole, whole, pl.BlockSpec(memory_space=pltpu.HBM)],
        out_specs=[scalar] + [whole for _ in [*places, *counts]],
        scratch_shapes=[VMEM((rows, features), bf16), pltpu.SemaphoreType.DMA((loads,))],
        compiler_params=params(12),
        cost_estimate=cost(2 * sum(counts) * rows * features, 2 * features * (rows + sum(counts))),
        name="pack_rows",
    )(where, tenant, slot, in_hbm(activations))


def stage_kernel(down_ref, up_ref, down_out, up_out, sem):
    adapters, _, width = down_ref.shape
    copies = [
        pltpu.make_async_copy(
            down_ref.at[j], down_out.at[:, pl.ds(j * width, width)], sem.at[j]
        )
        for j in range(adapters)
    ]
    copies.append(pltpu.make_async_copy(up_ref, up_out, sem.at[adapters]))
    for copy in copies:
        copy.start()
    for copy in copies:
        copy.wait()


def stage(down_weight, up_weight):
    adapters, features, width = down_weight.shape
    whole = pl.BlockSpec(memory_space=VMEM)
    return pl.pallas_call(
        stage_kernel,
        out_shape=[
            pltpu.VMEM((features, adapters * width), down_weight.dtype),
            pltpu.VMEM(up_weight.shape, up_weight.dtype),
        ],
        in_specs=[pl.BlockSpec(memory_space=pltpu.HBM)] * 2,
        out_specs=[whole, whole],
        scratch_shapes=[pltpu.SemaphoreType.DMA((adapters + 1,))],
        compiler_params=params(12),
        cost_estimate=cost(10, 10),
        name="stage_maps",
    )(in_hbm(down_weight), in_hbm(up_weight))


def down_kernel(shifts, cols, narrow_size, per_step, where_ref, weight_ref, *refs):
    count = len(shifts)
    xs, refs = refs[:count], refs[count:]
    before, refs = (refs[:3], refs[3:]) if narrow_size else ((), refs)
    flag_ref, ids_ref, *outs, held_ref = refs
    steps = weight_ref.shape[1] // (per_step * LANES)

    flag = jnp.zeros((1, LANES), f32)
    ids = []
    offset = 0
    for x, shift in zip(xs, shifts):
        rows = x.shape[0]
        held_ref[pl.ds(offset, rows), :] = x[...]
        last = x[pl.ds(rows - 16, 16), :LANES].astype(f32)[15:]
        flag = jnp.maximum(flag, last)
        turned = jnp.broadcast_to(last, (LANES, LANES)).T[:rows]
        keep = lax.broadcasted_iota(i32, (rows, LANES), 0) < rows - 1
        ids.append(jnp.where(keep, turned - shift, 0.0))
        offset += rows
    ids = jnp.concatenate(ids, axis=0)
    lane = lax.broadcasted_iota(i32, (1, LANES), 1)
    flag = jnp.max(jnp.where(lane == LANES - 1, flag, 0.0)).astype(i32)

    total = jnp.zeros(ids.shape, f32)
    for c in range(steps):
        weights = weight_ref[:, c * per_step * LANES : (c + 1) * per_step * LANES]
        found = jnp.dot(held_ref[...], weights, preferred_element_type=f32)
        for j in range(per_step):
            name = c * per_step + j + 1.0
            total = jnp.where(ids == name, found[:, j * LANES : (j + 1) * LANES], total)

    if not narrow_size:
        flag_ref[0, 0] = flag
        ids_ref[...] = ids
        outs[0][...] = total
        return
    if before:
        flag = jnp.maximum(flag, before[0][0, 0])
        ids = jnp.concatenate([before[1][...], ids], axis=0)
        total = jnp.concatenate([before[2][...], total], axis=0)
    flag_ref[0, 0] = flag
    padding = jnp.zeros((ids_ref.shape[0] - ids.shape[0], LANES), f32)
    if padding.shape[0]:
        ids = jnp.concatenate([ids, padding], axis=0)
        total = jnp.concatenate([total, padding], axis=0)
    ids_ref[...] = ids
    half = total.shape[0] // 2
    rank = LANES // 2
    top, bottom = total[:half], total[half:]
    low = lax.broadcasted_iota(i32, (half, LANES), 1) < rank
    keys = jnp.where(low, top, pltpu.roll(bottom, rank, 1))
    values = jnp.where(low, pltpu.roll(top, rank, 1), bottom)
    for j in range(narrow_size):
        start = jnp.bitwise_xor(where_ref[1], j) * cols
        outs[j][...] = jnp.where(start >= KEY_VALUE_COLS, values, keys).astype(outs[j].dtype)


def down(where, blocks, shifts, weight, cols, before, narrow_size, scale):
    features, width = weight.shape
    new_rows = sum(b.shape[0] for b in blocks)
    per_step = min(4, width // LANES)
    whole = pl.BlockSpec(memory_space=VMEM)
    scalar = pl.BlockSpec(memory_space=pltpu.SMEM)
    if narrow_size:
        rows = -(-(new_rows + before[1].shape[0]) // 32) * 32
        sums = [((rows // 2, LANES), bf16 if j else f32) for j in range(narrow_size)]
    else:
        rows = new_rows
        sums = [((rows, LANES), f32)]
    return pl.pallas_call(
        functools.partial(down_kernel, shifts, cols, narrow_size, per_step),
        out_shape=[
            jax.ShapeDtypeStruct((1, 1), i32),
            jax.ShapeDtypeStruct((rows, LANES), f32),
        ]
        + [jax.ShapeDtypeStruct(*s) for s in sums],
        in_specs=[scalar, whole]
        + [whole for _ in blocks]
        + ([scalar, whole, whole] if narrow_size else []),
        out_specs=[scalar, whole] + [whole for _ in sums],
        scratch_shapes=[VMEM((new_rows, features), bf16)],
        compiler_params=params(18),
        cost_estimate=cost(
            2 * new_rows * features * width, 2 * features * (new_rows + width), scale
        ),
        name="down_maps",
    )(where, weight, *blocks, *(before if narrow_size else []))


def up_kernel(narrow_size, pieces, ids_ref, *refs):
    parts, weight_ref, outs = refs[:narrow_size], refs[narrow_size], refs[narrow_size + 1 :]
    total = parts[0][...]
    for part in parts[1:]:
        total = total + part[...].astype(f32)
    low_rank = total.astype(bf16).astype(f32)
    rank = LANES // 2
    turned = pltpu.roll(low_rank, rank, 1)
    low = lax.broadcasted_iota(i32, low_rank.shape, 1) < rank
    twice = jnp.concatenate(
        [jnp.where(low, low_rank, turned), jnp.where(low, turned, low_rank)], axis=0
    )
    ids = ids_ref[...]
    second = (lax.broadcasted_iota(i32, ids.shape, 1) >= rank).astype(f32)
    adapters = weight_ref.shape[0] // rank
    left = [
        jnp.where(ids - second == 2.0 * pair + 1.0, twice, 0.0).astype(bf16)
        for pair in range(adapters // 2)
    ]
    found = jnp.dot(jnp.concatenate(left, axis=1), weight_ref[...], preferred_element_type=f32)
    for out, spans in zip(outs, pieces):
        parts_of = [found[start : start + count] for start, count in spans]
        out[...] = jnp.concatenate(parts_of, axis=0).astype(bf16)


def up(ids, parts, weight, pieces):
    cols = weight.shape[1]
    counts = [sum(count for _, count in spans) for spans in pieces]
    return pl.pallas_call(
        functools.partial(up_kernel, len(parts), pieces),
        out_shape=[jax.ShapeDtypeStruct((c, cols), bf16) for c in counts],
        compiler_params=params(10),
        cost_estimate=cost(2 * sum(counts) * weight.size, 2 * weight.size + 2 * sum(counts) * (cols + 512)),
        name="up_maps",
    )(ids, *parts, weight)


def base_kernel(count, where_ref, *refs):
    acts, weight_ref, so_far, out_ref = refs[:count], refs[count], refs[count + 1 : -1], refs[-1]
    step = pl.program_id(0)
    for j in range(count):

        @pl.when(step == j)
        def _(j=j):
            found = jnp.dot(acts[j][...], weight_ref[...], preferred_element_type=f32)
            if j:
                found = out_ref[...] + found
            elif so_far:
                found = so_far[0][...] + found
            out_ref[...] = found


def base(where, acts, first, weight, so_far):
    rows, features = acts[0].shape
    cols = weight.shape[1]
    count = len(acts)
    given = [] if so_far is None else [so_far]
    return pl.pallas_call(
        functools.partial(base_kernel, count),
        grid_spec=pltpu.PrefetchScalarGridSpec(
            num_scalar_prefetch=1,
            grid=(count,),
            in_specs=[pl.BlockSpec((rows, features), lambda i, where: (0, 0)) for _ in acts]
            + [
                pl.BlockSpec(
                    (features, cols),
                    lambda i, where: (jnp.bitwise_xor(where[1], first + i), 0),
                )
            ]
            + [pl.BlockSpec((rows, cols), lambda i, where: (0, 0)) for _ in given],
            out_specs=pl.BlockSpec((rows, cols), lambda i, where: (0, 0)),
        ),
        out_shape=jax.ShapeDtypeStruct((rows, cols), f32),
        compiler_params=params(14),
        cost_estimate=cost(2 * rows * features * count * cols, 2 * features * count * (cols + rows)),
        name="shared_projection",
    )(where, *acts, in_hbm(weight), *given)


def join_kernel(base_ref, place_ref, *refs):
    corrections, out_ref, held_ref, sem = refs[:-3], *refs[-3:]
    stacked = jnp.concatenate([c[...] for c in corrections], axis=0)
    rows, count = base_ref.shape[0], stacked.shape[0]
    parts = sem.shape[0]
    copies = []
    for n in range(parts):
        part = pl.ds(n * (rows // parts), rows // parts)
        place = place_ref[part, :1].astype(i32)
        perm = lax.broadcasted_iota(i32, (rows // parts, count), 1) == place
        found = jnp.dot(perm.astype(f32).astype(bf16), stacked, preferred_element_type=f32)
        held_ref[part, :] = (base_ref[part, :] + found).astype(out_ref.dtype)
        copy = pltpu.make_async_copy(held_ref.at[part, :], out_ref.at[part, :], sem.at[n])
        copy.start()
        copies.append(copy)
    for copy in copies:
        copy.wait()


def join(base_out, place, corrections, dtype):
    rows, cols = base_out.shape
    count = sum(c.shape[0] for c in corrections)
    parts = 2
    return pl.pallas_call(
        join_kernel,
        out_shape=pltpu.HBM((rows, cols), dtype),
        in_specs=[pl.BlockSpec(memory_space=VMEM)] * (2 + len(corrections)),
        out_specs=pl.BlockSpec(memory_space=pltpu.HBM),
        scratch_shapes=[VMEM((rows, cols), dtype), pltpu.SemaphoreType.DMA((parts,))],
        compiler_params=params(10),
        cost_estimate=cost(2 * rows * cols * count, 2 * cols * (count + 3 * rows)),
        name="join_corrections",
    )(base_out, place, *corrections)


def raise_sums(ids, sums, up_weight, pieces):
    sums = [swap(part, "narrow", j) if j else part for j, part in enumerate(sums)]
    return up(ids, sums, up_weight, pieces)


def later_turn(turn, axes, total, turns, tenant, slot, activations, down_weight, up_weight):
    wide_size, narrow_size = lax.axis_size("wide"), lax.axis_size("narrow")
    where = jnp.stack([*axes, turn])
    _, place, *sent = pack(
        where,
        tenant,
        slot,
        activations,
        down_weight.shape[0],
        wide_size,
        turns,
        (0, wide_size),
        True,
    )
    got = [swap(b, "wide", k) if k else b for k, b in enumerate(sent)]
    cols = up_weight.shape[1]
    down_weight, up_weight = stage(down_weight, up_weight)
    shifts = [0] * wide_size
    before = down(where, got[:1], shifts[:1], down_weight, cols, None, 0, 0.001)
    more, ids, *sums = down(
        where, got[1:], shifts[1:], down_weight, cols, before, narrow_size, 0.001
    )
    pieces = [[(k * LATER_ROWS, LATER_ROWS)] for k in range(wide_size)]
    outs = raise_sums(ids, sums, up_weight, pieces)
    answers = [swap(b, "wide", k) if k else b for k, b in enumerate(outs)]
    return join(total, place, answers, f32), more[0, 0]


def on_device(
    activations,
    request_tenants,
    adapter_slot,
    shared_weight,
    adapter_down_weight,
    adapter_up_weight,
):
    rows = activations.shape[0]
    wide_size, narrow_size = lax.axis_size("wide"), lax.axis_size("narrow")
    local_count = adapter_down_weight.shape[0]
    axes = (lax.axis_index("wide").astype(i32), lax.axis_index("narrow").astype(i32))
    where = jnp.stack([*axes, jnp.int32(0)])
    tenant = request_tenants.reshape(1, rows)
    slot = adapter_slot.reshape(1, -1)
    up_weight = adapter_up_weight.reshape(-1, adapter_up_weight.shape[-1])

    cols = up_weight.shape[1]
    turns = first_turn(wide_size, local_count)
    leaving, early, rest = turns
    own = len(leaving) - 1
    routed = (local_count, wide_size, turns)
    ahead = min(own, 1 + sum(shared for _, shared, _ in leaving))
    begun, *sent = pack(where, tenant, slot, activations, *routed, (0, ahead), False)
    half = narrow_size // 2

    def step(work, *operands):
        def never(*operands):
            return jax.tree.map(
                lambda s: jnp.zeros(s.shape, s.dtype), jax.eval_shape(work, *operands)
            )

        return lax.cond(begun[0, 0] > 0, work, never, *operands)

    def spread(act):
        acts, bit = {0: act}, half // 2
        while bit:
            acts.update({j ^ bit: swap(x, "narrow", bit) for j, x in list(acts.items())})
            bit //= 2
        return [acts[j] for j in sorted(acts)]

    def pack_away(tenant, slot, activations):
        blocks = pack(where, tenant, slot, activations, *routed, (ahead, own), False)[1:]
        return blocks, spread(activations)[1:]

    def pack_own(tenant, slot, activations):
        return pack(where, tenant, slot, activations, *routed, (own, own + 1), False)[1:]

    def work_before(acts, shared_weight, maps):
        return base(where, acts, 0, shared_weight, None), stage(*maps)

    def work_after(across, shared_weight, base_out):
        for n, act in enumerate(spread(across)):
            base_out = base(where, [act], half + n, shared_weight, base_out)
        return base_out

    if own == ahead:
        acts = spread(activations)[1:]
    else:
        away, acts = step(pack_away, tenant, slot, after(activations, *sent))
        sent += away
    acts = [activations, *acts]
    got = {}
    for (k, shared, _), block in zip(leaving, sent):
        got[k, shared] = swap(block, "wide", k)
    shared_weight, maps = after_all((shared_weight, (adapter_down_weight, up_weight)), *sent)
    place, own_block = step(pack_own, tenant, slot, after(activations, *sent))
    got[0, False] = own_block
    across = swap(after(activations, *sent[:ahead]), "narrow", half) if half else None
    base_out, (down_beside, up_beside) = step(
        work_before, *after_all((acts, shared_weight, maps), own_block)
    )

    for k, shared, _ in leaving:
        if shared:
            got[k ^ 1, True] = swap(after(got[k, True], base_out), "wide", 1)

    def blocks_of(entries):
        shifts = [local_count if shared and k % 2 else 0 for k, shared, _ in entries]
        return [got[k, shared] for k, shared, _ in entries], shifts

    blocks, shifts = blocks_of(early)
    blocks[-1] = after(blocks[-1], base_out)
    before = down(where, blocks, shifts, down_beside, cols, None, 0, 0.001)
    blocks, shifts = blocks_of(rest)
    more, ids, *sums = down(
        where, after_all(blocks, *before), shifts, down_beside, cols, before, narrow_size, 0.001
    )
    starts, start = {}, 0
    for k, shared, count in early + rest:
        starts[k, shared] = start
        start += count
    spans = {}
    for k, shared, count in answer_order(early, rest):
        spans.setdefault(k, []).append((starts[k, shared], count))
    outs = raise_sums(ids, sums, up_beside, list(spans.values()))
    answers = [swap(b, "wide", k) if k else b for k, b in zip(spans, outs)]
    if half:
        base_out = step(work_after, *after_all((across, shared_weight, base_out), *outs))
    more = more[0, 0]

    def done(base_out):
        return join(base_out, place, answers, bf16)

    def go_on(base_out):
        def turn_of(state):
            turn, _, total = state
            total, more = later_turn(
                turn, axes, total, turns, tenant, slot, activations, adapter_down_weight, up_weight
            )
            return turn + 1, more, total

        state = (jnp.int32(0), jnp.int32(1), join(base_out, place, answers, f32))
        return lax.while_loop(lambda s: s[1] > 0, turn_of, state)[2].astype(bf16)

    return lax.cond(more > 0, go_on, done, base_out)


def solution(mesh):
    in_specs = (
        P(("groups", "wide"), "narrow"),
        P(("groups", "wide"), None),
        P(),
        P(None, "narrow"),
        P("wide", "narrow", None),
        P("wide", None, "narrow"),
    )
    out_specs = P(("groups", "wide"), "narrow")
    return jax.shard_map(
        on_device, mesh=mesh, in_specs=in_specs, out_specs=out_specs, check_vma=False
    )
```

```python
import functools

import jax
import jax.numpy as jnp
from jax import lax
from jax.experimental import pallas as pl
from jax.experimental.pallas import tpu as pltpu
from jax.sharding import PartitionSpec as P

KEY_VALUE_COLS = 1024
LANES = 128
MOST = 16
OWN_ROWS = 112
NEAR_ROWS = 112
FAR_ROWS = 64
SHARED_ROWS = 48
LATER_ROWS = 32
DOWN_SCALE = 6
VMEM = pltpu.VMEM
MIB = 1 << 20

f32, bf16, i32 = jnp.float32, jnp.bfloat16, jnp.int32


def first_turn(wide_size, local_count):
    most = -(-(local_count * MOST + 1) // 32) * 32
    plain = {k: min(FAR_ROWS if k > 1 else NEAR_ROWS if k else OWN_ROWS, most) for k in range(wide_size)}
    far = range(2, wide_size)
    shares = FAR_ROWS - 1 < local_count * MOST

    near = [(k, False, plain[k]) for k in range(min(2, wide_size))][::-1]
    apart, passed = [], []
    for k in far[::-1]:
        apart += [(k, False, plain[k])] + [(k, True, SHARED_ROWS)] * (shares and k % 2)
        passed += [(k, True, SHARED_ROWS)] * (shares and k % 2 == 0)
    ahead = 1 + shares if apart else 1
    return [*apart, *near], [*apart[:ahead], *near], [*apart[ahead:], *passed]


def answer_order(early, rest):
    return sorted(early + rest, key=lambda entry: (-entry[0], entry[1]))


def swap(x, axis, k):
    size = lax.axis_size(axis)
    return lax.ppermute(x, axis, [(i, i ^ k) for i in range(size)])


def after(x, *others):
    return lax.optimization_barrier((x, *others))[0]


def after_all(xs, *others):
    return lax.optimization_barrier((xs, others))[0]


def cost(flops, bytes_accessed, scale=0.001):
    return pl.CostEstimate(
        flops=int(flops * scale), bytes_accessed=int(bytes_accessed * scale), transcendentals=0
    )


def params(mib):
    return pltpu.CompilerParams(vmem_limit_bytes=mib * MIB)


def in_hbm(x):
    return pltpu.with_memory_space_constraint(x, pltpu.HBM)


def pack_kernel(
    local_count, wide_size, turns, span, later, where_ref, tenant_ref, slot_ref, act_ref, *refs
):
    leaving, early, rest = turns
    layout = [(k, False, LATER_ROWS) for k in range(wide_size)] if later else leaving
    answers = layout if later else answer_order(early, rest)
    picked = range(*span)
    begun_ref, refs = refs[0], refs[1:]
    last_span = span[1] == len(layout)
    place_ref, refs = (refs[0], refs[1:]) if last_span else (None, refs)
    blocks = dict(zip(picked, refs[:-2]))
    if len(refs) - 2 < len(picked):
        starts = [sum(layout[m][2] for m in picked[:n]) for n in range(len(picked))]
        blocks = {n: refs[0].at[pl.ds(start, layout[n][2]), :] for n, start in zip(picked, starts)}
    act_held, in_sem = refs[-2:]
    rows, features = act_held.shape
    chunks = 4
    width = features // chunks
    loads = in_sem.shape[0]

    def load(n):
        part = pl.ds(n * (rows // loads), rows // loads)
        return pltpu.make_async_copy(act_ref.at[part, :], act_held.at[part, :], in_sem.at[n])

    for n in range(loads):
        load(n).start()
    begun_ref[0, 0] = jnp.int32(1)

    tenants = slot_ref.shape[1]
    tenant = tenant_ref[...]
    named = tenant == lax.broadcasted_iota(i32, (tenants, rows), 0)
    slots = jnp.broadcast_to(slot_ref[...].astype(f32), (8, tenants)).astype(bf16)
    slot = jnp.dot(slots, named.astype(f32).astype(bf16), preferred_element_type=f32)[:1]
    dest = jnp.floor((slot + 0.5) * (1.0 / local_count))
    adapter = slot - dest * local_count + 1.0
    leap = jnp.bitwise_xor(dest.astype(i32), where_ref[0])
    padded = max(8, wide_size)
    goes = (leap == lax.broadcasted_iota(i32, (padded, rows), 0)).astype(f32)
    earlier = lax.broadcasted_iota(i32, (rows, rows), 0) < lax.broadcasted_iota(
        i32, (rows, rows), 1
    )
    before = jnp.dot(
        goes.astype(bf16), earlier.astype(f32).astype(bf16), preferred_element_type=f32
    )
    position = jnp.sum(goes * before, axis=0, keepdims=True).astype(i32)
    held = {k: count - 1 for k, shared, count in leaving if not shared}
    end, extra = dict(held), {}
    for k, shared, count in leaving:
        if shared:
            named_k = jnp.sum(goes[k : k + 1], axis=1, keepdims=True).astype(i32)
            extra[k] = jnp.maximum(named_k - held[k], 0)
            end[k] = held[k] + count - 1
            end[k ^ 1] = held[k ^ 1] + count - 1 - jnp.minimum(extra[k], count - 1)
    offsets, offset = {}, 0
    for k, shared, count in answers:
        offsets[k, shared] = offset
        offset += count
    place = jnp.full((1, rows), -1, i32)
    more = jnp.zeros((1, rows), f32)
    here, adapters = [], []
    for k, shared, count in layout:
        numbers = adapter
        if later:
            mine = position - end[k] - where_ref[2] * (count - 1)
            mine = jnp.where(leap == k, mine, -1)
            more = jnp.where(mine >= count - 1, 1.0, more)
        elif shared:
            mine = jnp.where(leap == k, position - held[k], -1)
            other = jnp.where(position >= held[k ^ 1], position - held[k ^ 1] + extra[k], -1)
            mine = jnp.where(leap == k ^ 1, other, mine)
            numbers = adapter + jnp.where(leap == k ^ 1, 1.0 * local_count, 0.0)
        else:
            mine = jnp.where(leap == k, position, -1)
            more = jnp.where((leap == k) & (position >= end[k]), 1.0, more)
        mine = jnp.where((mine >= 0) & (mine < count - 1), mine, -1)
        for j in (k, k ^ 1) if shared else (k,):
            place = jnp.where((mine >= 0) & (leap == j), mine + offsets[j, shared], place)
        here.append(mine)
        adapters.append(jnp.broadcast_to(numbers, (8, rows)).astype(bf16))
    any_more = jnp.max(more, axis=1, keepdims=True)

    perm = jnp.concatenate(
        [
            (lax.broadcasted_iota(i32, (LANES, rows), 0) == here[n]).astype(f32).astype(bf16)
            for n in picked
        ],
        axis=0,
    )
    all_ids = [
        lax.dot_general(
            adapters[n],
            perm[m * LANES : (m + 1) * LANES],
            (((1,), (1,)), ((), ())),
            preferred_element_type=f32,
        )[:1]
        for m, n in enumerate(picked)
    ]
    lane = lax.broadcasted_iota(i32, (1, LANES), 1)
    for n in range(loads):
        load(n).wait()
    for c in range(chunks):
        cols = pl.ds(c * width, width)
        body = jnp.dot(perm, act_held[:, cols], preferred_element_type=f32)
        for m, n in enumerate(picked):
            count = layout[n][2]
            part = body[m * LANES : m * LANES + count]
            if c == 0:
                ids = jnp.where(lane == LANES - 1, any_more, all_ids[m])
                last = lax.broadcasted_iota(i32, (count, LANES), 0) == count - 1
                first = jnp.where(last, ids, part[:, :LANES])
                part = jnp.concatenate([first, part[:, LANES:]], axis=1)
            blocks[n][:, cols] = part.astype(bf16)
    if last_span:
        place_ref[...] = jnp.broadcast_to(place.astype(f32), (LANES, rows)).T


def pack(
    where, tenant, slot, activations, local_count, wide_size, turns, span, later, in_one=False
):
    rows, features = activations.shape
    total = wide_size if later else len(turns[0])
    counts = [LATER_ROWS if later else turns[0][n][2] for n in range(*span)]
    counts = [sum(counts)] if in_one else counts
    places = [jax.ShapeDtypeStruct((rows, LANES), f32)] if span[1] == total else []
    loads = 4
    whole = pl.BlockSpec(memory_space=VMEM)
    scalar = pl.BlockSpec(memory_space=pltpu.SMEM)
    return pl.pallas_call(
        functools.partial(pack_kernel, local_count, wide_size, turns, span, later),
        out_shape=[
            jax.ShapeDtypeStruct((1, 1), i32),
            *places,
        ]
        + [pltpu.VMEM((c, features), bf16) for c in counts],
        in_specs=[scalar, whole, whole, pl.BlockSpec(memory_space=pltpu.HBM)],
        out_specs=[scalar] + [whole for _ in [*places, *counts]],
        scratch_shapes=[VMEM((rows, features), bf16), pltpu.SemaphoreType.DMA((loads,))],
        compiler_params=params(12),
        cost_estimate=cost(2 * sum(counts) * rows * features, 2 * features * (rows + sum(counts))),
        name="pack_rows",
    )(where, tenant, slot, in_hbm(activations))


def stage_kernel(down_ref, up_ref, down_out, up_out, sem):
    adapters, _, width = down_ref.shape
    copies = [
        pltpu.make_async_copy(
            down_ref.at[j], down_out.at[:, pl.ds(j * width, width)], sem.at[j]
        )
        for j in range(adapters)
    ]
    copies.append(pltpu.make_async_copy(up_ref, up_out, sem.at[adapters]))
    for copy in copies:
        copy.start()
    for copy in copies:
        copy.wait()


def stage(down_weight, up_weight):
    adapters, features, width = down_weight.shape
    whole = pl.BlockSpec(memory_space=VMEM)
    return pl.pallas_call(
        stage_kernel,
        out_shape=[
            pltpu.VMEM((features, adapters * width), down_weight.dtype),
            pltpu.VMEM(up_weight.shape, up_weight.dtype),
        ],
        in_specs=[pl.BlockSpec(memory_space=pltpu.HBM)] * 2,
        out_specs=[whole, whole],
        scratch_shapes=[pltpu.SemaphoreType.DMA((adapters + 1,))],
        compiler_params=params(12),
        cost_estimate=cost(10, 10),
        name="stage_maps",
    )(in_hbm(down_weight), in_hbm(up_weight))


def down_kernel(views, cols, narrow_size, per_step, where_ref, weight_ref, *refs):
    count = len(views)
    xs, refs = refs[:count], refs[count:]
    before, refs = (refs[:3], refs[3:]) if narrow_size else ((), refs)
    flag_ref, ids_ref, *outs, held_ref = refs
    steps = weight_ref.shape[1] // (per_step * LANES)

    flag = jnp.zeros((1, LANES), f32)
    ids = []
    offset = 0
    for x, (begin, rows, shift) in zip(xs, views):
        held_ref[pl.ds(offset, rows), :] = x[pl.ds(begin, rows), :]
        last = x[pl.ds(begin + rows - 16, 16), :LANES].astype(f32)[15:]
        flag = jnp.maximum(flag, last)
        turned = jnp.broadcast_to(last, (LANES, LANES)).T[:rows]
        keep = lax.broadcasted_iota(i32, (rows, LANES), 0) < rows - 1
        ids.append(jnp.where(keep, turned - shift, 0.0))
        offset += rows
    ids = jnp.concatenate(ids, axis=0)
    lane = lax.broadcasted_iota(i32, (1, LANES), 1)
    flag = jnp.max(jnp.where(lane == LANES - 1, flag, 0.0)).astype(i32)

    total = jnp.zeros(ids.shape, f32)
    for c in range(steps):
        weights = weight_ref[:, c * per_step * LANES : (c + 1) * per_step * LANES]
        found = jnp.dot(held_ref[...], weights, preferred_element_type=f32)
        for j in range(per_step):
            name = c * per_step + j + 1.0
            total = jnp.where(ids == name, found[:, j * LANES : (j + 1) * LANES], total)

    if not narrow_size:
        flag_ref[0, 0] = flag
        ids_ref[...] = ids
        outs[0][...] = total
        return
    if before:
        flag = jnp.maximum(flag, before[0][0, 0])
        ids = jnp.concatenate([before[1][...], ids], axis=0)
        total = jnp.concatenate([before[2][...], total], axis=0)
    flag_ref[0, 0] = flag
    padding = jnp.zeros((ids_ref.shape[0] - ids.shape[0], LANES), f32)
    if padding.shape[0]:
        ids = jnp.concatenate([ids, padding], axis=0)
        total = jnp.concatenate([total, padding], axis=0)
    ids_ref[...] = ids
    half = total.shape[0] // 2
    rank = LANES // 2
    top, bottom = total[:half], total[half:]
    low = lax.broadcasted_iota(i32, (half, LANES), 1) < rank
    keys = jnp.where(low, top, pltpu.roll(bottom, rank, 1))
    values = jnp.where(low, pltpu.roll(top, rank, 1), bottom)
    for j in range(narrow_size):
        start = jnp.bitwise_xor(where_ref[1], j) * cols
        outs[j][...] = jnp.where(start >= KEY_VALUE_COLS, values, keys).astype(outs[j].dtype)


def down(where, blocks, views, weight, cols, before, narrow_size, scale):
    features, width = weight.shape
    new_rows = sum(rows for _, rows, _ in views)
    per_step = min(4, width // LANES)
    whole = pl.BlockSpec(memory_space=VMEM)
    scalar = pl.BlockSpec(memory_space=pltpu.SMEM)
    if narrow_size:
        rows = -(-(new_rows + before[1].shape[0]) // 32) * 32
        sums = [((rows // 2, LANES), bf16 if j else f32) for j in range(narrow_size)]
    else:
        rows = new_rows
        sums = [((rows, LANES), f32)]
    return pl.pallas_call(
        functools.partial(down_kernel, views, cols, narrow_size, per_step),
        out_shape=[
            jax.ShapeDtypeStruct((1, 1), i32),
            jax.ShapeDtypeStruct((rows, LANES), f32),
        ]
        + [jax.ShapeDtypeStruct(*s) for s in sums],
        in_specs=[scalar, whole]
        + [whole for _ in blocks]
        + ([scalar, whole, whole] if narrow_size else []),
        out_specs=[scalar, whole] + [whole for _ in sums],
        scratch_shapes=[VMEM((new_rows, features), bf16)],
        compiler_params=params(18),
        cost_estimate=cost(
            2 * new_rows * features * width, 2 * features * (new_rows + width), scale
        ),
        name="down_maps",
    )(where, weight, *blocks, *(before if narrow_size else []))


def up_kernel(narrow_size, pieces, ids_ref, *refs):
    parts, weight_ref, outs = refs[:narrow_size], refs[narrow_size], refs[narrow_size + 1 :]
    total = parts[0][...]
    for part in parts[1:]:
        total = total + part[...].astype(f32)
    low_rank = total.astype(bf16).astype(f32)
    rank = LANES // 2
    turned = pltpu.roll(low_rank, rank, 1)
    low = lax.broadcasted_iota(i32, low_rank.shape, 1) < rank
    twice = jnp.concatenate(
        [jnp.where(low, low_rank, turned), jnp.where(low, turned, low_rank)], axis=0
    )
    ids = ids_ref[...]
    second = (lax.broadcasted_iota(i32, ids.shape, 1) >= rank).astype(f32)
    adapters = weight_ref.shape[0] // rank
    left = [
        jnp.where(ids - second == 2.0 * pair + 1.0, twice, 0.0).astype(bf16)
        for pair in range(adapters // 2)
    ]
    found = jnp.dot(jnp.concatenate(left, axis=1), weight_ref[...], preferred_element_type=f32)
    for out, spans in zip(outs, pieces):
        parts_of = [found[start : start + count] for start, count in spans]
        out[...] = jnp.concatenate(parts_of, axis=0).astype(bf16)


def up(ids, parts, weight, pieces):
    cols = weight.shape[1]
    counts = [sum(count for _, count in spans) for spans in pieces]
    return pl.pallas_call(
        functools.partial(up_kernel, len(parts), pieces),
        out_shape=[jax.ShapeDtypeStruct((c, cols), bf16) for c in counts],
        compiler_params=params(10),
        cost_estimate=cost(2 * sum(counts) * weight.size, 2 * weight.size + 2 * sum(counts) * (cols + 512)),
        name="up_maps",
    )(ids, *parts, weight)


def base_kernel(count, where_ref, *refs):
    acts, weight_ref, so_far, out_ref = refs[:count], refs[count], refs[count + 1 : -1], refs[-1]
    step = pl.program_id(0)
    for j in range(count):

        @pl.when(step == j)
        def _(j=j):
            found = jnp.dot(acts[j][...], weight_ref[...], preferred_element_type=f32)
            if j:
                found = out_ref[...] + found
            elif so_far:
                found = so_far[0][...] + found
            out_ref[...] = found


def base(where, acts, first, weight, so_far):
    rows, features = acts[0].shape
    cols = weight.shape[1]
    count = len(acts)
    given = [] if so_far is None else [so_far]
    return pl.pallas_call(
        functools.partial(base_kernel, count),
        grid_spec=pltpu.PrefetchScalarGridSpec(
            num_scalar_prefetch=1,
            grid=(count,),
            in_specs=[pl.BlockSpec((rows, features), lambda i, where: (0, 0)) for _ in acts]
            + [
                pl.BlockSpec(
                    (features, cols),
                    lambda i, where: (jnp.bitwise_xor(where[1], first + i), 0),
                )
            ]
            + [pl.BlockSpec((rows, cols), lambda i, where: (0, 0)) for _ in given],
            out_specs=pl.BlockSpec((rows, cols), lambda i, where: (0, 0)),
        ),
        out_shape=jax.ShapeDtypeStruct((rows, cols), f32),
        compiler_params=params(14),
        cost_estimate=cost(2 * rows * features * count * cols, 2 * features * count * (cols + rows)),
        name="shared_projection",
    )(where, *acts, in_hbm(weight), *given)


def join_kernel(base_ref, place_ref, *refs):
    corrections, out_ref, held_ref, sem = refs[:-3], *refs[-3:]
    stacked = jnp.concatenate([c[...] for c in corrections], axis=0)
    rows, count = base_ref.shape[0], stacked.shape[0]
    parts = sem.shape[0]
    copies = []
    for n in range(parts):
        part = pl.ds(n * (rows // parts), rows // parts)
        place = place_ref[part, :1].astype(i32)
        perm = lax.broadcasted_iota(i32, (rows // parts, count), 1) == place
        found = jnp.dot(perm.astype(f32).astype(bf16), stacked, preferred_element_type=f32)
        held_ref[part, :] = (base_ref[part, :] + found).astype(out_ref.dtype)
        copy = pltpu.make_async_copy(held_ref.at[part, :], out_ref.at[part, :], sem.at[n])
        copy.start()
        copies.append(copy)
    for copy in copies:
        copy.wait()


def join(base_out, place, corrections, dtype):
    rows, cols = base_out.shape
    count = sum(c.shape[0] for c in corrections)
    parts = 2
    return pl.pallas_call(
        join_kernel,
        out_shape=pltpu.HBM((rows, cols), dtype),
        in_specs=[pl.BlockSpec(memory_space=VMEM)] * (2 + len(corrections)),
        out_specs=pl.BlockSpec(memory_space=pltpu.HBM),
        scratch_shapes=[VMEM((rows, cols), dtype), pltpu.SemaphoreType.DMA((parts,))],
        compiler_params=params(10),
        cost_estimate=cost(2 * rows * cols * count, 2 * cols * (count + 3 * rows)),
        name="join_corrections",
    )(base_out, place, *corrections)


def raise_sums(ids, sums, up_weight, pieces):
    sums = [swap(part, "narrow", j) if j else part for j, part in enumerate(sums)]
    return up(ids, sums, up_weight, pieces)


def later_turn(turn, axes, total, turns, tenant, slot, activations, down_weight, up_weight):
    wide_size, narrow_size = lax.axis_size("wide"), lax.axis_size("narrow")
    where = jnp.stack([*axes, turn])
    _, place, *sent = pack(
        where,
        tenant,
        slot,
        activations,
        down_weight.shape[0],
        wide_size,
        turns,
        (0, wide_size),
        True,
    )
    got = [swap(b, "wide", k) if k else b for k, b in enumerate(sent)]
    cols = up_weight.shape[1]
    down_weight, up_weight = stage(down_weight, up_weight)
    views = [(0, LATER_ROWS, 0)] * wide_size
    before = down(where, got[:1], views[:1], down_weight, cols, None, 0, 0.001)
    more, ids, *sums = down(
        where, got[1:], views[1:], down_weight, cols, before, narrow_size, 0.001
    )
    pieces = [[(k * LATER_ROWS, LATER_ROWS)] for k in range(wide_size)]
    outs = raise_sums(ids, sums, up_weight, pieces)
    answers = [swap(b, "wide", k) if k else b for k, b in enumerate(outs)]
    return join(total, place, answers, f32), more[0, 0]


def on_device(
    activations,
    request_tenants,
    adapter_slot,
    shared_weight,
    adapter_down_weight,
    adapter_up_weight,
):
    rows = activations.shape[0]
    wide_size, narrow_size = lax.axis_size("wide"), lax.axis_size("narrow")
    local_count = adapter_down_weight.shape[0]
    axes = (lax.axis_index("wide").astype(i32), lax.axis_index("narrow").astype(i32))
    where = jnp.stack([*axes, jnp.int32(0)])
    tenant = request_tenants.reshape(1, rows)
    slot = adapter_slot.reshape(1, -1)
    up_weight = adapter_up_weight.reshape(-1, adapter_up_weight.shape[-1])

    cols = up_weight.shape[1]
    turns = first_turn(wide_size, local_count)
    leaving, early, rest = turns
    own = len(leaving) - 1
    routed = (local_count, wide_size, turns)
    ahead = 1 + sum(shared for _, shared, _ in leaving[:2])
    begun, first = pack(where, tenant, slot, activations, *routed, (0, ahead), False, True)
    sent = []
    if own > ahead:
        sent = pack(where, tenant, slot, after(activations, first), *routed, (ahead, own), False)[1:]
    half = narrow_size // 2

    def step(work, *operands):
        def never(*operands):
            return jax.tree.map(
                lambda s: jnp.zeros(s.shape, s.dtype), jax.eval_shape(work, *operands)
            )

        return lax.cond(begun[0, 0] > 0, work, never, *operands)

    def spread(act):
        acts, bit = {0: act}, half // 2
        while bit:
            acts.update({j ^ bit: swap(x, "narrow", bit) for j, x in list(acts.items())})
            bit //= 2
        return [acts[j] for j in sorted(acts)]

    def pack_own(tenant, slot, activations):
        return pack(where, tenant, slot, activations, *routed, (own, own + 1), False)[1:]

    def work_before(activations, shared_weight, maps):
        return base(where, spread(activations), 0, shared_weight, None), stage(*maps)

    def work_after(across, shared_weight, base_out):
        for n, act in enumerate(spread(across)):
            base_out = base(where, [act], half + n, shared_weight, base_out)
        return base_out

    got = {}
    arrived = swap(first, "wide", leaving[0][0])
    for n, (k, shared, count) in enumerate(leaving[:ahead]):
        got[k, shared] = arrived, sum(entry[2] for entry in leaving[:n])
    for (k, shared, _), block in zip(leaving[ahead:], sent):
        got[k, shared] = swap(block, "wide", k), 0
    shared_weight, maps = after_all((shared_weight, (adapter_down_weight, up_weight)), first, *sent)
    place, own_block = step(pack_own, tenant, slot, after(activations, first, *sent))
    across = swap(after(activations, own_block), "narrow", half) if half else None
    base_out, (down_beside, up_beside) = step(
        work_before, *after_all((activations, shared_weight, maps), own_block)
    )
    got[0, False] = after(own_block, base_out), 0
    for k, shared, count in leaving:
        if shared:
            block, begin = got[k, True]
            block = after(block, base_out)
            got[k ^ 1, True] = swap(block[begin : begin + count], "wide", 1), 0

    def blocks_of(entries):
        blocks = [got[k, shared][0] for k, shared, _ in entries]
        views = [
            (got[k, shared][1], count, local_count if shared and k % 2 == 0 else 0)
            for k, shared, count in entries
        ]
        return blocks, views

    blocks, views = blocks_of(early)
    before = down(where, blocks, views, down_beside, cols, None, 0, 0.001)
    blocks, views = blocks_of(rest)
    more, ids, *sums = down(
        where, after_all(blocks, *before), views, down_beside, cols, before, narrow_size, DOWN_SCALE
    )
    starts, start = {}, 0
    for k, shared, count in early + rest:
        starts[k, shared] = start
        start += count
    spans = {}
    for k, shared, count in answer_order(early, rest):
        spans.setdefault(k, []).append((starts[k, shared], count))
    outs = raise_sums(ids, sums, up_beside, list(spans.values()))
    answers = [swap(b, "wide", k) if k else b for k, b in zip(spans, outs)]
    if half:
        base_out = step(work_after, *after_all((across, shared_weight, base_out), *outs))
    more = more[0, 0]

    def done(base_out):
        return join(base_out, place, answers, bf16)

    def go_on(base_out):
        def turn_of(state):
            turn, _, total = state
            total, more = later_turn(
                turn, axes, total, turns, tenant, slot, activations, adapter_down_weight, up_weight
            )
            return turn + 1, more, total

        state = (jnp.int32(0), jnp.int32(1), join(base_out, place, answers, f32))
        return lax.while_loop(lambda s: s[1] > 0, turn_of, state)[2].astype(bf16)

    return lax.cond(more > 0, go_on, done, base_out)


def solution(mesh):
    in_specs = (
        P(("groups", "wide"), "narrow"),
        P(("groups", "wide"), None),
        P(),
        P(None, "narrow"),
        P("wide", "narrow", None),
        P("wide", None, "narrow"),
    )
    out_specs = P(("groups", "wide"), "narrow")
    return jax.shard_map(
        on_device, mesh=mesh, in_specs=in_specs, out_specs=out_specs, check_vma=False
    )
```

```python
import functools

import jax
import jax.numpy as jnp
from jax import lax
from jax.experimental import pallas as pl
from jax.experimental.pallas import tpu as pltpu
from jax.sharding import PartitionSpec as P

KEY_VALUE_COLS = 1024
LANES = 128
MOST = 16
OWN_ROWS = 112
NEAR_ROWS = 112
FAR_ROWS = 64
SHARED_ROWS = 48
LATER_ROWS = 32
DOWN_SCALE = 6
VMEM = pltpu.VMEM
MIB = 1 << 20

f32, bf16, i32 = jnp.float32, jnp.bfloat16, jnp.int32


def first_turn(wide_size, local_count):
    most = -(-(local_count * MOST + 1) // 32) * 32
    plain = {k: min(FAR_ROWS if k > 1 else NEAR_ROWS if k else OWN_ROWS, most) for k in range(wide_size)}
    far = range(2, wide_size)
    shares = FAR_ROWS - 1 < local_count * MOST

    near = [(k, False, plain[k]) for k in range(min(2, wide_size))][::-1]
    apart, passed = [], []
    for k in far[::-1]:
        apart += [(k, False, plain[k])] + [(k, True, SHARED_ROWS)] * (shares and k % 2)
        passed += [(k, True, SHARED_ROWS)] * (shares and k % 2 == 0)
    ahead = 1 + shares if apart else 1
    return [*apart, *near], [*apart[:ahead], *near], [*apart[ahead:], *passed]


def answer_order(early, rest):
    return sorted(early + rest, key=lambda entry: (-entry[0], entry[1]))


def swap(x, axis, k):
    size = lax.axis_size(axis)
    return lax.ppermute(x, axis, [(i, i ^ k) for i in range(size)])


def after(x, *others):
    return lax.optimization_barrier((x, *others))[0]


def after_all(xs, *others):
    return lax.optimization_barrier((xs, others))[0]


def cost(flops, bytes_accessed, scale=0.001):
    return pl.CostEstimate(
        flops=int(flops * scale), bytes_accessed=int(bytes_accessed * scale), transcendentals=0
    )


def params(mib):
    return pltpu.CompilerParams(vmem_limit_bytes=mib * MIB)


def in_hbm(x):
    return pltpu.with_memory_space_constraint(x, pltpu.HBM)


def pack_kernel(
    local_count, wide_size, turns, span, later, where_ref, tenant_ref, slot_ref, act_ref, *refs
):
    leaving, early, rest = turns
    layout = [(k, False, LATER_ROWS) for k in range(wide_size)] if later else leaving
    answers = layout if later else answer_order(early, rest)
    picked = range(*span)
    begun_ref, refs = refs[0], refs[1:]
    last_span = span[1] == len(layout)
    place_ref, refs = (refs[0], refs[1:]) if last_span else (None, refs)
    blocks = dict(zip(picked, refs[:-2]))
    if len(refs) - 2 < len(picked):
        starts = [sum(layout[m][2] for m in picked[:n]) for n in range(len(picked))]
        blocks = {n: refs[0].at[pl.ds(start, layout[n][2]), :] for n, start in zip(picked, starts)}
    act_held, in_sem = refs[-2:]
    rows, features = act_held.shape
    chunks = 4
    width = features // chunks
    loads = in_sem.shape[0]

    def load(n):
        part = pl.ds(n * (rows // loads), rows // loads)
        return pltpu.make_async_copy(act_ref.at[part, :], act_held.at[part, :], in_sem.at[n])

    for n in range(loads):
        load(n).start()
    begun_ref[0, 0] = jnp.int32(1)

    tenants = slot_ref.shape[1]
    tenant = tenant_ref[...]
    named = tenant == lax.broadcasted_iota(i32, (tenants, rows), 0)
    slots = jnp.broadcast_to(slot_ref[...].astype(f32), (8, tenants)).astype(bf16)
    slot = jnp.dot(slots, named.astype(f32).astype(bf16), preferred_element_type=f32)[:1]
    dest = jnp.floor((slot + 0.5) * (1.0 / local_count))
    adapter = slot - dest * local_count + 1.0
    leap = jnp.bitwise_xor(dest.astype(i32), where_ref[0])
    padded = max(8, wide_size)
    goes = (leap == lax.broadcasted_iota(i32, (padded, rows), 0)).astype(f32)
    earlier = lax.broadcasted_iota(i32, (rows, rows), 0) < lax.broadcasted_iota(
        i32, (rows, rows), 1
    )
    before = jnp.dot(
        goes.astype(bf16), earlier.astype(f32).astype(bf16), preferred_element_type=f32
    )
    position = jnp.sum(goes * before, axis=0, keepdims=True).astype(i32)
    held = {k: count - 1 for k, shared, count in leaving if not shared}
    end, extra = dict(held), {}
    for k, shared, count in leaving:
        if shared:
            named_k = jnp.sum(goes[k : k + 1], axis=1, keepdims=True).astype(i32)
            extra[k] = jnp.maximum(named_k - held[k], 0)
            end[k] = held[k] + count - 1
            end[k ^ 1] = held[k ^ 1] + count - 1 - jnp.minimum(extra[k], count - 1)
    offsets, offset = {}, 0
    for k, shared, count in answers:
        offsets[k, shared] = offset
        offset += count
    place = jnp.full((1, rows), -1, i32)
    more = jnp.zeros((1, rows), f32)
    here, adapters = [], []
    for k, shared, count in layout:
        numbers = adapter
        if later:
            mine = position - end[k] - where_ref[2] * (count - 1)
            mine = jnp.where(leap == k, mine, -1)
            more = jnp.where(mine >= count - 1, 1.0, more)
        elif shared:
            mine = jnp.where(leap == k, position - held[k], -1)
            other = jnp.where(position >= held[k ^ 1], position - held[k ^ 1] + extra[k], -1)
            mine = jnp.where(leap == k ^ 1, other, mine)
            numbers = adapter + jnp.where(leap == k ^ 1, 1.0 * local_count, 0.0)
        else:
            mine = jnp.where(leap == k, position, -1)
            more = jnp.where((leap == k) & (position >= end[k]), 1.0, more)
        mine = jnp.where((mine >= 0) & (mine < count - 1), mine, -1)
        for j in (k, k ^ 1) if shared else (k,):
            place = jnp.where((mine >= 0) & (leap == j), mine + offsets[j, shared], place)
        here.append(mine)
        adapters.append(jnp.broadcast_to(numbers, (8, rows)).astype(bf16))
    any_more = jnp.max(more, axis=1, keepdims=True)

    perm = jnp.concatenate(
        [
            (lax.broadcasted_iota(i32, (LANES, rows), 0) == here[n]).astype(f32).astype(bf16)
            for n in picked
        ],
        axis=0,
    )
    all_ids = [
        lax.dot_general(
            adapters[n],
            perm[m * LANES : (m + 1) * LANES],
            (((1,), (1,)), ((), ())),
            preferred_element_type=f32,
        )[:1]
        for m, n in enumerate(picked)
    ]
    lane = lax.broadcasted_iota(i32, (1, LANES), 1)
    for n in range(loads):
        load(n).wait()
    for c in range(chunks):
        cols = pl.ds(c * width, width)
        body = jnp.dot(perm, act_held[:, cols], preferred_element_type=f32)
        for m, n in enumerate(picked):
            count = layout[n][2]
            part = body[m * LANES : m * LANES + count]
            if c == 0:
                ids = jnp.where(lane == LANES - 1, any_more, all_ids[m])
                last = lax.broadcasted_iota(i32, (count, LANES), 0) == count - 1
                first = jnp.where(last, ids, part[:, :LANES])
                part = jnp.concatenate([first, part[:, LANES:]], axis=1)
            blocks[n][:, cols] = part.astype(bf16)
    if last_span:
        place_ref[...] = jnp.broadcast_to(place.astype(f32), (LANES, rows)).T


def pack(
    where, tenant, slot, activations, local_count, wide_size, turns, span, later, in_one=False
):
    rows, features = activations.shape
    total = wide_size if later else len(turns[0])
    counts = [LATER_ROWS if later else turns[0][n][2] for n in range(*span)]
    counts = [sum(counts)] if in_one else counts
    places = [jax.ShapeDtypeStruct((rows, LANES), f32)] if span[1] == total else []
    loads = 4
    whole = pl.BlockSpec(memory_space=VMEM)
    scalar = pl.BlockSpec(memory_space=pltpu.SMEM)
    return pl.pallas_call(
        functools.partial(pack_kernel, local_count, wide_size, turns, span, later),
        out_shape=[
            jax.ShapeDtypeStruct((1, 1), i32),
            *places,
        ]
        + [pltpu.VMEM((c, features), bf16) for c in counts],
        in_specs=[scalar, whole, whole, pl.BlockSpec(memory_space=pltpu.HBM)],
        out_specs=[scalar] + [whole for _ in [*places, *counts]],
        scratch_shapes=[VMEM((rows, features), bf16), pltpu.SemaphoreType.DMA((loads,))],
        compiler_params=params(12),
        cost_estimate=cost(2 * sum(counts) * rows * features, 2 * features * (rows + sum(counts))),
        name="pack_rows",
    )(where, tenant, slot, in_hbm(activations))


def stage_kernel(down_ref, up_ref, down_out, up_out, sem):
    adapters, _, width = down_ref.shape
    copies = [
        pltpu.make_async_copy(
            down_ref.at[j], down_out.at[:, pl.ds(j * width, width)], sem.at[j]
        )
        for j in range(adapters)
    ]
    copies.append(pltpu.make_async_copy(up_ref, up_out, sem.at[adapters]))
    for copy in copies:
        copy.start()
    for copy in copies:
        copy.wait()


def stage(down_weight, up_weight):
    adapters, features, width = down_weight.shape
    whole = pl.BlockSpec(memory_space=VMEM)
    return pl.pallas_call(
        stage_kernel,
        out_shape=[
            pltpu.VMEM((features, adapters * width), down_weight.dtype),
            pltpu.VMEM(up_weight.shape, up_weight.dtype),
        ],
        in_specs=[pl.BlockSpec(memory_space=pltpu.HBM)] * 2,
        out_specs=[whole, whole],
        scratch_shapes=[pltpu.SemaphoreType.DMA((adapters + 1,))],
        compiler_params=params(12),
        cost_estimate=cost(10, 10),
        name="stage_maps",
    )(in_hbm(down_weight), in_hbm(up_weight))


def down_kernel(views, cols, narrow_size, per_step, where_ref, weight_ref, *refs):
    count = len(views)
    xs, refs = refs[:count], refs[count:]
    before, refs = (refs[:3], refs[3:]) if narrow_size else ((), refs)
    flag_ref, ids_ref, *outs, held_ref = refs
    steps = weight_ref.shape[1] // (per_step * LANES)

    flag = jnp.zeros((1, LANES), f32)
    ids = []
    offset = 0
    for x, (begin, rows, shift) in zip(xs, views):
        held_ref[pl.ds(offset, rows), :] = x[pl.ds(begin, rows), :]
        last = x[pl.ds(begin + rows - 16, 16), :LANES].astype(f32)[15:]
        flag = jnp.maximum(flag, last)
        turned = jnp.broadcast_to(last, (LANES, LANES)).T[:rows]
        keep = lax.broadcasted_iota(i32, (rows, LANES), 0) < rows - 1
        ids.append(jnp.where(keep, turned - shift, 0.0))
        offset += rows
    ids = jnp.concatenate(ids, axis=0)
    lane = lax.broadcasted_iota(i32, (1, LANES), 1)
    flag = jnp.max(jnp.where(lane == LANES - 1, flag, 0.0)).astype(i32)

    total = jnp.zeros(ids.shape, f32)
    for c in range(steps):
        weights = weight_ref[:, c * per_step * LANES : (c + 1) * per_step * LANES]
        found = jnp.dot(held_ref[...], weights, preferred_element_type=f32)
        for j in range(per_step):
            name = c * per_step + j + 1.0
            total = jnp.where(ids == name, found[:, j * LANES : (j + 1) * LANES], total)

    if not narrow_size:
        flag_ref[0, 0] = flag
        ids_ref[...] = ids
        outs[0][...] = total
        return
    if before:
        flag = jnp.maximum(flag, before[0][0, 0])
        ids = jnp.concatenate([before[1][...], ids], axis=0)
        total = jnp.concatenate([before[2][...], total], axis=0)
    flag_ref[0, 0] = flag
    padding = jnp.zeros((ids_ref.shape[0] - ids.shape[0], LANES), f32)
    if padding.shape[0]:
        ids = jnp.concatenate([ids, padding], axis=0)
        total = jnp.concatenate([total, padding], axis=0)
    ids_ref[...] = ids
    half = total.shape[0] // 2
    rank = LANES // 2
    top, bottom = total[:half], total[half:]
    low = lax.broadcasted_iota(i32, (half, LANES), 1) < rank
    keys = jnp.where(low, top, pltpu.roll(bottom, rank, 1))
    values = jnp.where(low, pltpu.roll(top, rank, 1), bottom)
    for j in range(narrow_size):
        start = jnp.bitwise_xor(where_ref[1], j) * cols
        outs[j][...] = jnp.where(start >= KEY_VALUE_COLS, values, keys).astype(outs[j].dtype)


def down(where, blocks, views, weight, cols, before, narrow_size, scale):
    features, width = weight.shape
    new_rows = sum(rows for _, rows, _ in views)
    per_step = min(8, width // LANES)
    whole = pl.BlockSpec(memory_space=VMEM)
    scalar = pl.BlockSpec(memory_space=pltpu.SMEM)
    if narrow_size:
        rows = -(-(new_rows + before[1].shape[0]) // 32) * 32
        sums = [((rows // 2, LANES), bf16 if j else f32) for j in range(narrow_size)]
    else:
        rows = new_rows
        sums = [((rows, LANES), f32)]
    return pl.pallas_call(
        functools.partial(down_kernel, views, cols, narrow_size, per_step),
        out_shape=[
            jax.ShapeDtypeStruct((1, 1), i32),
            jax.ShapeDtypeStruct((rows, LANES), f32),
        ]
        + [jax.ShapeDtypeStruct(*s) for s in sums],
        in_specs=[scalar, whole]
        + [whole for _ in blocks]
        + ([scalar, whole, whole] if narrow_size else []),
        out_specs=[scalar, whole] + [whole for _ in sums],
        scratch_shapes=[VMEM((new_rows, features), bf16)],
        compiler_params=params(18),
        cost_estimate=cost(
            2 * new_rows * features * width, 2 * features * (new_rows + width), scale
        ),
        name="down_maps",
    )(where, weight, *blocks, *(before if narrow_size else []))


def up_kernel(narrow_size, pieces, ids_ref, *refs):
    parts, weight_ref, outs = refs[:narrow_size], refs[narrow_size], refs[narrow_size + 1 :]
    total = parts[0][...]
    for part in parts[1:]:
        total = total + part[...].astype(f32)
    low_rank = total.astype(bf16).astype(f32)
    rank = LANES // 2
    turned = pltpu.roll(low_rank, rank, 1)
    low = lax.broadcasted_iota(i32, low_rank.shape, 1) < rank
    twice = jnp.concatenate(
        [jnp.where(low, low_rank, turned), jnp.where(low, turned, low_rank)], axis=0
    )
    ids = ids_ref[...]
    second = (lax.broadcasted_iota(i32, ids.shape, 1) >= rank).astype(f32)
    adapters = weight_ref.shape[0] // rank
    left = [
        jnp.where(ids - second == 2.0 * pair + 1.0, twice, 0.0).astype(bf16)
        for pair in range(adapters // 2)
    ]
    found = jnp.dot(jnp.concatenate(left, axis=1), weight_ref[...], preferred_element_type=f32)
    for out, spans in zip(outs, pieces):
        parts_of = [found[start : start + count] for start, count in spans]
        out[...] = jnp.concatenate(parts_of, axis=0).astype(bf16)


def up(ids, parts, weight, pieces):
    cols = weight.shape[1]
    counts = [sum(count for _, count in spans) for spans in pieces]
    return pl.pallas_call(
        functools.partial(up_kernel, len(parts), pieces),
        out_shape=[jax.ShapeDtypeStruct((c, cols), bf16) for c in counts],
        compiler_params=params(10),
        cost_estimate=cost(2 * sum(counts) * weight.size, 2 * weight.size + 2 * sum(counts) * (cols + 512)),
        name="up_maps",
    )(ids, *parts, weight)


def base_kernel(count, where_ref, *refs):
    acts, weight_ref, so_far, out_ref = refs[:count], refs[count], refs[count + 1 : -1], refs[-1]
    step = pl.program_id(0)
    for j in range(count):

        @pl.when(step == j)
        def _(j=j):
            found = jnp.dot(acts[j][...], weight_ref[...], preferred_element_type=f32)
            if j:
                found = out_ref[...] + found
            elif so_far:
                found = so_far[0][...] + found
            out_ref[...] = found


def base(where, acts, first, weight, so_far):
    rows, features = acts[0].shape
    cols = weight.shape[1]
    count = len(acts)
    given = [] if so_far is None else [so_far]
    return pl.pallas_call(
        functools.partial(base_kernel, count),
        grid_spec=pltpu.PrefetchScalarGridSpec(
            num_scalar_prefetch=1,
            grid=(count,),
            in_specs=[pl.BlockSpec((rows, features), lambda i, where: (0, 0)) for _ in acts]
            + [
                pl.BlockSpec(
                    (features, cols),
                    lambda i, where: (jnp.bitwise_xor(where[1], first + i), 0),
                )
            ]
            + [pl.BlockSpec((rows, cols), lambda i, where: (0, 0)) for _ in given],
            out_specs=pl.BlockSpec((rows, cols), lambda i, where: (0, 0)),
        ),
        out_shape=jax.ShapeDtypeStruct((rows, cols), f32),
        compiler_params=params(14),
        cost_estimate=cost(2 * rows * features * count * cols, 2 * features * count * (cols + rows)),
        name="shared_projection",
    )(where, *acts, in_hbm(weight), *given)


def join_kernel(base_ref, place_ref, *refs):
    corrections, out_ref, held_ref, sem = refs[:-3], *refs[-3:]
    stacked = jnp.concatenate([c[...] for c in corrections], axis=0)
    rows, count = base_ref.shape[0], stacked.shape[0]
    parts = sem.shape[0]
    copies = []
    for n in range(parts):
        part = pl.ds(n * (rows // parts), rows // parts)
        place = place_ref[part, :1].astype(i32)
        perm = lax.broadcasted_iota(i32, (rows // parts, count), 1) == place
        found = jnp.dot(perm.astype(f32).astype(bf16), stacked, preferred_element_type=f32)
        held_ref[part, :] = (base_ref[part, :] + found).astype(out_ref.dtype)
        copy = pltpu.make_async_copy(held_ref.at[part, :], out_ref.at[part, :], sem.at[n])
        copy.start()
        copies.append(copy)
    for copy in copies:
        copy.wait()


def join(base_out, place, corrections, dtype):
    rows, cols = base_out.shape
    count = sum(c.shape[0] for c in corrections)
    parts = 2
    return pl.pallas_call(
        join_kernel,
        out_shape=pltpu.HBM((rows, cols), dtype),
        in_specs=[pl.BlockSpec(memory_space=VMEM)] * (2 + len(corrections)),
        out_specs=pl.BlockSpec(memory_space=pltpu.HBM),
        scratch_shapes=[VMEM((rows, cols), dtype), pltpu.SemaphoreType.DMA((parts,))],
        compiler_params=params(10),
        cost_estimate=cost(2 * rows * cols * count, 2 * cols * (count + 3 * rows)),
        name="join_corrections",
    )(base_out, place, *corrections)


def raise_sums(ids, sums, up_weight, pieces):
    sums = [swap(part, "narrow", j) if j else part for j, part in enumerate(sums)]
    return up(ids, sums, up_weight, pieces)


def later_turn(turn, axes, total, turns, tenant, slot, activations, down_weight, up_weight):
    wide_size, narrow_size = lax.axis_size("wide"), lax.axis_size("narrow")
    where = jnp.stack([*axes, turn])
    _, place, *sent = pack(
        where,
        tenant,
        slot,
        activations,
        down_weight.shape[0],
        wide_size,
        turns,
        (0, wide_size),
        True,
    )
    got = [swap(b, "wide", k) if k else b for k, b in enumerate(sent)]
    cols = up_weight.shape[1]
    down_weight, up_weight = stage(down_weight, up_weight)
    views = [(0, LATER_ROWS, 0)] * wide_size
    before = down(where, got[:1], views[:1], down_weight, cols, None, 0, 0.001)
    more, ids, *sums = down(
        where, got[1:], views[1:], down_weight, cols, before, narrow_size, 0.001
    )
    pieces = [[(k * LATER_ROWS, LATER_ROWS)] for k in range(wide_size)]
    outs = raise_sums(ids, sums, up_weight, pieces)
    answers = [swap(b, "wide", k) if k else b for k, b in enumerate(outs)]
    return join(total, place, answers, f32), more[0, 0]


def on_device(
    activations,
    request_tenants,
    adapter_slot,
    shared_weight,
    adapter_down_weight,
    adapter_up_weight,
):
    rows = activations.shape[0]
    wide_size, narrow_size = lax.axis_size("wide"), lax.axis_size("narrow")
    local_count = adapter_down_weight.shape[0]
    axes = (lax.axis_index("wide").astype(i32), lax.axis_index("narrow").astype(i32))
    where = jnp.stack([*axes, jnp.int32(0)])
    tenant = request_tenants.reshape(1, rows)
    slot = adapter_slot.reshape(1, -1)
    up_weight = adapter_up_weight.reshape(-1, adapter_up_weight.shape[-1])

    cols = up_weight.shape[1]
    turns = first_turn(wide_size, local_count)
    leaving, early, rest = turns
    own = len(leaving) - 1
    routed = (local_count, wide_size, turns)
    ahead = 1 + sum(shared for _, shared, _ in leaving[:2])
    begun, first = pack(where, tenant, slot, activations, *routed, (0, ahead), False, True)
    sent = []
    if own > ahead:
        sent = pack(where, tenant, slot, after(activations, first), *routed, (ahead, own), False)[1:]
    half = narrow_size // 2

    def step(work, *operands):
        def never(*operands):
            return jax.tree.map(
                lambda s: jnp.zeros(s.shape, s.dtype), jax.eval_shape(work, *operands)
            )

        return lax.cond(begun[0, 0] > 0, work, never, *operands)

    def spread(act):
        acts, bit = {0: act}, half // 2
        while bit:
            acts.update({j ^ bit: swap(x, "narrow", bit) for j, x in list(acts.items())})
            bit //= 2
        return [acts[j] for j in sorted(acts)]

    def pack_own(tenant, slot, activations):
        return pack(where, tenant, slot, activations, *routed, (own, own + 1), False)[1:]

    def work_before(activations, shared_weight, maps):
        return base(where, spread(activations), 0, shared_weight, None), stage(*maps)

    def work_after(across, shared_weight, base_out):
        for n, act in enumerate(spread(across)):
            base_out = base(where, [act], half + n, shared_weight, base_out)
        return base_out

    got = {}
    arrived = swap(first, "wide", leaving[0][0])
    for n, (k, shared, count) in enumerate(leaving[:ahead]):
        got[k, shared] = arrived, sum(entry[2] for entry in leaving[:n])
    for (k, shared, _), block in zip(leaving[ahead:], sent):
        got[k, shared] = swap(block, "wide", k), 0
    shared_weight, maps = after_all((shared_weight, (adapter_down_weight, up_weight)), first, *sent)
    place, own_block = step(pack_own, tenant, slot, after(activations, first, *sent))
    across = swap(after(activations, own_block), "narrow", half) if half else None
    base_out, (down_beside, up_beside) = step(
        work_before, *after_all((activations, shared_weight, maps), own_block)
    )
    got[0, False] = after(own_block, base_out), 0
    for k, shared, count in leaving:
        if shared:
            block, begin = got[k, True]
            block = after(block, base_out)
            got[k ^ 1, True] = swap(block[begin : begin + count], "wide", 1), 0

    def blocks_of(entries):
        blocks = [got[k, shared][0] for k, shared, _ in entries]
        views = [
            (got[k, shared][1], count, local_count if shared and k % 2 == 0 else 0)
            for k, shared, count in entries
        ]
        return blocks, views

    blocks, views = blocks_of(early)
    before = down(where, blocks, views, down_beside, cols, None, 0, 0.001)
    blocks, views = blocks_of(rest)
    more, ids, *sums = down(
        where, after_all(blocks, *before), views, down_beside, cols, before, narrow_size, DOWN_SCALE
    )
    starts, start = {}, 0
    for k, shared, count in early + rest:
        starts[k, shared] = start
        start += count
    spans = {}
    for k, shared, count in answer_order(early, rest):
        spans.setdefault(k, []).append((starts[k, shared], count))
    outs = raise_sums(ids, sums, up_beside, list(spans.values()))
    answers = [swap(b, "wide", k) if k else b for k, b in zip(spans, outs)]
    if half:
        base_out = step(work_after, *after_all((across, shared_weight, base_out), *outs))
    more = more[0, 0]

    def done(base_out):
        return join(base_out, place, answers, bf16)

    def go_on(base_out):
        def turn_of(state):
            turn, _, total = state
            total, more = later_turn(
                turn, axes, total, turns, tenant, slot, activations, adapter_down_weight, up_weight
            )
            return turn + 1, more, total

        state = (jnp.int32(0), jnp.int32(1), join(base_out, place, answers, f32))
        return lax.while_loop(lambda s: s[1] > 0, turn_of, state)[2].astype(bf16)

    return lax.cond(more > 0, go_on, done, base_out)


def solution(mesh):
    in_specs = (
        P(("groups", "wide"), "narrow"),
        P(("groups", "wide"), None),
        P(),
        P(None, "narrow"),
        P("wide", "narrow", None),
        P("wide", None, "narrow"),
    )
    out_specs = P(("groups", "wide"), "narrow")
    return jax.shard_map(
        on_device, mesh=mesh, in_specs=in_specs, out_specs=out_specs, check_vma=False
    )
```

```python
import functools

import jax
import jax.numpy as jnp
from jax import lax
from jax.experimental import pallas as pl
from jax.experimental.pallas import tpu as pltpu
from jax.sharding import PartitionSpec as P

KEY_VALUE_COLS = 1024
LANES = 128
MOST = 16
OWN_ROWS = 112
NEAR_ROWS = 112
FAR_ROWS = 64
SHARED_ROWS = 48
LATER_ROWS = 32
DOWN_SCALE = 6
VMEM = pltpu.VMEM
MIB = 1 << 20

f32, bf16, i32 = jnp.float32, jnp.bfloat16, jnp.int32


def first_turn(wide_size, local_count):
    most = -(-(local_count * MOST + 1) // 32) * 32
    plain = {k: min(FAR_ROWS if k > 1 else NEAR_ROWS if k else OWN_ROWS, most) for k in range(wide_size)}
    far = range(2, wide_size)
    shares = FAR_ROWS - 1 < local_count * MOST

    near = [(k, False, plain[k]) for k in range(min(2, wide_size))][::-1]
    apart, passed = [], []
    for k in far[::-1]:
        apart += [(k, False, plain[k])] + [(k, True, SHARED_ROWS)] * (shares and k % 2)
        passed += [(k, True, SHARED_ROWS)] * (shares and k % 2 == 0)
    ahead = 1 + shares if apart else 1
    return [*apart, *near], [*apart[:ahead], *near], [*apart[ahead:], *passed]


def answer_order(early, rest):
    return sorted(early + rest, key=lambda entry: (-(entry[0] ^ 1), entry[1]))


def swap(x, axis, k):
    size = lax.axis_size(axis)
    return lax.ppermute(x, axis, [(i, i ^ k) for i in range(size)])


def after(x, *others):
    return lax.optimization_barrier((x, *others))[0]


def after_all(xs, *others):
    return lax.optimization_barrier((xs, others))[0]


def cost(flops, bytes_accessed, scale=0.001):
    return pl.CostEstimate(
        flops=int(flops * scale), bytes_accessed=int(bytes_accessed * scale), transcendentals=0
    )


def params(mib):
    return pltpu.CompilerParams(vmem_limit_bytes=mib * MIB)


def in_hbm(x):
    return pltpu.with_memory_space_constraint(x, pltpu.HBM)


def pack_kernel(
    local_count, wide_size, turns, span, later, where_ref, tenant_ref, slot_ref, act_ref, *refs
):
    leaving, early, rest = turns
    layout = [(k, False, LATER_ROWS) for k in range(wide_size)] if later else leaving
    answers = layout if later else answer_order(early, rest)
    picked = range(*span)
    begun_ref, refs = refs[0], refs[1:]
    last_span = span[1] == len(layout)
    place_ref, refs = (refs[0], refs[1:]) if last_span else (None, refs)
    blocks = dict(zip(picked, refs[:-2]))
    if len(refs) - 2 < len(picked):
        starts = [sum(layout[m][2] for m in picked[:n]) for n in range(len(picked))]
        blocks = {n: refs[0].at[pl.ds(start, layout[n][2]), :] for n, start in zip(picked, starts)}
    act_held, in_sem = refs[-2:]
    rows, features = act_held.shape
    chunks = 4
    width = features // chunks
    loads = in_sem.shape[0]

    def load(n):
        part = pl.ds(n * (rows // loads), rows // loads)
        return pltpu.make_async_copy(act_ref.at[part, :], act_held.at[part, :], in_sem.at[n])

    for n in range(loads):
        load(n).start()
    begun_ref[0, 0] = jnp.int32(1)

    tenants = slot_ref.shape[1]
    tenant = tenant_ref[...]
    named = tenant == lax.broadcasted_iota(i32, (tenants, rows), 0)
    slots = jnp.broadcast_to(slot_ref[...].astype(f32), (8, tenants)).astype(bf16)
    slot = jnp.dot(slots, named.astype(f32).astype(bf16), preferred_element_type=f32)[:1]
    dest = jnp.floor((slot + 0.5) * (1.0 / local_count))
    adapter = slot - dest * local_count + 1.0
    leap = jnp.bitwise_xor(dest.astype(i32), where_ref[0])
    padded = max(8, wide_size)
    goes = (leap == lax.broadcasted_iota(i32, (padded, rows), 0)).astype(f32)
    earlier = lax.broadcasted_iota(i32, (rows, rows), 0) < lax.broadcasted_iota(
        i32, (rows, rows), 1
    )
    before = jnp.dot(
        goes.astype(bf16), earlier.astype(f32).astype(bf16), preferred_element_type=f32
    )
    position = jnp.sum(goes * before, axis=0, keepdims=True).astype(i32)
    held = {k: count - 1 for k, shared, count in leaving if not shared}
    end, extra = dict(held), {}
    for k, shared, count in leaving:
        if shared:
            named_k = jnp.sum(goes[k : k + 1], axis=1, keepdims=True).astype(i32)
            extra[k] = jnp.maximum(named_k - held[k], 0)
            end[k] = held[k] + count - 1
            end[k ^ 1] = held[k ^ 1] + count - 1 - jnp.minimum(extra[k], count - 1)
    offsets, offset = {}, 0
    for k, shared, count in answers:
        offsets[k, shared] = offset
        offset += count
    place = jnp.full((1, rows), -1, i32)
    more = jnp.zeros((1, rows), f32)
    here, adapters = [], []
    for k, shared, count in layout:
        numbers = adapter
        if later:
            mine = position - end[k] - where_ref[2] * (count - 1)
            mine = jnp.where(leap == k, mine, -1)
            more = jnp.where(mine >= count - 1, 1.0, more)
        elif shared:
            mine = jnp.where(leap == k, position - held[k], -1)
            other = jnp.where(position >= held[k ^ 1], position - held[k ^ 1] + extra[k], -1)
            mine = jnp.where(leap == k ^ 1, other, mine)
            numbers = adapter + jnp.where(leap == k ^ 1, 1.0 * local_count, 0.0)
        else:
            mine = jnp.where(leap == k, position, -1)
            more = jnp.where((leap == k) & (position >= end[k]), 1.0, more)
        mine = jnp.where((mine >= 0) & (mine < count - 1), mine, -1)
        for j in (k, k ^ 1) if shared else (k,):
            place = jnp.where((mine >= 0) & (leap == j), mine + offsets[j, shared], place)
        here.append(mine)
        adapters.append(jnp.broadcast_to(numbers, (8, rows)).astype(bf16))
    any_more = jnp.max(more, axis=1, keepdims=True)

    perm = jnp.concatenate(
        [
            (lax.broadcasted_iota(i32, (LANES, rows), 0) == here[n]).astype(f32).astype(bf16)
            for n in picked
        ],
        axis=0,
    )
    all_ids = [
        lax.dot_general(
            adapters[n],
            perm[m * LANES : (m + 1) * LANES],
            (((1,), (1,)), ((), ())),
            preferred_element_type=f32,
        )[:1]
        for m, n in enumerate(picked)
    ]
    lane = lax.broadcasted_iota(i32, (1, LANES), 1)
    for n in range(loads):
        load(n).wait()
    for c in range(chunks):
        cols = pl.ds(c * width, width)
        body = jnp.dot(perm, act_held[:, cols], preferred_element_type=f32)
        for m, n in enumerate(picked):
            count = layout[n][2]
            part = body[m * LANES : m * LANES + count]
            if c == 0:
                ids = jnp.where(lane == LANES - 1, any_more, all_ids[m])
                last = lax.broadcasted_iota(i32, (count, LANES), 0) == count - 1
                first = jnp.where(last, ids, part[:, :LANES])
                part = jnp.concatenate([first, part[:, LANES:]], axis=1)
            blocks[n][:, cols] = part.astype(bf16)
    if last_span:
        place_ref[...] = jnp.broadcast_to(place.astype(f32), (LANES, rows)).T


def pack(
    where, tenant, slot, activations, local_count, wide_size, turns, span, later, in_one=False
):
    rows, features = activations.shape
    total = wide_size if later else len(turns[0])
    counts = [LATER_ROWS if later else turns[0][n][2] for n in range(*span)]
    counts = [sum(counts)] if in_one else counts
    places = [jax.ShapeDtypeStruct((rows, LANES), f32)] if span[1] == total else []
    loads = 4
    whole = pl.BlockSpec(memory_space=VMEM)
    scalar = pl.BlockSpec(memory_space=pltpu.SMEM)
    return pl.pallas_call(
        functools.partial(pack_kernel, local_count, wide_size, turns, span, later),
        out_shape=[
            jax.ShapeDtypeStruct((1, 1), i32),
            *places,
        ]
        + [pltpu.VMEM((c, features), bf16) for c in counts],
        in_specs=[scalar, whole, whole, pl.BlockSpec(memory_space=pltpu.HBM)],
        out_specs=[scalar] + [whole for _ in [*places, *counts]],
        scratch_shapes=[VMEM((rows, features), bf16), pltpu.SemaphoreType.DMA((loads,))],
        compiler_params=params(12),
        cost_estimate=cost(2 * sum(counts) * rows * features, 2 * features * (rows + sum(counts))),
        name="pack_rows",
    )(where, tenant, slot, in_hbm(activations))


def stage_kernel(down_ref, up_ref, down_out, up_out, sem):
    adapters, _, width = down_ref.shape
    copies = [
        pltpu.make_async_copy(
            down_ref.at[j], down_out.at[:, pl.ds(j * width, width)], sem.at[j]
        )
        for j in range(adapters)
    ]
    copies.append(pltpu.make_async_copy(up_ref, up_out, sem.at[adapters]))
    for copy in copies:
        copy.start()
    for copy in copies:
        copy.wait()


def stage(down_weight, up_weight):
    adapters, features, width = down_weight.shape
    whole = pl.BlockSpec(memory_space=VMEM)
    return pl.pallas_call(
        stage_kernel,
        out_shape=[
            pltpu.VMEM((features, adapters * width), down_weight.dtype),
            pltpu.VMEM(up_weight.shape, up_weight.dtype),
        ],
        in_specs=[pl.BlockSpec(memory_space=pltpu.HBM)] * 2,
        out_specs=[whole, whole],
        scratch_shapes=[pltpu.SemaphoreType.DMA((adapters + 1,))],
        compiler_params=params(12),
        cost_estimate=cost(10, 10),
        name="stage_maps",
    )(in_hbm(down_weight), in_hbm(up_weight))


def down_kernel(views, cols, narrow_size, per_step, where_ref, weight_ref, *refs):
    count = len(views)
    xs, refs = refs[:count], refs[count:]
    before, refs = (refs[:3], refs[3:]) if narrow_size else ((), refs)
    flag_ref, ids_ref, *outs, held_ref = refs
    steps = weight_ref.shape[1] // (per_step * LANES)

    flag = jnp.zeros((1, LANES), f32)
    ids = []
    offset = 0
    for x, (begin, rows, shift) in zip(xs, views):
        held_ref[pl.ds(offset, rows), :] = x[pl.ds(begin, rows), :]
        last = x[pl.ds(begin + rows - 16, 16), :LANES].astype(f32)[15:]
        flag = jnp.maximum(flag, last)
        turned = jnp.broadcast_to(last, (LANES, LANES)).T[:rows]
        keep = lax.broadcasted_iota(i32, (rows, LANES), 0) < rows - 1
        ids.append(jnp.where(keep, turned - shift, 0.0))
        offset += rows
    ids = jnp.concatenate(ids, axis=0)
    lane = lax.broadcasted_iota(i32, (1, LANES), 1)
    flag = jnp.max(jnp.where(lane == LANES - 1, flag, 0.0)).astype(i32)

    total = jnp.zeros(ids.shape, f32)
    for c in range(steps):
        weights = weight_ref[:, c * per_step * LANES : (c + 1) * per_step * LANES]
        found = jnp.dot(held_ref[...], weights, preferred_element_type=f32)
        for j in range(per_step):
            name = c * per_step + j + 1.0
            total = jnp.where(ids == name, found[:, j * LANES : (j + 1) * LANES], total)

    if not narrow_size:
        flag_ref[0, 0] = flag
        ids_ref[...] = ids
        outs[0][...] = total
        return
    if before:
        flag = jnp.maximum(flag, before[0][0, 0])
        ids = jnp.concatenate([before[1][...], ids], axis=0)
        total = jnp.concatenate([before[2][...], total], axis=0)
    flag_ref[0, 0] = flag
    padding = jnp.zeros((ids_ref.shape[0] - ids.shape[0], LANES), f32)
    if padding.shape[0]:
        ids = jnp.concatenate([ids, padding], axis=0)
        total = jnp.concatenate([total, padding], axis=0)
    ids_ref[...] = ids
    half = total.shape[0] // 2
    rank = LANES // 2
    top, bottom = total[:half], total[half:]
    low = lax.broadcasted_iota(i32, (half, LANES), 1) < rank
    keys = jnp.where(low, top, pltpu.roll(bottom, rank, 1))
    values = jnp.where(low, pltpu.roll(top, rank, 1), bottom)
    for j in range(narrow_size):
        start = jnp.bitwise_xor(where_ref[1], j) * cols
        outs[j][...] = jnp.where(start >= KEY_VALUE_COLS, values, keys).astype(outs[j].dtype)


def down(where, blocks, views, weight, cols, before, narrow_size, scale):
    features, width = weight.shape
    new_rows = sum(rows for _, rows, _ in views)
    per_step = min(4, width // LANES)
    whole = pl.BlockSpec(memory_space=VMEM)
    scalar = pl.BlockSpec(memory_space=pltpu.SMEM)
    if narrow_size:
        rows = -(-(new_rows + before[1].shape[0]) // 32) * 32
        sums = [((rows // 2, LANES), bf16 if j else f32) for j in range(narrow_size)]
    else:
        rows = new_rows
        sums = [((rows, LANES), f32)]
    return pl.pallas_call(
        functools.partial(down_kernel, views, cols, narrow_size, per_step),
        out_shape=[
            jax.ShapeDtypeStruct((1, 1), i32),
            jax.ShapeDtypeStruct((rows, LANES), f32),
        ]
        + [jax.ShapeDtypeStruct(*s) for s in sums],
        in_specs=[scalar, whole]
        + [whole for _ in blocks]
        + ([scalar, whole, whole] if narrow_size else []),
        out_specs=[scalar, whole] + [whole for _ in sums],
        scratch_shapes=[VMEM((new_rows, features), bf16)],
        compiler_params=params(18),
        cost_estimate=cost(
            2 * new_rows * features * width, 2 * features * (new_rows + width), scale
        ),
        name="down_maps",
    )(where, weight, *blocks, *(before if narrow_size else []))


def up_kernel(narrow_size, pieces, ids_ref, *refs):
    parts, weight_ref, outs = refs[:narrow_size], refs[narrow_size], refs[narrow_size + 1 :]
    total = parts[0][...]
    for part in parts[1:]:
        total = total + part[...].astype(f32)
    low_rank = total.astype(bf16).astype(f32)
    rank = LANES // 2
    turned = pltpu.roll(low_rank, rank, 1)
    low = lax.broadcasted_iota(i32, low_rank.shape, 1) < rank
    twice = jnp.concatenate(
        [jnp.where(low, low_rank, turned), jnp.where(low, turned, low_rank)], axis=0
    )
    ids = ids_ref[...]
    second = (lax.broadcasted_iota(i32, ids.shape, 1) >= rank).astype(f32)
    adapters = weight_ref.shape[0] // rank
    left = [
        jnp.where(ids - second == 2.0 * pair + 1.0, twice, 0.0).astype(bf16)
        for pair in range(adapters // 2)
    ]
    found = jnp.dot(jnp.concatenate(left, axis=1), weight_ref[...], preferred_element_type=f32)
    for out, spans in zip(outs, pieces):
        parts_of = [found[start : start + count] for start, count in spans]
        out[...] = jnp.concatenate(parts_of, axis=0).astype(bf16)


def up(ids, parts, weight, pieces):
    cols = weight.shape[1]
    counts = [sum(count for _, count in spans) for spans in pieces]
    return pl.pallas_call(
        functools.partial(up_kernel, len(parts), pieces),
        out_shape=[jax.ShapeDtypeStruct((c, cols), bf16) for c in counts],
        compiler_params=params(10),
        cost_estimate=cost(2 * sum(counts) * weight.size, 2 * weight.size + 2 * sum(counts) * (cols + 512)),
        name="up_maps",
    )(ids, *parts, weight)


def base_kernel(count, where_ref, *refs):
    acts, weight_ref, so_far, out_ref = refs[:count], refs[count], refs[count + 1 : -1], refs[-1]
    step = pl.program_id(0)
    for j in range(count):

        @pl.when(step == j)
        def _(j=j):
            found = jnp.dot(acts[j][...], weight_ref[...], preferred_element_type=f32)
            if j:
                found = out_ref[...] + found
            elif so_far:
                found = so_far[0][...] + found
            out_ref[...] = found


def base(where, acts, first, weight, so_far):
    rows, features = acts[0].shape
    cols = weight.shape[1]
    count = len(acts)
    given = [] if so_far is None else [so_far]
    return pl.pallas_call(
        functools.partial(base_kernel, count),
        grid_spec=pltpu.PrefetchScalarGridSpec(
            num_scalar_prefetch=1,
            grid=(count,),
            in_specs=[pl.BlockSpec((rows, features), lambda i, where: (0, 0)) for _ in acts]
            + [
                pl.BlockSpec(
                    (features, cols),
                    lambda i, where: (jnp.bitwise_xor(where[1], first + i), 0),
                )
            ]
            + [pl.BlockSpec((rows, cols), lambda i, where: (0, 0)) for _ in given],
            out_specs=pl.BlockSpec((rows, cols), lambda i, where: (0, 0)),
        ),
        out_shape=jax.ShapeDtypeStruct((rows, cols), f32),
        compiler_params=params(14),
        cost_estimate=cost(2 * rows * features * count * cols, 2 * features * count * (cols + rows)),
        name="shared_projection",
    )(where, *acts, in_hbm(weight), *given)


def join_kernel(base_ref, place_ref, *refs):
    corrections, out_ref, held_ref, sem = refs[:-3], *refs[-3:]
    stacked = jnp.concatenate([c[...] for c in corrections], axis=0)
    rows, count = base_ref.shape[0], stacked.shape[0]
    parts = sem.shape[0]
    copies = []
    for n in range(parts):
        part = pl.ds(n * (rows // parts), rows // parts)
        place = place_ref[part, :1].astype(i32)
        perm = lax.broadcasted_iota(i32, (rows // parts, count), 1) == place
        found = jnp.dot(perm.astype(f32).astype(bf16), stacked, preferred_element_type=f32)
        held_ref[part, :] = (base_ref[part, :] + found).astype(out_ref.dtype)
        copy = pltpu.make_async_copy(held_ref.at[part, :], out_ref.at[part, :], sem.at[n])
        copy.start()
        copies.append(copy)
    for copy in copies:
        copy.wait()


def join(base_out, place, corrections, dtype):
    rows, cols = base_out.shape
    count = sum(c.shape[0] for c in corrections)
    parts = 2
    return pl.pallas_call(
        join_kernel,
        out_shape=pltpu.HBM((rows, cols), dtype),
        in_specs=[pl.BlockSpec(memory_space=VMEM)] * (2 + len(corrections)),
        out_specs=pl.BlockSpec(memory_space=pltpu.HBM),
        scratch_shapes=[VMEM((rows, cols), dtype), pltpu.SemaphoreType.DMA((parts,))],
        compiler_params=params(10),
        cost_estimate=cost(2 * rows * cols * count, 2 * cols * (count + 3 * rows)),
        name="join_corrections",
    )(base_out, place, *corrections)


def raise_sums(ids, sums, up_weight, pieces):
    sums = [swap(part, "narrow", j) if j else part for j, part in enumerate(sums)]
    return up(ids, sums, up_weight, pieces)


def later_turn(turn, axes, total, turns, tenant, slot, activations, down_weight, up_weight):
    wide_size, narrow_size = lax.axis_size("wide"), lax.axis_size("narrow")
    where = jnp.stack([*axes, turn])
    _, place, *sent = pack(
        where,
        tenant,
        slot,
        activations,
        down_weight.shape[0],
        wide_size,
        turns,
        (0, wide_size),
        True,
    )
    got = [swap(b, "wide", k) if k else b for k, b in enumerate(sent)]
    cols = up_weight.shape[1]
    down_weight, up_weight = stage(down_weight, up_weight)
    views = [(0, LATER_ROWS, 0)] * wide_size
    before = down(where, got[:1], views[:1], down_weight, cols, None, 0, 0.001)
    more, ids, *sums = down(
        where, got[1:], views[1:], down_weight, cols, before, narrow_size, 0.001
    )
    pieces = [[(k * LATER_ROWS, LATER_ROWS)] for k in range(wide_size)]
    outs = raise_sums(ids, sums, up_weight, pieces)
    answers = [swap(b, "wide", k) if k else b for k, b in enumerate(outs)]
    return join(total, place, answers, f32), more[0, 0]


def on_device(
    activations,
    request_tenants,
    adapter_slot,
    shared_weight,
    adapter_down_weight,
    adapter_up_weight,
):
    rows = activations.shape[0]
    wide_size, narrow_size = lax.axis_size("wide"), lax.axis_size("narrow")
    local_count = adapter_down_weight.shape[0]
    axes = (lax.axis_index("wide").astype(i32), lax.axis_index("narrow").astype(i32))
    where = jnp.stack([*axes, jnp.int32(0)])
    tenant = request_tenants.reshape(1, rows)
    slot = adapter_slot.reshape(1, -1)
    up_weight = adapter_up_weight.reshape(-1, adapter_up_weight.shape[-1])

    cols = up_weight.shape[1]
    turns = first_turn(wide_size, local_count)
    leaving, early, rest = turns
    own = len(leaving) - 1
    routed = (local_count, wide_size, turns)
    ahead = 1 + sum(shared for _, shared, _ in leaving[:2])
    begun, first = pack(where, tenant, slot, activations, *routed, (0, ahead), False, True)
    sent = []
    if own > ahead:
        sent = pack(where, tenant, slot, after(activations, first), *routed, (ahead, own), False)[1:]
    half = narrow_size // 2

    def step(work, *operands):
        def never(*operands):
            return jax.tree.map(
                lambda s: jnp.zeros(s.shape, s.dtype), jax.eval_shape(work, *operands)
            )

        return lax.cond(begun[0, 0] > 0, work, never, *operands)

    def spread(act):
        acts, bit = {0: act}, half // 2
        while bit:
            acts.update({j ^ bit: swap(x, "narrow", bit) for j, x in list(acts.items())})
            bit //= 2
        return [acts[j] for j in sorted(acts)]

    def pack_own(tenant, slot, activations):
        return pack(where, tenant, slot, activations, *routed, (own, own + 1), False)[1:]

    def work_before(activations, shared_weight, maps):
        return base(where, spread(activations), 0, shared_weight, None), stage(*maps)

    def work_after(across, shared_weight, base_out):
        for n, act in enumerate(spread(across)):
            base_out = base(where, [act], half + n, shared_weight, base_out)
        return base_out

    got = {}
    arrived = swap(first, "wide", leaving[0][0])
    for n, (k, shared, count) in enumerate(leaving[:ahead]):
        got[k, shared] = arrived, sum(entry[2] for entry in leaving[:n])
    for (k, shared, _), block in zip(leaving[ahead:], sent):
        got[k, shared] = swap(block, "wide", k), 0
    shared_weight, maps = after_all((shared_weight, (adapter_down_weight, up_weight)), first, *sent)
    place, own_block = step(pack_own, tenant, slot, after(activations, first, *sent))
    across = swap(after(activations, own_block), "narrow", half) if half else None
    base_out, (down_beside, up_beside) = step(
        work_before, *after_all((activations, shared_weight, maps), own_block)
    )
    got[0, False] = after(own_block, base_out), 0
    for k, shared, count in leaving:
        if shared:
            block, begin = got[k, True]
            block = after(block, base_out)
            got[k ^ 1, True] = swap(block[begin : begin + count], "wide", 1), 0

    def blocks_of(entries):
        blocks = [got[k, shared][0] for k, shared, _ in entries]
        views = [
            (got[k, shared][1], count, local_count if shared and k % 2 == 0 else 0)
            for k, shared, count in entries
        ]
        return blocks, views

    blocks, views = blocks_of(early)
    before = down(where, blocks, views, down_beside, cols, None, 0, 0.001)
    blocks, views = blocks_of(rest)
    more, ids, *sums = down(
        where, after_all(blocks, *before), views, down_beside, cols, before, narrow_size, DOWN_SCALE
    )
    starts, start = {}, 0
    for k, shared, count in early + rest:
        starts[k, shared] = start
        start += count
    spans = {}
    for k, shared, count in answer_order(early, rest):
        spans.setdefault(k, []).append((starts[k, shared], count))
    outs = raise_sums(ids, sums, up_beside, list(spans.values()))
    answers = [swap(b, "wide", k) if k else b for k, b in zip(spans, outs)]
    if half:
        base_out = step(work_after, *after_all((across, shared_weight, base_out), *outs))
    more = more[0, 0]

    def done(base_out):
        return join(base_out, place, answers, bf16)

    def go_on(base_out):
        def turn_of(state):
            turn, _, total = state
            total, more = later_turn(
                turn, axes, total, turns, tenant, slot, activations, adapter_down_weight, up_weight
            )
            return turn + 1, more, total

        state = (jnp.int32(0), jnp.int32(1), join(base_out, place, answers, f32))
        return lax.while_loop(lambda s: s[1] > 0, turn_of, state)[2].astype(bf16)

    return lax.cond(more > 0, go_on, done, base_out)


def solution(mesh):
    in_specs = (
        P(("groups", "wide"), "narrow"),
        P(("groups", "wide"), None),
        P(),
        P(None, "narrow"),
        P("wide", "narrow", None),
        P("wide", None, "narrow"),
    )
    out_specs = P(("groups", "wide"), "narrow")
    return jax.shard_map(
        on_device, mesh=mesh, in_specs=in_specs, out_specs=out_specs, check_vma=False
    )
```
